32 devices in a mesh: dom: 16 (over z, y, core), col: 2 (over x).
Axes of the slice: x: 2, y: 2, z: 4, core: 2. Of those that a mesh axis runs over, the one named last changes fastest.
Arguments:
- tmat: bfloat16 [65536, 1024], P('dom', 'col'), may hold values from -6 to 6
- stored_mass_blocks: bfloat16 [4096, 128, 128], P('dom'), may hold values from -0.0009765625 to 0.0009765625
- block_index: int32 [4096, 2], P('dom'), may hold values from 0 to 35, as said below
- live_block_count: int32 [16], P('dom'), may hold values from 36 to 256, as said below
- send_rows: int32 [32, 256], P('dom'), may hold values from 0 to 4095, as said below
Outputs:
- reduced: float32 [512, 1024], P('dom', 'col')
The draws below stay inside these ranges and needn't reach their ends.
Inputs may be any that keep to these rules, and one draw needn't show every extreme that they name: `block_index`: row entries lie in 0 to 31 and column entries in 0 to 35. In each partition's list slot k < 32 is block (k, k), and slot 32 + m for m < 4 has block column 32 + m. `live_block_count`: some partition uses all 256 slots in every draw. `send_rows`: the 256 rows in each list are distinct local row numbers of the sending partition.
All inputs are finite; a program needn't handle non-finite values.
Results may differ from the reference program's by a relative error of at most 0.0029.
Values may be sent and summed in bfloat16 or wider, within the bound.
No kernel may reach another device: no remote copies, remote signals or barrier semaphores. Data moves between devices by JAX's collectives and lax.ppermute only.
A program may use at most 128 MiB of HBM per device.

```python
import jax
import jax.numpy as jnp
from jax import lax

BS = 128
CB = 512
R_DEV = 4096
HB = 2
NBR = 32
NBLK = 256
HALO = 256
NROWS = 65536
KCOLS = 1024


def draw_block_index(key, part):
    parts = NROWS // R_DEV
    base = jax.random.fold_in(key, 11)
    key_one, key_two, key_three = jax.random.split(base, 3)
    extra = NBLK - NBR - 2 * HB
    rows_halo = jax.random.randint(key_one, (parts, 2 * HB), 0, NBR)
    additional_rows = jax.random.randint(key_two, (parts, extra), 0, NBR)
    cols_extra = jax.random.randint(key_three, (parts, extra), 0, NBR + 2 * HB)
    diag = jnp.broadcast_to(jnp.arange(NBR, dtype=jnp.int32)[None, :], (parts, NBR))
    halo_cols = jnp.broadcast_to((NBR + jnp.arange(2 * HB, dtype=jnp.int32))[None, :], (parts, 2 * HB))
    rows = jnp.concatenate([diag, rows_halo.astype(jnp.int32), additional_rows.astype(jnp.int32)], 1)
    cols = jnp.concatenate([diag, halo_cols, cols_extra.astype(jnp.int32)], 1)
    return jnp.stack([rows, cols], -1).reshape(parts * NBLK, 2).astype(jnp.int32)


def draw_live_block_count(key, part):
    parts = NROWS // R_DEV
    base = jax.random.fold_in(key, 23)
    key_one, key_two = jax.random.split(base)
    counts = jax.random.randint(key_one, (parts,), NBR + 2 * HB, NBLK + 1)
    chosen = jax.random.randint(key_two, (), 0, parts)
    counts = jnp.where(jnp.arange(parts) == chosen, NBLK, counts)
    return counts.astype(jnp.int32)


def draw_send_rows(key, part):
    parts = NROWS // R_DEV
    keys = jax.random.split(jax.random.fold_in(key, 37), 2 * parts)
    picked = jax.vmap(lambda k: jax.random.permutation(k, R_DEV)[:HALO])(keys)
    return picked.astype(jnp.int32)


def block_levels(key, dims, cuts, smallest, largest):
    def one(position, shards_of):
        steps = jax.random.uniform(jax.random.fold_in(jax.random.fold_in(key, 6), position), (shards_of,), jnp.float32, smallest / len(cuts), largest / len(cuts))
        return jnp.repeat(jnp.exp(steps), dims[position] // shards_of).reshape((-1,) + (1,) * (len(dims) - position - 1))

    level = one(*cuts[0])
    for cut in cuts[1:]:
        level = level * one(*cut)
    return level


def noise(stream_key, extent, scale, limit, shards=(), kind=jnp.bfloat16):
    drawn = jax.random.normal(stream_key, extent, jnp.float32) * scale
    if len(shards) > 0:
        drawn = block_levels(stream_key, extent, shards, -0.22, 0.18) * drawn
    return jnp.clip(drawn, min=-limit, max=limit).astype(kind)


def setup_inputs(seed: int = 0) -> dict:
    splits = jax.random.split(jax.random.key(seed), 6)
    tmat = noise(splits[0], (NROWS, KCOLS), 1.0, 6.0, ((0, 16), (1, 2)))
    stored_mass_blocks = noise(splits[1], (NROWS // BS * 8, BS, BS), (4 * BS * NROWS) ** -0.5, 0.0009765625, ((0, 16),))
    block_index = draw_block_index(jax.random.fold_in(splits[5], 71), 0)
    live_block_count = draw_live_block_count(jax.random.fold_in(splits[5], 71), 0)
    send_rows = draw_send_rows(jax.random.fold_in(splits[5], 71), 0)
    return dict(tmat=tmat, stored_mass_blocks=stored_mass_blocks, block_index=block_index, live_block_count=live_block_count, send_rows=send_rows)


def reference(tmat, stored_mass_blocks, block_index, live_block_count, send_rows):
    parts = NROWS // R_DEV
    panel = tmat[:, KCOLS - CB:]
    panel_parts = panel.reshape(parts, R_DEV, CB)
    sends = send_rows.reshape(parts, 2, HALO)
    picked = jax.vmap(lambda p, s: jnp.take(p, s, axis=0))(panel_parts, sends)
    zeros = jnp.zeros((1, HALO, CB), tmat.dtype)
    from_lower = jnp.concatenate([zeros, picked[:-1, 1]], 0)
    from_upper = jnp.concatenate([picked[1:, 0], zeros], 0)
    blocks = stored_mass_blocks.reshape(parts, NBLK, BS, BS)
    index = block_index.reshape(parts, NBLK, 2)
    tparts = tmat.reshape(parts, R_DEV, KCOLS)

    def one(acc, part):
        ext = jnp.concatenate([panel_parts[part], from_lower[part], from_upper[part]], 0)
        ext = ext.reshape(NBR + 2 * HB, BS, CB)
        sel = jnp.take(ext, index[part, :, 1], axis=0)
        prod = jnp.einsum("kab,kbw->kaw", blocks[part].astype(jnp.float32), sel.astype(jnp.float32),
                          precision=lax.Precision.HIGHEST)
        live_flags = jnp.arange(NBLK) < live_block_count[part]
        onehot = ((index[part, :, 0][None, :] == jnp.arange(NBR)[:, None]) & live_flags[None, :]).astype(jnp.float32)
        summed = jnp.einsum("rk,kaw->raw", onehot, prod, precision=lax.Precision.HIGHEST)
        interface_mass_panel = summed.reshape(R_DEV, CB).astype(jnp.bfloat16)
        term = lax.dot_general(interface_mass_panel, tparts[part], (((0,), (0,)), ((), ())),
                               preferred_element_type=jnp.float32)
        return acc + term, None

    total, _ = lax.scan(one, jnp.zeros((CB, KCOLS), jnp.float32), jnp.arange(parts))
    return total
```

```python
import functools

import jax
import jax.numpy as jnp
from jax import lax
from jax.experimental import pallas as pl
from jax.experimental.pallas import tpu as pltpu
from jax.sharding import PartitionSpec as P

GROUP = 4
UNROLL = 8
CHUNKS = 2


def contract(left, right):
    return lax.dot_general(
        left, right, (((0,), (0,)), ((), ())), preferred_element_type=jnp.float32
    )


def slot_list(block_index, live, nrows_blk, shift):
    slots = block_index.shape[0]
    rows, cols = block_index[:, 0], block_index[:, 1]
    k = jnp.arange(slots)
    alive = k < live
    earlier = (rows[:, None] == rows[None, :]) & alive[None, :] & (k[None, :] < k[:, None])
    rank = jnp.sum(earlier.astype(jnp.int32), 1)
    r = jnp.arange(nrows_blk)
    count = jnp.sum(((rows[None, :] == r[:, None]) & alive[None, :]).astype(jnp.int32), 1)
    groups = (count + GROUP - 1) // GROUP
    bounds = jnp.arange(nrows_blk + 1)
    first = jnp.sum(jnp.where(r[None, :] < bounds[:, None], groups[None, :], 0), 1)
    begin = jnp.sum(jnp.where(rows[:, None] == r[None, :], first[None, :nrows_blk], 0), 1)
    place = begin * GROUP + rank
    total = slots // GROUP + nrows_blk
    g = jnp.arange(total)
    owner_row = jnp.sum((first[None, 1:nrows_blk] <= g[:, None]).astype(jnp.int32), 1)
    hit = (place[None, :] == jnp.arange(total * GROUP)[:, None]) & alive[None, :]
    value = ((k + 1) << shift) + cols
    return first, owner_row, jnp.sum(jnp.where(hit, value[None, :], 0), 1)


def spmm_kernel(row0, nrows, col0, width, shift, first, owner_row, entries, blocks, panel, low, up, after, out, ext, acc, sem):
    bsize = blocks.shape[1]
    rows_dev, halo = panel.shape[0], low.shape[0]
    cols = pl.ds(col0, width)
    copies = [
        pltpu.make_async_copy(panel.at[:, cols], ext.at[pl.ds(0, rows_dev)], sem.at[0]),
        pltpu.make_async_copy(low.at[:, cols], ext.at[pl.ds(rows_dev, halo)], sem.at[1]),
        pltpu.make_async_copy(up.at[:, cols], ext.at[pl.ds(rows_dev + halo, halo)], sem.at[2]),
    ]
    for copy in copies:
        copy.start()
    acc[...] = jnp.zeros_like(acc)
    for copy in copies:
        copy.wait()
    begin, end = first[row0], first[row0 + nrows]

    @pl.loop(0, (end - begin + UNROLL - 1) // UNROLL)
    def _(step):
        rows, prods = [], []
        for u in range(UNROLL):
            g = begin + step * UNROLL + u
            inside = g < end
            g = jnp.minimum(g, end - 1)
            rows.append(jnp.where(inside, owner_row[g] - row0, 0))
            left, right = [], []
            for j in range(GROUP):
                entry = jnp.where(inside, entries[g * GROUP + j], 0)
                block = blocks[jnp.maximum((entry >> shift) - 1, 0)]
                column = entry & ((1 << shift) - 1)
                left.append(jnp.where(entry > 0, block, jnp.zeros_like(block)))
                right.append(ext[pl.ds(pl.multiple_of(column * bsize, bsize), bsize), :])
            prods.append(
                jnp.dot(jnp.concatenate(left, 1), jnp.concatenate(right, 0), preferred_element_type=jnp.float32)
            )
        for row, prod in zip(rows, prods):
            acc[pl.ds(pl.multiple_of(row * bsize, bsize), bsize), :] += prod

    @pl.loop(0, nrows)
    def _(i):
        rows = pl.ds(pl.multiple_of(i * bsize, bsize), bsize)
        out[rows, :] = acc[rows, :].astype(out.dtype)


def spmm(lists, blocks, panel, low, up, after, shift, row0, nrows, col0, width):
    nblk, bsize, _ = blocks.shape
    ext_rows = panel.shape[0] + 2 * low.shape[0]
    near = pl.BlockSpec(memory_space=pltpu.VMEM)
    scalar = pl.BlockSpec(memory_space=pltpu.SMEM)
    blocks, panel, low, up = (pltpu.with_memory_space_constraint(a, pltpu.VMEM) for a in (blocks, panel, low, up))
    return pl.pallas_call(
        functools.partial(spmm_kernel, row0, nrows, col0, width, shift),
        out_shape=jax.ShapeDtypeStruct((nrows * bsize, width), jnp.bfloat16),
        in_specs=[scalar] * 3 + [near] * 4 + [pl.BlockSpec(memory_space=pl.ANY)],
        out_specs=near,
        scratch_shapes=[
            pltpu.VMEM((ext_rows, width), panel.dtype),
            pltpu.VMEM((nrows * bsize, width), jnp.float32),
            pltpu.SemaphoreType.DMA((3,)),
        ],
        compiler_params=pltpu.CompilerParams(vmem_limit_bytes=32 << 20),
        cost_estimate=pl.CostEstimate(
            flops=2 * nrows * 8 * bsize * bsize * width,
            bytes_accessed=2 * (ext_rows * width + nrows * bsize * width),
            transcendentals=0,
        ),
    )(*lists, blocks, panel, low, up, after)


def scatter(x):
    n_dom = lax.axis_size("dom")
    bits = n_dom.bit_length() - 1
    x = x.reshape((2,) * bits + x.shape[1:])
    for b in range(bits):
        bit = 1 << b
        mine = (lax.axis_index("dom") // bit) % 2
        keep = lax.dynamic_index_in_dim(x, mine, bits - 1 - b, keepdims=False)
        send = lax.dynamic_index_in_dim(x, 1 - mine, bits - 1 - b, keepdims=False)
        x = keep + lax.ppermute(send, "dom", [(i, i ^ bit) for i in range(n_dom)])
    return x


def halo_rows(panel, send_rows, order, owner):
    n_dom, n_col = lax.axis_size("dom"), lax.axis_size("col")
    sides, halo = send_rows.shape
    picks = send_rows.reshape(sides * halo, 1) == jnp.arange(panel.shape[0])[None, :]
    rows = jnp.dot(picks.astype(panel.dtype), panel, preferred_element_type=jnp.float32).astype(panel.dtype)
    if order is not None:
        rows = jnp.dot(rows, order, preferred_element_type=jnp.float32).astype(panel.dtype)
    up = [(i * n_col + owner, (i + 1) * n_col + owner) for i in range(n_dom - 1)]
    from_lower = lax.ppermute(rows[halo:], ("dom", "col"), up)
    from_upper = lax.ppermute(rows[:halo], ("dom", "col"), [(b, a) for a, b in up])
    return from_lower, from_upper


def body(tmat, stored_mass_blocks, block_index, live_block_count, send_rows):
    n_col, n_dom = lax.axis_size("col"), lax.axis_size("dom")
    owner = n_col - 1
    col = lax.axis_index("col")
    rows_dev, width = tmat.shape
    bsize = stored_mass_blocks.shape[1]
    nrows_blk = rows_dev // bsize
    share = width // n_dom
    shift = (nrows_blk + 2 * send_rows.shape[1] // bsize).bit_length()
    live = jnp.where(col == owner, live_block_count[0], 0)
    lists = slot_list(block_index, live, nrows_blk, shift)

    if n_col != 2 or n_dom & (n_dom - 1) or share % CHUNKS:
        low, up = halo_rows(tmat, send_rows, None, owner)
        mass = spmm(lists, stored_mass_blocks, tmat, low, up, low, shift, 0, nrows_blk, 0, width)
        total = lax.psum(contract(lax.psum(mass, "col"), tmat), "dom")
        return lax.dynamic_slice_in_dim(total, lax.axis_index("dom") * share, share, 0)

    sub, part = share // CHUNKS, width // CHUNKS
    new = jnp.arange(width)
    old = (new // sub % n_dom) * share + (new // part) * sub + new % sub
    order = (jnp.arange(width)[:, None] == old[None, :]).astype(tmat.dtype)

    na = (nrows_blk * 7) // 16
    cut = rows_dev - na * bsize
    early = cut - na * bsize
    t_b, t_a = tmat[:cut], tmat[cut:]
    ahead = [lax.ppermute(tmat[:early, h * part : (h + 1) * part], "col", [(0, 1)]) for h in range(CHUNKS)]

    low, up = halo_rows(tmat, send_rows, order, owner)
    panel = jnp.dot(tmat, order, preferred_element_type=jnp.float32).astype(tmat.dtype)

    def mass(after, row0, nrows, col0, cols):
        return spmm(lists, stored_mass_blocks, panel, low, up, after, shift, row0, nrows, col0, cols)

    mass_a, got = [], []
    for h in range(CHUNKS):
        mass_a.append(mass(ahead[h], nrows_blk - na, na, h * part, part))
        piece = jnp.where(col == owner, mass_a[h], tmat[early:cut, h * part : (h + 1) * part])
        got.append(lax.ppermute(piece, "col", [(0, 1), (1, 0)]))
    mass_b = mass(low, 0, nrows_blk - na, 0, width)

    own = jnp.concatenate([contract(m, t_a) for m in mass_a], 0) + contract(mass_b, t_b)
    own = own.reshape(CHUNKS, n_dom, sub, width).transpose(1, 0, 2, 3).reshape(n_dom, share, width)

    def in_panel_column(ahead, got):
        x = contract(mass_b, jnp.concatenate([ahead, got], 0))
        return x.reshape(CHUNKS, n_dom, sub, part).transpose(1, 2, 0, 3).reshape(n_dom, sub, width)

    def in_other_column(ahead, got):
        return contract(got, t_a).reshape(n_dom, sub, width)

    sums, back = [], []
    for h in range(CHUNKS):
        x = lax.cond(col == owner, in_panel_column, in_other_column, ahead[h], got[h])
        if h == 0:
            x = jnp.concatenate([x, own], 1)
        x = scatter(x)
        if h == 0:
            own = x[sub:]
        sums.append(x[:sub])
        back.append(lax.ppermute(x[:sub], "col", [(1, 0)]))
    back = jnp.stack(back).reshape(CHUNKS, sub, CHUNKS, part).transpose(2, 1, 0, 3)
    other = jnp.concatenate(sums, 0) + back.reshape(share, width)
    return jnp.where(col == owner, own, other)


def solution(mesh):
    return jax.shard_map(
        body,
        mesh=mesh,
        in_specs=(P("dom", "col"), P("dom", None, None), P("dom", None), P("dom"), P("dom", None)),
        out_specs=P("dom", "col"),
        check_vma=False,
    )
```

```python
import functools

import jax
import jax.numpy as jnp
from jax import lax
from jax.experimental import pallas as pl
from jax.experimental.pallas import tpu as pltpu
from jax.sharding import PartitionSpec as P

GROUP = 4
UNROLL = 8
VMEM_LIMIT = 32 << 20

ANYWHERE = pl.BlockSpec(memory_space=pl.ANY)
FAR = pl.BlockSpec(memory_space=pltpu.HBM)
NEAR = pl.BlockSpec(memory_space=pltpu.VMEM)
SCALAR = pl.BlockSpec(memory_space=pltpu.SMEM)


def contract(left, right):
    return lax.dot_general(
        left, right, (((0,), (0,)), ((), ())), preferred_element_type=jnp.float32
    )


def far(*arrays):
    return [pltpu.with_memory_space_constraint(a, pltpu.HBM) for a in arrays]


def near_nothing():
    return pl.CostEstimate(flops=1, bytes_accessed=1, transcendentals=0)


def slot_list(block_index, live, nrows_blk, shift):
    slots = block_index.shape[0]
    rows, cols = block_index[:, 0], block_index[:, 1]
    shared = cols >= nrows_blk
    keys = rows + jnp.where(shared, nrows_blk, 0)
    nkeys = 2 * nrows_blk
    k = jnp.arange(slots)
    alive = k < live
    earlier = (keys[:, None] == keys[None, :]) & alive[None, :] & (k[None, :] < k[:, None])
    rank = jnp.sum(earlier.astype(jnp.int32), 1)
    r = jnp.arange(nkeys)
    count = jnp.sum(((keys[None, :] == r[:, None]) & alive[None, :]).astype(jnp.int32), 1)
    groups = (count + GROUP - 1) // GROUP
    bounds = jnp.arange(nkeys + 1)
    first = jnp.sum(jnp.where(r[None, :] < bounds[:, None], groups[None, :], 0), 1)
    begin = jnp.sum(jnp.where(keys[:, None] == r[None, :], first[None, :nkeys], 0), 1)
    place = begin * GROUP + rank
    total = slots // GROUP + nkeys
    g = jnp.arange(total)
    owner_row = jnp.sum((first[None, 1:nkeys] <= g[:, None]).astype(jnp.int32), 1) % nrows_blk
    hit = (place[None, :] == jnp.arange(total * GROUP)[:, None]) & alive[None, :]
    value = ((k + 1) << shift) + cols - jnp.where(shared, nrows_blk, 0)
    return first, owner_row, jnp.sum(jnp.where(hit, value[None, :], 0), 1)


def products(lists, begin, end, row0, shift, block_of, source, acc, bsize):
    _, owner_row, entries = lists

    @pl.loop(0, (end - begin + UNROLL - 1) // UNROLL)
    def _(step):
        rows, prods = [], []
        for u in range(UNROLL):
            g = begin + step * UNROLL + u
            inside = g < end
            g = jnp.minimum(g, end - 1)
            rows.append(jnp.where(inside, owner_row[g] - row0, 0))
            left, right = [], []
            for j in range(GROUP):
                entry = jnp.where(inside, entries[g * GROUP + j], 0)
                block = block_of(g, j, entry)
                column = entry & ((1 << shift) - 1)
                left.append(jnp.where(entry > 0, block, jnp.zeros_like(block)))
                right.append(source[pl.ds(pl.multiple_of(column * bsize, bsize), bsize), :])
            prods.append(
                jnp.dot(jnp.concatenate(left, 1), jnp.concatenate(right, 0), preferred_element_type=jnp.float32)
            )
        for row, prod in zip(rows, prods):
            acc[pl.ds(pl.multiple_of(row * bsize, bsize), bsize), :] += prod


def stored(blocks, shift):
    return lambda g, j, entry: blocks[jnp.maximum((entry >> shift) - 1, 0)]


def shared_range(first, row0, nrows):
    nkeys = (first.shape[0] - 1) // 2
    return first[nkeys + row0], first[nkeys + row0 + nrows]


def begin_kernel(row0, nrows, shift, bsize, first, owner_row, entries, send_rows, blocks, tmat, first_rows, second_rows, own, ahead, panel, near_blocks, picked, acc, staged, sem):
    lists = (first, owner_row, entries)
    depth = picked.shape[0]
    steps = panel.shape[0] // depth
    copy_blocks = pltpu.make_async_copy(blocks, near_blocks, sem.at[steps])

    def part(step):
        chunk = pl.ds(pl.multiple_of(step * depth, depth), depth)
        return pltpu.make_async_copy(tmat.at[chunk], panel.at[chunk], sem.at[step])

    for step in range(steps):
        part(step).start()
    copy_blocks.start()
    picked[...] = jnp.zeros_like(picked)
    acc[...] = jnp.zeros_like(acc)

    @pl.loop(0, steps)
    def _(step):
        part(step).wait()
        begin = pl.multiple_of(step * depth, depth)
        numbers = lax.broadcasted_iota(jnp.int32, (depth, depth), 1) + begin
        picks = jnp.where(send_rows[...] == numbers, 1.0, 0.0).astype(panel.dtype)
        picked[...] += jnp.dot(picks, panel[pl.ds(begin, depth), :], preferred_element_type=jnp.float32)

    half = depth // 2
    odd = lax.axis_index("dom") % 2
    first_rows[...] = picked[pl.ds(pl.multiple_of((1 - odd) * half, half), half), :].astype(first_rows.dtype)
    second_rows[...] = picked[pl.ds(pl.multiple_of(odd * half, half), half), :].astype(second_rows.dtype)
    copy_blocks.wait()
    begin, end = shared_range(first, row0, nrows)

    @pl.loop(begin, end)
    def _(g):
        for j in range(GROUP):
            staged[(g - begin) * GROUP + j] = stored(near_blocks, shift)(g, j, entries[g * GROUP + j])

    batch = UNROLL * GROUP
    batches = (end - begin + UNROLL - 1) // UNROLL

    def out_blocks(step):
        some = pl.ds(step * batch, batch)
        return pltpu.make_async_copy(staged.at[some], ahead.at[some], sem.at[0])

    @pl.loop(0, batches)
    def _(step):
        out_blocks(step).start()

    products(lists, first[row0], first[row0 + nrows], row0, shift, stored(near_blocks, shift), panel, acc, bsize)
    out_own = pltpu.make_async_copy(acc, own, sem.at[1])
    out_own.start()

    @pl.loop(0, batches)
    def _(step):
        out_blocks(step).wait()

    out_own.wait()


def begin_work(lists, send_rows, blocks, tmat, shift, row0, nrows):
    bsize, width, picked = blocks.shape[1], tmat.shape[1], send_rows.size
    batch = UNROLL * GROUP
    room = -(-(blocks.shape[0] + nrows * GROUP) // batch) * batch
    tmat, blocks = far(tmat, blocks)
    return pl.pallas_call(
        functools.partial(begin_kernel, row0, nrows, shift, bsize),
        out_shape=[
            jax.ShapeDtypeStruct((picked // 2, width), tmat.dtype),
            jax.ShapeDtypeStruct((picked // 2, width), tmat.dtype),
            pltpu.HBM((nrows * bsize, width), jnp.float32),
            pltpu.HBM((room, bsize, bsize), blocks.dtype),
        ],
        in_specs=[SCALAR] * 3 + [NEAR] + [FAR] * 2,
        out_specs=[NEAR] * 2 + [FAR] * 2,
        scratch_shapes=[
            pltpu.VMEM(tmat.shape, tmat.dtype),
            pltpu.VMEM(blocks.shape, blocks.dtype),
            pltpu.VMEM((picked, width), jnp.float32),
            pltpu.VMEM((nrows * bsize, width), jnp.float32),
            pltpu.VMEM((room, bsize, bsize), blocks.dtype),
            pltpu.SemaphoreType.DMA((tmat.shape[0] // picked + 1,)),
        ],
        compiler_params=pltpu.CompilerParams(vmem_limit_bytes=VMEM_LIMIT),
        cost_estimate=near_nothing(),
    )(*lists, send_rows.reshape(picked, 1), blocks, tmat)


def place_halo(even, odd, halo):
    sides = even.shape[0]
    odd_partition = lax.axis_index("dom") % 2
    halo[pl.ds(pl.multiple_of((1 - odd_partition) * sides, sides), sides), :] = even[...]
    halo[pl.ds(pl.multiple_of(odd_partition * sides, sides), sides), :] = odd[...]


def pieces_kernel(row0, nrows, shift, bsize, other0, n_col, first, owner_row, entries, blocks, even, odd, own, tmat, after, *refs):
    *outs, near_blocks, halo, acc, sem, block_sem = refs
    panel_column = lax.axis_index("col") == n_col - 1
    size, part = outs[0].shape
    batch = UNROLL * GROUP

    @pl.when(panel_column)
    def _():
        begin, end = shared_range(first, row0, nrows)
        steps = (end - begin + UNROLL - 1) // UNROLL

        def in_blocks(step):
            return pltpu.make_async_copy(blocks.at[pl.ds(step * batch, batch)], near_blocks.at[pl.ds(step * batch, batch)], block_sem)

        in_own = pltpu.make_async_copy(own, acc, sem.at[0])

        @pl.loop(0, steps)
        def _(step):
            in_blocks(step).start()

        in_own.start()
        place_halo(even, odd, halo)

        @pl.loop(0, steps)
        def _(step):
            in_blocks(step).wait()

        in_own.wait()
        block_of = lambda g, j, entry: near_blocks[(g - begin) * GROUP + j]
        products((first, owner_row, entries), begin, end, row0, shift, block_of, halo, acc, bsize)
        for h, out in enumerate(outs):
            out[...] = acc[:, pl.ds(h * part, part)].astype(out.dtype)

    @pl.when(jnp.logical_not(panel_column))
    def _():
        copies = [
            pltpu.make_async_copy(tmat.at[pl.ds(other0, size), pl.ds(h * part, part)], out, sem.at[h])
            for h, out in enumerate(outs)
        ]
        for copy in copies:
            copy.start()
        for copy in copies:
            copy.wait()


def pieces(lists, blocks, even, odd, own, tmat, after, shift, row0, nrows, other0, chunks, n_col):
    bsize, width = blocks.shape[1], tmat.shape[1]
    size, part = nrows * bsize, width // chunks
    return pl.pallas_call(
        functools.partial(pieces_kernel, row0, nrows, shift, bsize, other0, n_col),
        out_shape=[jax.ShapeDtypeStruct((size, part), tmat.dtype)] * chunks,
        in_specs=[SCALAR] * 3 + [FAR] + [NEAR] * 2 + [FAR] * 2 + [ANYWHERE],
        out_specs=[NEAR] * chunks,
        scratch_shapes=[
            pltpu.VMEM(blocks.shape, blocks.dtype),
            pltpu.VMEM((2 * even.shape[0], width), tmat.dtype),
            pltpu.VMEM((size, width), jnp.float32),
            pltpu.SemaphoreType.DMA((chunks,)),
            pltpu.SemaphoreType.DMA,
        ],
        compiler_params=pltpu.CompilerParams(vmem_limit_bytes=VMEM_LIMIT),
        cost_estimate=near_nothing(),
    )(*lists, *far(blocks), even, odd, *far(own, tmat), after)


def mass_kernel(row0, nrows, shift, bsize, first, owner_row, entries, blocks, tmat, even, odd, after, out, panel, near_blocks, halo, acc, sem):
    lists = (first, owner_row, entries)
    copies = [pltpu.make_async_copy(tmat, panel, sem.at[0]), pltpu.make_async_copy(blocks, near_blocks, sem.at[1])]
    for copy in copies:
        copy.start()
    acc[...] = jnp.zeros_like(acc)
    place_halo(even, odd, halo)
    for copy in copies:
        copy.wait()
    block_of = stored(near_blocks, shift)
    products(lists, first[row0], first[row0 + nrows], row0, shift, block_of, panel, acc, bsize)
    products(lists, *shared_range(first, row0, nrows), row0, shift, block_of, halo, acc, bsize)
    out[...] = acc[...].astype(out.dtype)


def known_kernel(left, right, out):
    out[...] = contract(left[...], right[...])


def known_product(left, right):
    rows = right.shape[0]
    width = left.shape[1]
    return pl.pallas_call(
        known_kernel,
        grid=(1,),
        out_shape=jax.ShapeDtypeStruct((width, right.shape[1]), jnp.float32),
        in_specs=[pl.BlockSpec((rows, width), lambda i: (0, 0)), pl.BlockSpec(right.shape, lambda i: (0, 0))],
        out_specs=pl.BlockSpec((width, right.shape[1]), lambda i: (0, 0)),
        compiler_params=pltpu.CompilerParams(vmem_limit_bytes=VMEM_LIMIT),
        cost_estimate=near_nothing(),
    )(left, right)


def mass_rows(lists, blocks, tmat, even, odd, after, shift, row0, nrows):
    bsize, width = blocks.shape[1], tmat.shape[1]
    return pl.pallas_call(
        functools.partial(mass_kernel, row0, nrows, shift, bsize),
        out_shape=jax.ShapeDtypeStruct((nrows * bsize, width), tmat.dtype),
        in_specs=[SCALAR] * 3 + [FAR] * 2 + [NEAR] * 2 + [ANYWHERE],
        out_specs=NEAR,
        scratch_shapes=[
            pltpu.VMEM(tmat.shape, tmat.dtype),
            pltpu.VMEM(blocks.shape, blocks.dtype),
            pltpu.VMEM((2 * even.shape[0], width), tmat.dtype),
            pltpu.VMEM((nrows * bsize, width), jnp.float32),
            pltpu.SemaphoreType.DMA((2,)),
        ],
        compiler_params=pltpu.CompilerParams(vmem_limit_bytes=VMEM_LIMIT),
        cost_estimate=near_nothing(),
    )(*lists, *far(blocks, tmat), even, odd, after)


def halving(x, bit, axis, route):
    mine = (lax.axis_index("dom") // bit) % 2
    keep = lax.dynamic_index_in_dim(x, mine, axis, keepdims=False)
    send = lax.dynamic_index_in_dim(x, 1 - mine, axis, keepdims=False)
    return keep + lax.ppermute(send, *route(bit))


def body(tmat, stored_mass_blocks, block_index, live_block_count, send_rows):
    n_col, n_dom = lax.axis_size("col"), lax.axis_size("dom")
    owner = n_col - 1
    col, dom = lax.axis_index("col"), lax.axis_index("dom")
    rows_dev, width = tmat.shape
    bsize = stored_mass_blocks.shape[1]
    nrows_blk = rows_dev // bsize
    share = width // n_dom
    shift = nrows_blk.bit_length()
    live = jnp.where(col == owner, live_block_count[0], 0)
    lists = slot_list(block_index, live, nrows_blk, shift)

    blocks = stored_mass_blocks

    def exchange(block, begin):
        pairs = [(i * n_col + owner, (i + 1) * n_col + owner) for i in range(begin, n_dom - 1, 2)]
        return lax.ppermute(block, ("dom", "col"), pairs + [(b, a) for a, b in pairs])

    na = (nrows_blk * 13) // 32
    nb = nrows_blk - na
    *rows, own_a, blocks_a = begin_work(lists, send_rows, blocks, tmat, shift, nb, na)
    even, odd = exchange(rows[0], 0), exchange(rows[1], 1)

    if n_col != 2 or n_dom < 4 or n_dom & (n_dom - 1):
        mass = mass_rows(lists, blocks, tmat, even, odd, even, shift, 0, nrows_blk)
        total = lax.psum(contract(lax.psum(mass, "col"), tmat), "dom")
        return lax.dynamic_slice_in_dim(total, dom * share, share, 0)

    half = n_dom // 2
    cut = nb * bsize
    early = cut - na * bsize
    ahead = lax.ppermute(tmat[:early], "col", [(0, 1)])

    (sent,) = pieces(lists, blocks_a, even, odd, own_a, tmat, ahead, shift, nb, na, early, 1, n_col)
    got = lax.ppermute(sent, "col", [(0, 1), (1, 0)])
    mass_b = mass_rows(lists, blocks, tmat, even, odd, sent, shift, 0, nb)
    known = known_product(mass_b, ahead)
    own = contract(sent, tmat[cut:]) + contract(mass_b, tmat[:cut])

    def both(bit):
        return "dom", [(i, i ^ bit) for i in range(n_dom)]

    def panel_column(bit):
        return ("dom", "col"), [(i * n_col + owner, (i ^ bit) * n_col + owner) for i in range(n_dom)]

    bits = half.bit_length() - 1
    own = own.reshape((2,) * (bits + 1) + (share, width))
    for b in range(bits + 1):
        if b == bits - 1:
            got, own = lax.optimization_barrier((got, own))
        own = halving(own, 1 << b, bits - b, panel_column)

    def in_panel_column(got, known):
        x = (known + contract(mass_b[early:], got)).reshape(2, half, share, width)
        return jnp.concatenate([x[0], x[1]], 2)

    def in_other_column(got, known):
        x = contract(got, tmat[cut:]).reshape(2, half, share, width)
        return jnp.concatenate([x[0], x[1]], 2)

    x = lax.cond(col == owner, in_panel_column, in_other_column, got, known)
    x = x.reshape((2,) * bits + (share, 2 * width))
    for b in range(bits):
        x = halving(x, 1 << b, bits - 1 - b, both)
    x = jnp.stack([x[:, :width], x[:, width:]])
    x = halving(x, half, 0, both)
    other = x + lax.ppermute(x, "col", [(1, 0)])
    return jnp.where(col == owner, own, other)


def solution(mesh):
    return jax.shard_map(
        body,
        mesh=mesh,
        in_specs=(P("dom", "col"), P("dom", None, None), P("dom", None), P("dom"), P("dom", None)),
        out_specs=P("dom", "col"),
        check_vma=False,
    )
```

```python
import functools

import jax
import jax.numpy as jnp
from jax import lax
from jax.experimental import pallas as pl
from jax.experimental.pallas import tpu as pltpu
from jax.sharding import PartitionSpec as P

GROUP = 4
UNROLL = 8

ANYWHERE = pl.BlockSpec(memory_space=pl.ANY)
FAR = pl.BlockSpec(memory_space=pltpu.HBM)
NEAR = pl.BlockSpec(memory_space=pltpu.VMEM)
SCALAR = pl.BlockSpec(memory_space=pltpu.SMEM)


def contract(left, right):
    return lax.dot_general(
        left, right, (((0,), (0,)), ((), ())), preferred_element_type=jnp.float32
    )


def far(*arrays):
    return [pltpu.with_memory_space_constraint(a, pltpu.HBM) for a in arrays]


def room_for(*sizes):
    return pltpu.CompilerParams(vmem_limit_bytes=(6 << 20) + sum(sizes))


def nbytes(array):
    return array.size * array.dtype.itemsize


def near_nothing():
    return pl.CostEstimate(flops=1, bytes_accessed=1, transcendentals=0)


def columns_of(rows):
    count, width = rows.shape
    return jnp.concatenate([rows, jnp.zeros((8 - count, width), rows.dtype)], 0).T


def slot_kernel(nrows_blk, shift, n_col, live_count, index, first, owner_row, entries):
    slots = index.shape[1]
    nkeys = 2 * nrows_blk
    live = jnp.where(lax.axis_index("col") == n_col - 1, live_count[0], 0)

    def count_up(shape, axis):
        return lax.broadcasted_iota(jnp.int32, shape, axis)

    def keys_of(rows, cols):
        return rows + jnp.where(cols >= nrows_blk, nrows_blk, 0)

    def groups_of(hits, axis):
        return (jnp.sum(hits.astype(jnp.int32), axis, keepdims=True) + (GROUP - 1)) // GROUP

    across = index[...]
    down = columns_of(across)
    row_a, col_a = across[0:1], across[1:2]
    row_d, col_d = down[:, 0:1], down[:, 1:2]
    key_a, key_d = keys_of(row_a, col_a), keys_of(row_d, col_d)
    k_a, k_d = count_up((1, slots), 1), count_up((slots, 1), 0)
    alive_a, alive_d = k_a < live, k_d < live
    rank = jnp.sum(((key_a == key_d) & alive_a & (k_a < k_d)).astype(jnp.int32), 1, keepdims=True)
    groups_d = groups_of((key_a == count_up((nkeys, 1), 0)) & alive_a, 1)
    groups_a = groups_of((key_d == count_up((1, nkeys), 1)) & alive_d, 0)
    room = first.shape[1]
    first_a = jnp.sum(jnp.where(count_up((nkeys, room), 0) < count_up((nkeys, room), 1), groups_d, 0), 0, keepdims=True)
    first_d = jnp.sum(jnp.where(count_up((nkeys, nkeys), 1) < count_up((nkeys, nkeys), 0), groups_a, 0), 1, keepdims=True)
    first[...] = first_a
    started = (first_d <= count_up((nkeys, owner_row.shape[1]), 1)).astype(jnp.int32)
    key = jnp.sum(started, 0, keepdims=True) - 1
    owner_row[...] = jnp.where(key >= nrows_blk, key - nrows_blk, key)
    begin = jnp.sum(jnp.where(key_d == count_up((slots, room), 1), first_a, 0), 1, keepdims=True)
    place = begin * GROUP + rank
    value = ((k_d + 1) << shift) + col_d - jnp.where(col_d >= nrows_blk, nrows_blk, 0)
    hit = (place == count_up((slots, entries.shape[1]), 1)) & alive_d
    entries[...] = jnp.sum(jnp.where(hit, value, 0), 0, keepdims=True)


def slot_list(block_index, live_block_count, nrows_blk, shift, n_col):
    slots = block_index.shape[0]
    total = slots // GROUP + 2 * nrows_blk

    def lanes(n):
        return jax.ShapeDtypeStruct((1, -(-n // 128) * 128), jnp.int32)

    return pl.pallas_call(
        functools.partial(slot_kernel, nrows_blk, shift, n_col),
        out_shape=[lanes(2 * nrows_blk + 1), lanes(total), lanes(total * GROUP)],
        in_specs=[SCALAR, NEAR],
        out_specs=[NEAR] * 3,
        compiler_params=room_for(),
        cost_estimate=near_nothing(),
    )(live_block_count, block_index.T)


def products(lists, begin, end, row0, shift, block_of, source, acc, bsize):
    _, owner_row, entries = lists

    @pl.loop(0, (end - begin + UNROLL - 1) // UNROLL)
    def _(step):
        rows, prods = [], []
        for u in range(UNROLL):
            g = begin + step * UNROLL + u
            inside = g < end
            g = jnp.minimum(g, end - 1)
            rows.append(jnp.where(inside, owner_row[0, g] - row0, 0))
            left, right = [], []
            for j in range(GROUP):
                entry = jnp.where(inside, entries[0, g * GROUP + j], 0)
                block = block_of(g, j, entry)
                column = entry & ((1 << shift) - 1)
                left.append(jnp.where(entry > 0, block, jnp.zeros_like(block)))
                right.append(source[pl.ds(pl.multiple_of(column * bsize, bsize), bsize), :])
            prods.append(
                jnp.dot(jnp.concatenate(left, 1), jnp.concatenate(right, 0), preferred_element_type=jnp.float32)
            )
        for row, prod in zip(rows, prods):
            acc[pl.ds(pl.multiple_of(row * bsize, bsize), bsize), :] += prod


def stored(blocks, shift):
    return lambda g, j, entry: blocks[jnp.maximum((entry >> shift) - 1, 0)]


def shared_range(first, nrows_blk, row0, nrows):
    return first[0, nrows_blk + row0], first[0, nrows_blk + row0 + nrows]


def gather_kernel(send_rows, tmat, blocks, first_rows, second_rows, panel, near_blocks, picked, sem):
    depth = picked.shape[0]
    steps = panel.shape[0] // depth
    copy_blocks = pltpu.make_async_copy(blocks, near_blocks, sem.at[steps])

    def part(step):
        chunk = pl.ds(pl.multiple_of(step * depth, depth), depth)
        return pltpu.make_async_copy(tmat.at[chunk], panel.at[chunk], sem.at[step])

    for step in range(steps):
        part(step).start()
    copy_blocks.start()
    picked[...] = jnp.zeros_like(picked)
    lists = columns_of(send_rows[...])
    wanted = jnp.concatenate([lists[:, 0:1], lists[:, 1:2]], 0)

    @pl.loop(0, steps)
    def _(step):
        part(step).wait()
        begin = pl.multiple_of(step * depth, depth)
        numbers = lax.broadcasted_iota(jnp.int32, (depth, depth), 1) + begin
        picks = jnp.where(wanted == numbers, 1.0, 0.0).astype(panel.dtype)
        picked[...] += jnp.dot(picks, panel[pl.ds(begin, depth), :], preferred_element_type=jnp.float32)

    half = depth // 2
    odd = lax.axis_index("dom") % 2
    first_rows[...] = picked[pl.ds(pl.multiple_of((1 - odd) * half, half), half), :].astype(first_rows.dtype)
    second_rows[...] = picked[pl.ds(pl.multiple_of(odd * half, half), half), :].astype(second_rows.dtype)
    copy_blocks.wait()


def gather_rows(send_rows, tmat, blocks):
    width, picked = tmat.shape[1], send_rows.size
    return pl.pallas_call(
        gather_kernel,
        out_shape=[jax.ShapeDtypeStruct((picked // 2, width), tmat.dtype)] * 2
        + [jax.ShapeDtypeStruct(a.shape, a.dtype) for a in (tmat, blocks)],
        in_specs=[NEAR] + [FAR] * 2,
        out_specs=[NEAR] * 4,
        scratch_shapes=[
            pltpu.VMEM((picked, width), jnp.float32),
            pltpu.SemaphoreType.DMA((tmat.shape[0] // picked + 1,)),
        ],
        compiler_params=room_for(nbytes(tmat), nbytes(blocks), 6 * picked * width),
        cost_estimate=near_nothing(),
    )(send_rows, *far(tmat, blocks))


def own_kernel(row0, nrows, shift, bsize, first, owner_row, entries, blocks, panel, acc):
    acc[...] = jnp.zeros_like(acc)
    lists = (first, owner_row, entries)
    products(lists, first[0, row0], first[0, row0 + nrows], row0, shift, stored(blocks, shift), panel, acc, bsize)


def own_products(lists, blocks, panel, shift, row0, nrows):
    bsize, width = blocks.shape[1], panel.shape[1]
    return pl.pallas_call(
        functools.partial(own_kernel, row0, nrows, shift, bsize),
        out_shape=jax.ShapeDtypeStruct((nrows * bsize, width), jnp.float32),
        in_specs=[SCALAR] * 3 + [NEAR] * 2,
        out_specs=NEAR,
        compiler_params=room_for(4 * nrows * bsize * width),
        cost_estimate=near_nothing(),
    )(*lists, blocks, panel)


def place_halo(even, odd, halo):
    sides = even.shape[0]
    odd_partition = lax.axis_index("dom") % 2
    halo[pl.ds(pl.multiple_of((1 - odd_partition) * sides, sides), sides), :] = even[...]
    halo[pl.ds(pl.multiple_of(odd_partition * sides, sides), sides), :] = odd[...]


def pieces_kernel(nrows_blk, row0, nrows, shift, bsize, other0, n_col, first, owner_row, entries, blocks, even, odd, own, tmat, after, out, halo, acc, sem):
    panel_column = lax.axis_index("col") == n_col - 1

    @pl.when(panel_column)
    def _():
        acc[...] = own[...]
        place_halo(even, odd, halo)
        lists = (first, owner_row, entries)
        products(lists, *shared_range(first, nrows_blk, row0, nrows), row0, shift, stored(blocks, shift), halo, acc, bsize)
        out[...] = acc[...].astype(out.dtype)

    @pl.when(jnp.logical_not(panel_column))
    def _():
        copy = pltpu.make_async_copy(tmat.at[pl.ds(other0, out.shape[0])], out, sem)
        copy.start()
        copy.wait()


def piece(lists, blocks, even, odd, own, tmat, after, shift, row0, nrows, other0, n_col):
    bsize, width = blocks.shape[1], tmat.shape[1]
    size = nrows * bsize
    return pl.pallas_call(
        functools.partial(pieces_kernel, tmat.shape[0] // bsize, row0, nrows, shift, bsize, other0, n_col),
        out_shape=jax.ShapeDtypeStruct((size, width), tmat.dtype),
        in_specs=[SCALAR] * 3 + [NEAR] * 4 + [FAR, ANYWHERE],
        out_specs=NEAR,
        scratch_shapes=[
            pltpu.VMEM((2 * even.shape[0], width), tmat.dtype),
            pltpu.VMEM((size, width), jnp.float32),
            pltpu.SemaphoreType.DMA,
        ],
        compiler_params=room_for(2 * nbytes(even), 6 * size * width),
        cost_estimate=near_nothing(),
    )(*lists, blocks, even, odd, own, *far(tmat), after)


def mass_kernel(nrows_blk, row0, nrows, shift, bsize, first, owner_row, entries, blocks, panel, even, odd, after, out, halo, acc):
    lists = (first, owner_row, entries)
    acc[...] = jnp.zeros_like(acc)
    place_halo(even, odd, halo)
    block_of = stored(blocks, shift)
    products(lists, first[0, row0], first[0, row0 + nrows], row0, shift, block_of, panel, acc, bsize)
    products(lists, *shared_range(first, nrows_blk, row0, nrows), row0, shift, block_of, halo, acc, bsize)
    out[...] = acc[...].astype(out.dtype)


def known_kernel(left, right, out):
    out[...] = contract(left[...], right[...])


def known_product(left, right):
    rows, width = right.shape[0], left.shape[1]
    return pl.pallas_call(
        known_kernel,
        grid=(1,),
        out_shape=jax.ShapeDtypeStruct((width, right.shape[1]), jnp.float32),
        in_specs=[pl.BlockSpec((rows, width), lambda i: (0, 0)), pl.BlockSpec(right.shape, lambda i: (0, 0))],
        out_specs=pl.BlockSpec((width, right.shape[1]), lambda i: (0, 0)),
        compiler_params=room_for(4 * nbytes(right), 8 * width * width),
        cost_estimate=near_nothing(),
    )(left, right)


def mass_rows(lists, blocks, panel, even, odd, after, shift, row0, nrows):
    bsize, width = blocks.shape[1], panel.shape[1]
    return pl.pallas_call(
        functools.partial(mass_kernel, panel.shape[0] // bsize, row0, nrows, shift, bsize),
        out_shape=jax.ShapeDtypeStruct((nrows * bsize, width), panel.dtype),
        in_specs=[SCALAR] * 3 + [NEAR] * 4 + [ANYWHERE],
        out_specs=NEAR,
        scratch_shapes=[
            pltpu.VMEM((2 * even.shape[0], width), panel.dtype),
            pltpu.VMEM((nrows * bsize, width), jnp.float32),
        ],
        compiler_params=room_for(4 * nbytes(even), 6 * nrows * bsize * width),
        cost_estimate=near_nothing(),
    )(*lists, blocks, panel, even, odd, after)


def fold_kernel(bit, terms, *refs):
    parts, (keep, send) = refs[:terms], refs[terms:]
    mine = (lax.axis_index("dom") // bit) % 2
    for o in range(keep.shape[0]):
        for out, side in ((keep, mine), (send, 1 - mine)):
            total = parts[0][o, side]
            for part in parts[1:]:
                total += part[o, side]
            out[o] = total


def fold(bit, *parts):
    outer, _, rows, width = parts[0].shape
    half = jax.ShapeDtypeStruct((outer, rows, width), jnp.float32)
    return pl.pallas_call(
        functools.partial(fold_kernel, bit, len(parts)),
        out_shape=[half] * 2,
        in_specs=[NEAR] * len(parts),
        out_specs=[NEAR] * 2,
        compiler_params=pltpu.CompilerParams(vmem_limit_bytes=12 << 20),
        cost_estimate=near_nothing(),
    )(*parts)


def scatter(x, bits, route, beside=()):
    targets, rows, width = x.shape
    parts = (x,)
    for bit in reversed(bits):
        targets //= 2
        keep, send = fold(bit, *(p.reshape(targets, 2, rows, width) for p in parts))
        got = lax.ppermute(send, *route(bit))
        if beside and bit == bits[-2]:
            got, *beside = lax.optimization_barrier((got, *beside))
        parts = (keep, got)
    return (parts[0] + parts[1]).reshape(rows, width), *beside


def body(tmat, stored_mass_blocks, block_index, live_block_count, send_rows):
    n_col, n_dom = lax.axis_size("col"), lax.axis_size("dom")
    owner = n_col - 1
    col, dom = lax.axis_index("col"), lax.axis_index("dom")
    rows_dev, width = tmat.shape
    bsize = stored_mass_blocks.shape[1]
    nrows_blk = rows_dev // bsize
    share = width // n_dom
    shift = nrows_blk.bit_length()
    lists = slot_list(block_index, live_block_count, nrows_blk, shift, n_col)


    def exchange(block, begin):
        pairs = [(i * n_col + owner, (i + 1) * n_col + owner) for i in range(begin, n_dom - 1, 2)]
        return lax.ppermute(block, ("dom", "col"), pairs + [(b, a) for a, b in pairs])

    na = (nrows_blk * 13) // 32
    nb = nrows_blk - na
    *rows, panel, blocks = gather_rows(send_rows, tmat, stored_mass_blocks)
    even, odd = exchange(rows[0], 0), exchange(rows[1], 1)

    if n_col != 2 or n_dom < 4 or n_dom & (n_dom - 1):
        mass = mass_rows(lists, blocks, panel, even, odd, even, shift, 0, nrows_blk)
        total = lax.psum(contract(lax.psum(mass, "col"), tmat), "dom")
        return lax.dynamic_slice_in_dim(total, dom * share, share, 0)

    cut = nb * bsize
    early = cut - na * bsize
    ahead = lax.ppermute(tmat[:early], "col", [(0, 1)])

    own_a = own_products(lists, blocks, panel, shift, nb, na)
    sent = piece(lists, blocks, even, odd, own_a, tmat, ahead, shift, nb, na, early, n_col)
    got = lax.ppermute(sent, "col", [(0, 1), (1, 0)])
    mass_b = mass_rows(lists, blocks, panel, even, odd, sent, shift, 0, nb)
    own = contract(sent, tmat[cut:]) + contract(mass_b, tmat[:cut])
    known = known_product(mass_b, ahead)

    def both(bit):
        return "dom", [(i, i ^ bit) for i in range(n_dom)]

    def panel_column(bit):
        return ("dom", "col"), [(i * n_col + owner, (i ^ bit) * n_col + owner) for i in range(n_dom)]

    bits = [n_dom >> (b + 1) for b in range(n_dom.bit_length() - 1)]
    own, known = scatter(own.reshape(n_dom, share, width), bits, panel_column, (known,))
    got, own = lax.optimization_barrier((got, own))

    x = contract(jnp.where(col == owner, mass_b[early:], got), jnp.where(col == owner, got, tmat[cut:])) + known
    (x,) = scatter(x.reshape(n_dom, share, width), bits, both)
    other = x + lax.ppermute(x, "col", [(1, 0)])
    return jnp.where(col == owner, own, other)


def solution(mesh):
    return jax.shard_map(
        body,
        mesh=mesh,
        in_specs=(P("dom", "col"), P("dom", None, None), P("dom", None), P("dom"), P("dom", None)),
        out_specs=P("dom", "col"),
        check_vma=False,
    )
```

```python
import functools

import jax
import jax.numpy as jnp
from jax import lax
from jax.experimental import pallas as pl
from jax.experimental.pallas import tpu as pltpu
from jax.sharding import PartitionSpec as P

GROUP = 4
UNROLL = 8

ANYWHERE = pl.BlockSpec(memory_space=pl.ANY)
FAR = pl.BlockSpec(memory_space=pltpu.HBM)
NEAR = pl.BlockSpec(memory_space=pltpu.VMEM)
SCALAR = pl.BlockSpec(memory_space=pltpu.SMEM)


def contract(left, right):
    return lax.dot_general(
        left, right, (((0,), (0,)), ((), ())), preferred_element_type=jnp.float32
    )


def far(*arrays):
    return [pltpu.with_memory_space_constraint(a, pltpu.HBM) for a in arrays]


def room_for(*sizes):
    return pltpu.CompilerParams(vmem_limit_bytes=(6 << 20) + sum(sizes))


def nbytes(array):
    return array.size * array.dtype.itemsize


def near_nothing():
    return pl.CostEstimate(flops=1, bytes_accessed=1, transcendentals=0)


def columns_of(rows):
    count, width = rows.shape
    return jnp.concatenate([rows, jnp.zeros((8 - count, width), rows.dtype)], 0).T


def slot_kernel(nrows_blk, shift, n_col, live_count, index, first, owner_row, entries):
    slots = index.shape[1]
    nkeys = 2 * nrows_blk
    live = jnp.where(lax.axis_index("col") == n_col - 1, live_count[0], 0)

    def count_up(shape, axis):
        return lax.broadcasted_iota(jnp.int32, shape, axis)

    def keys_of(rows, cols):
        return rows + jnp.where(cols >= nrows_blk, nrows_blk, 0)

    def groups_of(hits, axis):
        return (jnp.sum(hits.astype(jnp.int32), axis, keepdims=True) + (GROUP - 1)) // GROUP

    across = index[...]
    down = columns_of(across)
    row_a, col_a = across[0:1], across[1:2]
    row_d, col_d = down[:, 0:1], down[:, 1:2]
    key_a, key_d = keys_of(row_a, col_a), keys_of(row_d, col_d)
    k_a, k_d = count_up((1, slots), 1), count_up((slots, 1), 0)
    alive_a, alive_d = k_a < live, k_d < live
    rank = jnp.sum(((key_a == key_d) & alive_a & (k_a < k_d)).astype(jnp.int32), 1, keepdims=True)
    groups_d = groups_of((key_a == count_up((nkeys, 1), 0)) & alive_a, 1)
    groups_a = groups_of((key_d == count_up((1, nkeys), 1)) & alive_d, 0)
    room = first.shape[1]
    first_a = jnp.sum(jnp.where(count_up((nkeys, room), 0) < count_up((nkeys, room), 1), groups_d, 0), 0, keepdims=True)
    first_d = jnp.sum(jnp.where(count_up((nkeys, nkeys), 1) < count_up((nkeys, nkeys), 0), groups_a, 0), 1, keepdims=True)
    first[...] = first_a
    started = (first_d <= count_up((nkeys, owner_row.shape[1]), 1)).astype(jnp.int32)
    key = jnp.sum(started, 0, keepdims=True) - 1
    owner_row[...] = jnp.where(key >= nrows_blk, key - nrows_blk, key)
    begin = jnp.sum(jnp.where(key_d == count_up((slots, room), 1), first_a, 0), 1, keepdims=True)
    place = begin * GROUP + rank
    value = ((k_d + 1) << shift) + col_d - jnp.where(col_d >= nrows_blk, nrows_blk, 0)
    hit = (place == count_up((slots, entries.shape[1]), 1)) & alive_d
    entries[...] = jnp.sum(jnp.where(hit, value, 0), 0, keepdims=True)


def slot_list(block_index, live_block_count, nrows_blk, shift, n_col):
    slots = block_index.shape[0]
    total = slots // GROUP + 2 * nrows_blk

    def lanes(n):
        return jax.ShapeDtypeStruct((1, -(-n // 128) * 128), jnp.int32)

    return pl.pallas_call(
        functools.partial(slot_kernel, nrows_blk, shift, n_col),
        out_shape=[lanes(2 * nrows_blk + 1), lanes(total), lanes(total * GROUP)],
        in_specs=[SCALAR, NEAR],
        out_specs=[NEAR] * 3,
        compiler_params=room_for(),
        cost_estimate=near_nothing(),
    )(live_block_count, block_index.T)


def products(lists, begin, end, row0, shift, block_of, source, acc, bsize):
    _, owner_row, entries = lists

    @pl.loop(0, (end - begin + UNROLL - 1) // UNROLL)
    def _(step):
        rows, prods = [], []
        for u in range(UNROLL):
            g = begin + step * UNROLL + u
            inside = g < end
            g = jnp.minimum(g, end - 1)
            rows.append(jnp.where(inside, owner_row[0, g] - row0, 0))
            left, right = [], []
            for j in range(GROUP):
                entry = jnp.where(inside, entries[0, g * GROUP + j], 0)
                block = block_of(g, j, entry)
                column = entry & ((1 << shift) - 1)
                left.append(jnp.where(entry > 0, block, jnp.zeros_like(block)))
                right.append(source[pl.ds(pl.multiple_of(column * bsize, bsize), bsize), :])
            prods.append(
                jnp.dot(jnp.concatenate(left, 1), jnp.concatenate(right, 0), preferred_element_type=jnp.float32)
            )
        for row, prod in zip(rows, prods):
            acc[pl.ds(pl.multiple_of(row * bsize, bsize), bsize), :] += prod


def stored(blocks, shift):
    return lambda g, j, entry: blocks[jnp.maximum((entry >> shift) - 1, 0)]


def shared_range(first, nrows_blk, row0, nrows):
    return first[0, nrows_blk + row0], first[0, nrows_blk + row0 + nrows]


def gather_kernel(send_rows, tmat, blocks, first_rows, second_rows, panel, near_blocks, picked, sem):
    count = picked.shape[0]
    depth = 2 * count
    steps = panel.shape[0] // depth
    copy_blocks = pltpu.make_async_copy(blocks, near_blocks, sem.at[steps])

    def part(step):
        chunk = pl.ds(pl.multiple_of(step * depth, depth), depth)
        return pltpu.make_async_copy(tmat.at[chunk], panel.at[chunk], sem.at[step])

    for step in range(steps):
        part(step).start()
    copy_blocks.start()
    picked[...] = jnp.zeros_like(picked)
    lists = columns_of(send_rows[...])
    wanted = jnp.concatenate([lists[:, 0:1], lists[:, 1:2]], 0)

    @pl.loop(0, steps)
    def _(step):
        part(step).wait()
        begin = pl.multiple_of(step * depth, depth)
        numbers = lax.broadcasted_iota(jnp.int32, (count, depth), 1) + begin
        picks = jnp.where(wanted == numbers, 1.0, 0.0).astype(panel.dtype)
        picked[...] += jnp.dot(picks, panel[pl.ds(begin, depth), :], preferred_element_type=jnp.float32)

    half = count // 2
    odd = lax.axis_index("dom") % 2
    first_rows[...] = picked[pl.ds(pl.multiple_of((1 - odd) * half, half), half), :].astype(first_rows.dtype)
    second_rows[...] = picked[pl.ds(pl.multiple_of(odd * half, half), half), :].astype(second_rows.dtype)
    copy_blocks.wait()


def gather_rows(send_rows, tmat, blocks):
    width, picked = tmat.shape[1], send_rows.size
    return pl.pallas_call(
        gather_kernel,
        out_shape=[jax.ShapeDtypeStruct((picked // 2, width), tmat.dtype)] * 2
        + [jax.ShapeDtypeStruct(a.shape, a.dtype) for a in (tmat, blocks)],
        in_specs=[NEAR] + [FAR] * 2,
        out_specs=[NEAR] * 4,
        scratch_shapes=[
            pltpu.VMEM((picked, width), jnp.float32),
            pltpu.SemaphoreType.DMA((tmat.shape[0] // (2 * picked) + 1,)),
        ],
        compiler_params=room_for(nbytes(tmat), nbytes(blocks), 6 * picked * width),
        cost_estimate=near_nothing(),
    )(send_rows, *far(tmat, blocks))


def own_kernel(row0, nrows, shift, bsize, first, owner_row, entries, blocks, panel, acc):
    acc[...] = jnp.zeros_like(acc)
    lists = (first, owner_row, entries)
    products(lists, first[0, row0], first[0, row0 + nrows], row0, shift, stored(blocks, shift), panel, acc, bsize)


def own_products(lists, blocks, panel, shift, row0, nrows):
    bsize, width = blocks.shape[1], panel.shape[1]
    return pl.pallas_call(
        functools.partial(own_kernel, row0, nrows, shift, bsize),
        out_shape=jax.ShapeDtypeStruct((nrows * bsize, width), jnp.float32),
        in_specs=[SCALAR] * 3 + [NEAR] * 2,
        out_specs=NEAR,
        compiler_params=room_for(4 * nrows * bsize * width),
        cost_estimate=near_nothing(),
    )(*lists, blocks, panel)


def place_halo(even, odd, halo):
    sides = even.shape[0]
    odd_partition = lax.axis_index("dom") % 2
    halo[pl.ds(pl.multiple_of((1 - odd_partition) * sides, sides), sides), :] = even[...]
    halo[pl.ds(pl.multiple_of(odd_partition * sides, sides), sides), :] = odd[...]


def pieces_kernel(nrows_blk, row0, nrows, shift, bsize, other0, n_col, first, owner_row, entries, blocks, odd, even, own, tmat, out, halo, acc, sem):
    panel_column = lax.axis_index("col") == n_col - 1

    @pl.when(panel_column)
    def _():
        acc[...] = own[...]
        place_halo(even, odd, halo)
        lists = (first, owner_row, entries)
        products(lists, *shared_range(first, nrows_blk, row0, nrows), row0, shift, stored(blocks, shift), halo, acc, bsize)
        out[...] = acc[...].astype(out.dtype)

    @pl.when(jnp.logical_not(panel_column))
    def _():
        copy = pltpu.make_async_copy(tmat.at[pl.ds(other0, out.shape[0])], out, sem)
        copy.start()
        copy.wait()


def piece(lists, blocks, odd, even, own, tmat, shift, row0, nrows, other0, n_col):
    bsize, width = blocks.shape[1], tmat.shape[1]
    size = nrows * bsize
    return pl.pallas_call(
        functools.partial(pieces_kernel, tmat.shape[0] // bsize, row0, nrows, shift, bsize, other0, n_col),
        out_shape=jax.ShapeDtypeStruct((size, width), tmat.dtype),
        in_specs=[SCALAR] * 3 + [NEAR] * 4 + [FAR],
        out_specs=NEAR,
        scratch_shapes=[
            pltpu.VMEM((2 * even.shape[0], width), tmat.dtype),
            pltpu.VMEM((size, width), jnp.float32),
            pltpu.SemaphoreType.DMA,
        ],
        compiler_params=room_for(2 * nbytes(even), 6 * size * width),
        cost_estimate=near_nothing(),
    )(*lists, blocks, odd, even, own, *far(tmat))


def mass_kernel(nrows_blk, row0, nrows, shift, bsize, first, owner_row, entries, blocks, panel, odd, even, after, out, halo, acc):
    lists = (first, owner_row, entries)
    acc[...] = jnp.zeros_like(acc)
    place_halo(even, odd, halo)
    block_of = stored(blocks, shift)
    products(lists, first[0, row0], first[0, row0 + nrows], row0, shift, block_of, panel, acc, bsize)
    products(lists, *shared_range(first, nrows_blk, row0, nrows), row0, shift, block_of, halo, acc, bsize)
    out[...] = acc[...].astype(out.dtype)


def known_kernel(left, right, out):
    out[...] = contract(left[...], right[...])


def known_product(left, right):
    rows, width = right.shape[0], left.shape[1]
    return pl.pallas_call(
        known_kernel,
        grid=(1,),
        out_shape=jax.ShapeDtypeStruct((width, right.shape[1]), jnp.float32),
        in_specs=[pl.BlockSpec((rows, width), lambda i: (0, 0)), pl.BlockSpec(right.shape, lambda i: (0, 0))],
        out_specs=pl.BlockSpec((width, right.shape[1]), lambda i: (0, 0)),
        compiler_params=room_for(4 * nbytes(right), 8 * width * width),
        cost_estimate=near_nothing(),
    )(left, right)


def mass_rows(lists, blocks, panel, odd, even, after, shift, row0, nrows):
    bsize, width = blocks.shape[1], panel.shape[1]
    return pl.pallas_call(
        functools.partial(mass_kernel, panel.shape[0] // bsize, row0, nrows, shift, bsize),
        out_shape=jax.ShapeDtypeStruct((nrows * bsize, width), panel.dtype),
        in_specs=[SCALAR] * 3 + [NEAR] * 5,
        out_specs=NEAR,
        scratch_shapes=[
            pltpu.VMEM((2 * even.shape[0], width), panel.dtype),
            pltpu.VMEM((nrows * bsize, width), jnp.float32),
        ],
        compiler_params=room_for(4 * nbytes(even), 6 * nrows * bsize * width, nbytes(after)),
        cost_estimate=near_nothing(),
    )(*lists, blocks, panel, odd, even, after)


def fold_kernel(bit, inner, counts, *refs):
    keep, send = refs[-2:]
    mine = (lax.axis_index("dom") // bit) % 2
    for t in range(keep.shape[0]):
        outer, rest = divmod(t, inner)
        for out, side in ((keep, mine), (send, 1 - mine)):
            place = (2 * outer + side) * inner + rest
            sources, col = refs[:-2], 0
            for count, begin, width in counts:
                cols = pl.ds(begin, width)
                total = sources[0][place, :, cols]
                for part in sources[1:count]:
                    total += part[place, :, cols]
                out[t, :, pl.ds(col, width)] = total
                sources, col = sources[count:], col + width


def fold(bit, inner, *columns):
    targets, rows, _ = columns[0][0][0].shape
    half = jax.ShapeDtypeStruct((targets // 2, rows, sum(width for _, _, width in columns)), jnp.float32)
    arrays = [a for some, _, _ in columns for a in some]
    return pl.pallas_call(
        functools.partial(fold_kernel, bit, inner, [(len(some), begin, width) for some, begin, width in columns]),
        out_shape=[half] * 2,
        in_specs=[NEAR] * len(arrays),
        out_specs=[NEAR] * 2,
        compiler_params=room_for(),
        cost_estimate=near_nothing(),
    )(*arrays)


def step(route, bit, inner, *columns):
    keep, send = fold(bit, inner, *columns)
    return [keep, lax.ppermute(send, *route(bit))]


def scatter(x, route):
    targets, rows, width = x.shape
    half = width // 2
    whole = step(route, 1, 1, ([x], 0, width))
    left, right = step(route, 2, 1, (whole, 0, half)), step(route, 4, 2, (whole, half, half))
    left, right = step(route, 4, 1, (left, 0, half)), step(route, 2, 1, (right, 0, half))
    bit, columns = 8, [(left, 0, half), (right, 0, half)]
    while bit < targets:
        columns = [(step(route, bit, 1, *columns), 0, width)]
        bit *= 2
    return jnp.concatenate([a + b for (a, b), _, _ in columns], 2).reshape(rows, width)


def body(tmat, stored_mass_blocks, block_index, live_block_count, send_rows):
    n_col, n_dom = lax.axis_size("col"), lax.axis_size("dom")
    owner = n_col - 1
    col, dom = lax.axis_index("col"), lax.axis_index("dom")
    rows_dev, width = tmat.shape
    bsize = stored_mass_blocks.shape[1]
    nrows_blk = rows_dev // bsize
    share = width // n_dom
    shift = nrows_blk.bit_length()
    lists = slot_list(block_index, live_block_count, nrows_blk, shift, n_col)


    def exchange(block, begin):
        pairs = [(i * n_col + owner, (i + 1) * n_col + owner) for i in range(begin, n_dom - 1, 2)]
        return lax.ppermute(block, ("dom", "col"), pairs + [(b, a) for a, b in pairs])

    na = (nrows_blk * 13) // 32
    nb = nrows_blk - na
    *rows, panel, blocks = gather_rows(send_rows, tmat, stored_mass_blocks)
    even, odd = exchange(rows[0], 0), exchange(rows[1], 1)

    if n_col != 2 or n_dom < 8 or n_dom & (n_dom - 1):
        mass = mass_rows(lists, blocks, panel, odd, even, even, shift, 0, nrows_blk)
        total = lax.psum(contract(lax.psum(mass, "col"), tmat), "dom")
        return lax.dynamic_slice_in_dim(total, dom * share, share, 0)

    cut = nb * bsize
    early = cut - na * bsize
    ahead = lax.ppermute(tmat[:early], "col", [(0, 1)])

    own_a = own_products(lists, blocks, panel, shift, nb, na)
    sent = piece(lists, blocks, odd, even, own_a, tmat, shift, nb, na, early, n_col)
    sent, ahead = lax.optimization_barrier((sent, ahead))
    got = lax.ppermute(sent, "col", [(0, 1), (1, 0)])
    mass_b = mass_rows(lists, blocks, panel, odd, even, sent, shift, 0, nb)
    own = contract(sent, panel[cut:]) + contract(mass_b, panel[:cut])
    known = known_product(mass_b, ahead)

    def both(bit):
        return "dom", [(i, i ^ bit) for i in range(n_dom)]

    def panel_column(bit):
        return ("dom", "col"), [(i * n_col + owner, (i ^ bit) * n_col + owner) for i in range(n_dom)]

    parts, bit = [own.reshape(n_dom, share, width)], 1
    while bit < n_dom // 2:
        parts = step(panel_column, bit, 1, (parts, 0, width))
        if bit == 2:
            parts[1], known = lax.optimization_barrier((parts[1], known))
        bit *= 2
    got, parts[1] = lax.optimization_barrier((got, parts[1]))
    parts = step(panel_column, bit, 1, (parts, 0, width))
    own = (parts[0] + parts[1]).reshape(share, width)

    x = contract(jnp.where(col == owner, mass_b[early:], got), jnp.where(col == owner, got, panel[cut:])) + known
    x = scatter(x.reshape(n_dom, share, width), both)
    other = x + lax.ppermute(x, "col", [(1, 0)])
    return jnp.where(col == owner, own, other)


def solution(mesh):
    return jax.shard_map(
        body,
        mesh=mesh,
        in_specs=(P("dom", "col"), P("dom", None, None), P("dom", None), P("dom"), P("dom", None)),
        out_specs=P("dom", "col"),
        check_vma=False,
    )
```

```python
import functools

import jax
import jax.numpy as jnp
from jax import lax
from jax.experimental import pallas as pl
from jax.experimental.pallas import tpu as pltpu
from jax.sharding import PartitionSpec as P

GROUP = 4
UNROLL = 8

ANYWHERE = pl.BlockSpec(memory_space=pl.ANY)
FAR = pl.BlockSpec(memory_space=pltpu.HBM)
NEAR = pl.BlockSpec(memory_space=pltpu.VMEM)
SCALAR = pl.BlockSpec(memory_space=pltpu.SMEM)


def contract(left, right):
    return lax.dot_general(
        left, right, (((0,), (0,)), ((), ())), preferred_element_type=jnp.float32
    )


def far(*arrays):
    return [pltpu.with_memory_space_constraint(a, pltpu.HBM) for a in arrays]


def room_for(*sizes):
    return pltpu.CompilerParams(vmem_limit_bytes=(6 << 20) + sum(sizes))


def nbytes(array):
    return array.size * array.dtype.itemsize


def near_nothing():
    return pl.CostEstimate(flops=1, bytes_accessed=1, transcendentals=0)


def columns_of(rows):
    count, width = rows.shape
    return jnp.concatenate([rows, jnp.zeros((8 - count, width), rows.dtype)], 0).T


def slot_kernel(nrows_blk, shift, n_col, live_count, index, first, owner_row, entries):
    slots = index.shape[1]
    nkeys = 2 * nrows_blk
    live = jnp.where(lax.axis_index("col") == n_col - 1, live_count[0], 0)

    def count_up(shape, axis):
        return lax.broadcasted_iota(jnp.int32, shape, axis)

    def keys_of(rows, cols):
        return rows + jnp.where(cols >= nrows_blk, nrows_blk, 0)

    def groups_of(hits, axis):
        return (jnp.sum(hits.astype(jnp.int32), axis, keepdims=True) + (GROUP - 1)) // GROUP

    across = index[...]
    down = columns_of(across)
    row_a, col_a = across[0:1], across[1:2]
    row_d, col_d = down[:, 0:1], down[:, 1:2]
    key_a, key_d = keys_of(row_a, col_a), keys_of(row_d, col_d)
    k_a, k_d = count_up((1, slots), 1), count_up((slots, 1), 0)
    alive_a, alive_d = k_a < live, k_d < live
    rank = jnp.sum(((key_a == key_d) & alive_a & (k_a < k_d)).astype(jnp.int32), 1, keepdims=True)
    groups_d = groups_of((key_a == count_up((nkeys, 1), 0)) & alive_a, 1)
    groups_a = groups_of((key_d == count_up((1, nkeys), 1)) & alive_d, 0)
    room = first.shape[1]
    first_a = jnp.sum(jnp.where(count_up((nkeys, room), 0) < count_up((nkeys, room), 1), groups_d, 0), 0, keepdims=True)
    first_d = jnp.sum(jnp.where(count_up((nkeys, nkeys), 1) < count_up((nkeys, nkeys), 0), groups_a, 0), 1, keepdims=True)
    first[...] = first_a
    started = (first_d <= count_up((nkeys, owner_row.shape[1]), 1)).astype(jnp.int32)
    key = jnp.sum(started, 0, keepdims=True) - 1
    owner_row[...] = jnp.where(key >= nrows_blk, key - nrows_blk, key)
    begin = jnp.sum(jnp.where(key_d == count_up((slots, room), 1), first_a, 0), 1, keepdims=True)
    place = begin * GROUP + rank
    value = ((k_d + 1) << shift) + col_d - jnp.where(col_d >= nrows_blk, nrows_blk, 0)
    hit = (place == count_up((slots, entries.shape[1]), 1)) & alive_d
    entries[...] = jnp.sum(jnp.where(hit, value, 0), 0, keepdims=True)


def slot_list(block_index, live_block_count, nrows_blk, shift, n_col):
    slots = block_index.shape[0]
    total = slots // GROUP + 2 * nrows_blk

    def lanes(n):
        return jax.ShapeDtypeStruct((1, -(-n // 128) * 128), jnp.int32)

    return pl.pallas_call(
        functools.partial(slot_kernel, nrows_blk, shift, n_col),
        out_shape=[lanes(2 * nrows_blk + 1), lanes(total), lanes(total * GROUP)],
        in_specs=[SCALAR, NEAR],
        out_specs=[NEAR] * 3,
        compiler_params=room_for(),
        cost_estimate=near_nothing(),
    )(live_block_count, block_index.T)


def products(lists, begin, end, row0, shift, block_of, source, acc, bsize):
    _, owner_row, entries = lists

    @pl.loop(0, (end - begin + UNROLL - 1) // UNROLL)
    def _(step):
        rows, prods = [], []
        for u in range(UNROLL):
            g = begin + step * UNROLL + u
            inside = g < end
            g = jnp.minimum(g, end - 1)
            rows.append(jnp.where(inside, owner_row[0, g] - row0, 0))
            left, right = [], []
            for j in range(GROUP):
                entry = jnp.where(inside, entries[0, g * GROUP + j], 0)
                block = block_of(g, j, entry)
                column = entry & ((1 << shift) - 1)
                left.append(jnp.where(entry > 0, block, jnp.zeros_like(block)))
                right.append(source[pl.ds(pl.multiple_of(column * bsize, bsize), bsize), :])
            prods.append(
                jnp.dot(jnp.concatenate(left, 1), jnp.concatenate(right, 0), preferred_element_type=jnp.float32)
            )
        for row, prod in zip(rows, prods):
            acc[pl.ds(pl.multiple_of(row * bsize, bsize), bsize), :] += prod


def stored(blocks, shift):
    return lambda g, j, entry: blocks[jnp.maximum((entry >> shift) - 1, 0)]


def shared_range(first, nrows_blk, row0, nrows):
    return first[0, nrows_blk + row0], first[0, nrows_blk + row0 + nrows]


def gather_kernel(send_rows, tmat, blocks, first_rows, second_rows, panel, near_blocks, picked, sem):
    count = picked.shape[0]
    depth = 2 * count
    steps = panel.shape[0] // depth
    copy_blocks = pltpu.make_async_copy(blocks, near_blocks, sem.at[steps])

    def part(step):
        chunk = pl.ds(pl.multiple_of(step * depth, depth), depth)
        return pltpu.make_async_copy(tmat.at[chunk], panel.at[chunk], sem.at[step])

    for step in range(steps):
        part(step).start()
    copy_blocks.start()
    picked[...] = jnp.zeros_like(picked)
    lists = columns_of(send_rows[...])
    wanted = jnp.concatenate([lists[:, 0:1], lists[:, 1:2]], 0)

    @pl.loop(0, steps)
    def _(step):
        part(step).wait()
        begin = pl.multiple_of(step * depth, depth)
        numbers = lax.broadcasted_iota(jnp.int32, (count, depth), 1) + begin
        picks = jnp.where(wanted == numbers, 1.0, 0.0).astype(panel.dtype)
        picked[...] += jnp.dot(picks, panel[pl.ds(begin, depth), :], preferred_element_type=jnp.float32)

    half = count // 2
    odd = lax.axis_index("dom") % 2
    first_rows[...] = picked[pl.ds(pl.multiple_of((1 - odd) * half, half), half), :].astype(first_rows.dtype)
    second_rows[...] = picked[pl.ds(pl.multiple_of(odd * half, half), half), :].astype(second_rows.dtype)
    copy_blocks.wait()


def gather_rows(send_rows, tmat, blocks):
    width, picked = tmat.shape[1], send_rows.size
    return pl.pallas_call(
        gather_kernel,
        out_shape=[jax.ShapeDtypeStruct((picked // 2, width), tmat.dtype)] * 2
        + [jax.ShapeDtypeStruct(a.shape, a.dtype) for a in (tmat, blocks)],
        in_specs=[NEAR] + [FAR] * 2,
        out_specs=[NEAR] * 4,
        scratch_shapes=[
            pltpu.VMEM((picked, width), jnp.float32),
            pltpu.SemaphoreType.DMA((tmat.shape[0] // (2 * picked) + 1,)),
        ],
        compiler_params=room_for(nbytes(tmat), nbytes(blocks), 6 * picked * width),
        cost_estimate=near_nothing(),
    )(send_rows, *far(tmat, blocks))


def own_kernel(row0, nrows, shift, bsize, first, owner_row, entries, blocks, panel, acc):
    acc[...] = jnp.zeros_like(acc)
    lists = (first, owner_row, entries)
    products(lists, first[0, row0], first[0, row0 + nrows], row0, shift, stored(blocks, shift), panel, acc, bsize)


def own_products(lists, blocks, panel, shift, row0, nrows):
    bsize, width = blocks.shape[1], panel.shape[1]
    return pl.pallas_call(
        functools.partial(own_kernel, row0, nrows, shift, bsize),
        out_shape=jax.ShapeDtypeStruct((nrows * bsize, width), jnp.float32),
        in_specs=[SCALAR] * 3 + [NEAR] * 2,
        out_specs=NEAR,
        compiler_params=room_for(4 * nrows * bsize * width),
        cost_estimate=near_nothing(),
    )(*lists, blocks, panel)


def place_halo(even, odd, halo):
    sides = even.shape[0]
    odd_partition = lax.axis_index("dom") % 2
    halo[pl.ds(pl.multiple_of((1 - odd_partition) * sides, sides), sides), :] = even[...]
    halo[pl.ds(pl.multiple_of(odd_partition * sides, sides), sides), :] = odd[...]


def pieces_kernel(nrows_blk, row0, nrows, shift, bsize, other0, n_col, first, owner_row, entries, blocks, odd, even, own, tmat, out, halo, acc, sem):
    panel_column = lax.axis_index("col") == n_col - 1

    @pl.when(panel_column)
    def _():
        acc[...] = own[...]
        place_halo(even, odd, halo)
        lists = (first, owner_row, entries)
        products(lists, *shared_range(first, nrows_blk, row0, nrows), row0, shift, stored(blocks, shift), halo, acc, bsize)
        out[...] = acc[...].astype(out.dtype)

    @pl.when(jnp.logical_not(panel_column))
    def _():
        copy = pltpu.make_async_copy(tmat.at[pl.ds(other0, out.shape[0])], out, sem)
        copy.start()
        copy.wait()


def piece(lists, blocks, odd, even, own, tmat, shift, row0, nrows, other0, n_col):
    bsize, width = blocks.shape[1], tmat.shape[1]
    size = nrows * bsize
    return pl.pallas_call(
        functools.partial(pieces_kernel, tmat.shape[0] // bsize, row0, nrows, shift, bsize, other0, n_col),
        out_shape=jax.ShapeDtypeStruct((size, width), tmat.dtype),
        in_specs=[SCALAR] * 3 + [NEAR] * 4 + [FAR],
        out_specs=NEAR,
        scratch_shapes=[
            pltpu.VMEM((2 * even.shape[0], width), tmat.dtype),
            pltpu.VMEM((size, width), jnp.float32),
            pltpu.SemaphoreType.DMA,
        ],
        compiler_params=room_for(2 * nbytes(even), 6 * size * width),
        cost_estimate=near_nothing(),
    )(*lists, blocks, odd, even, own, *far(tmat))


def mass_kernel(nrows_blk, row0, nrows, shift, bsize, first, owner_row, entries, blocks, panel, odd, even, after, out, halo, acc):
    lists = (first, owner_row, entries)
    acc[...] = jnp.zeros_like(acc)
    place_halo(even, odd, halo)
    block_of = stored(blocks, shift)
    products(lists, first[0, row0], first[0, row0 + nrows], row0, shift, block_of, panel, acc, bsize)
    products(lists, *shared_range(first, nrows_blk, row0, nrows), row0, shift, block_of, halo, acc, bsize)
    out[...] = acc[...].astype(out.dtype)


def add_contract(total, left, right, left0=0, right0=0, rows=None):
    depth = (left.shape[0] if rows is None else rows) // 4

    @pl.loop(0, 4)
    def _(i):
        begin = pl.multiple_of(i * depth, depth)
        total[...] += contract(left[pl.ds(left0 + begin, depth), :], right[pl.ds(right0 + begin, depth), :])


def panel_kernel(nrows_blk, nrows, shift, bsize, first, owner_row, entries, blocks, panel, odd, even, sent, out, result, halo, acc, near_sent, sem):
    copy = pltpu.make_async_copy(sent, near_sent, sem)
    copy.start()
    mass_kernel(nrows_blk, 0, nrows, shift, bsize, first, owner_row, entries, blocks, panel, odd, even, None, out, halo, acc)
    result[...] = jnp.zeros_like(result)
    add_contract(result, out, panel)
    copy.wait()
    add_contract(result, near_sent, panel, right0=nrows * bsize)


def panel_work(lists, blocks, panel, odd, even, sent, shift, nrows):
    bsize, width = blocks.shape[1], panel.shape[1]
    return pl.pallas_call(
        functools.partial(panel_kernel, panel.shape[0] // bsize, nrows, shift, bsize),
        out_shape=[
            jax.ShapeDtypeStruct((nrows * bsize, width), panel.dtype),
            jax.ShapeDtypeStruct((width, width), jnp.float32),
        ],
        in_specs=[SCALAR] * 3 + [NEAR] * 4 + [ANYWHERE],
        out_specs=[NEAR] * 2,
        scratch_shapes=[
            pltpu.VMEM((2 * even.shape[0], width), panel.dtype),
            pltpu.VMEM((nrows * bsize, width), jnp.float32),
            pltpu.VMEM(sent.shape, sent.dtype),
            pltpu.SemaphoreType.DMA,
        ],
        compiler_params=room_for(4 * nbytes(even), 6 * nrows * bsize * width, 2 * nbytes(sent), 4 * width * width),
        cost_estimate=near_nothing(),
    )(*lists, blocks, panel, odd, even, sent)


def partner_kernel(n_col, mass, ahead, panel, known, partner):
    early, rows = ahead.shape[0], partner.shape[0]
    panel_column = lax.axis_index("col") == n_col - 1
    known[...] = jnp.zeros_like(known)

    @pl.when(panel_column)
    def _():
        add_contract(known, mass, ahead, rows=early)
        partner[...] = mass[pl.ds(early, rows), :]

    @pl.when(jnp.logical_not(panel_column))
    def _():
        partner[...] = panel[pl.ds(panel.shape[0] - rows, rows), :]


def partner_rows(mass, ahead, panel, rows, n_col):
    width = mass.shape[1]
    return pl.pallas_call(
        functools.partial(partner_kernel, n_col),
        out_shape=[jax.ShapeDtypeStruct((width, width), jnp.float32), jax.ShapeDtypeStruct((rows, width), mass.dtype)],
        in_specs=[NEAR] * 3,
        out_specs=[NEAR] * 2,
        compiler_params=room_for(2 * nbytes(ahead), 4 * width * width, 4 * rows * width),
        cost_estimate=near_nothing(),
    )(mass, ahead, panel)


def meet_kernel(n_col, got, partner, known, out, near_got, sem):
    parts = sem.shape[0]
    depth = got.shape[0] // parts

    def part(i):
        some = pl.ds(pl.multiple_of(i * depth, depth), depth)
        return some, pltpu.make_async_copy(got.at[some], near_got.at[some], sem.at[i])

    for i in range(parts):
        part(i)[1].start()
    out[...] = known[...]
    panel_column = lax.axis_index("col") == n_col - 1

    @pl.when(panel_column)
    def _():
        @pl.loop(0, parts)
        def _(i):
            some, copy = part(i)
            copy.wait()
            out[...] += contract(partner[some, :], near_got[some, :])

    @pl.when(jnp.logical_not(panel_column))
    def _():
        @pl.loop(0, parts)
        def _(i):
            some, copy = part(i)
            copy.wait()
            out[...] += contract(near_got[some, :], partner[some, :])


def meet(got, partner, known, n_col):
    return pl.pallas_call(
        functools.partial(meet_kernel, n_col),
        out_shape=jax.ShapeDtypeStruct(known.shape, jnp.float32),
        in_specs=[ANYWHERE, NEAR, NEAR],
        out_specs=NEAR,
        scratch_shapes=[pltpu.VMEM(got.shape, got.dtype), pltpu.SemaphoreType.DMA((4,))],
        compiler_params=room_for(2 * nbytes(got), 2 * nbytes(known)),
        cost_estimate=near_nothing(),
    )(got, partner, known)


def mass_rows(lists, blocks, panel, odd, even, after, shift, row0, nrows):
    bsize, width = blocks.shape[1], panel.shape[1]
    return pl.pallas_call(
        functools.partial(mass_kernel, panel.shape[0] // bsize, row0, nrows, shift, bsize),
        out_shape=jax.ShapeDtypeStruct((nrows * bsize, width), panel.dtype),
        in_specs=[SCALAR] * 3 + [NEAR] * 5,
        out_specs=NEAR,
        scratch_shapes=[
            pltpu.VMEM((2 * even.shape[0], width), panel.dtype),
            pltpu.VMEM((nrows * bsize, width), jnp.float32),
        ],
        compiler_params=room_for(4 * nbytes(even), 6 * nrows * bsize * width, nbytes(after)),
        cost_estimate=near_nothing(),
    )(*lists, blocks, panel, odd, even, after)


def fold_kernel(bit, inner, counts, *refs):
    keep, send = refs[-2:]
    mine = (lax.axis_index("dom") // bit) % 2
    for t in range(keep.shape[0]):
        outer, rest = divmod(t, inner)
        for out, side in ((keep, mine), (send, 1 - mine)):
            place = (2 * outer + side) * inner + rest
            sources, col = refs[:-2], 0
            for count, begin, width in counts:
                cols = pl.ds(begin, width)
                total = sources[0][place, :, cols]
                for part in sources[1:count]:
                    total += part[place, :, cols]
                out[t, :, pl.ds(col, width)] = total
                sources, col = sources[count:], col + width


def fold(bit, inner, *columns):
    targets, rows, _ = columns[0][0][0].shape
    half = jax.ShapeDtypeStruct((targets // 2, rows, sum(width for _, _, width in columns)), jnp.float32)
    arrays = [a for some, _, _ in columns for a in some]
    return pl.pallas_call(
        functools.partial(fold_kernel, bit, inner, [(len(some), begin, width) for some, begin, width in columns]),
        out_shape=[half] * 2,
        in_specs=[NEAR] * len(arrays),
        out_specs=[NEAR] * 2,
        compiler_params=room_for(),
        cost_estimate=near_nothing(),
    )(*arrays)


def step(route, bit, inner, *columns):
    keep, send = fold(bit, inner, *columns)
    return [keep, lax.ppermute(send, *route(bit))]


def scatter(x, route):
    targets, rows, width = x.shape
    half = width // 2
    whole = step(route, 1, 1, ([x], 0, width))
    left, right = step(route, 2, 1, (whole, 0, half)), step(route, 4, 2, (whole, half, half))
    left, right = step(route, 4, 1, (left, 0, half)), step(route, 2, 1, (right, 0, half))
    bit, columns = 8, [(left, 0, half), (right, 0, half)]
    while bit < targets // 2:
        columns = [(step(route, bit, 1, *columns), 0, width)]
        bit *= 2
    return columns


def body(tmat, stored_mass_blocks, block_index, live_block_count, send_rows):
    n_col, n_dom = lax.axis_size("col"), lax.axis_size("dom")
    owner = n_col - 1
    col, dom = lax.axis_index("col"), lax.axis_index("dom")
    rows_dev, width = tmat.shape
    bsize = stored_mass_blocks.shape[1]
    nrows_blk = rows_dev // bsize
    share = width // n_dom
    shift = nrows_blk.bit_length()
    lists = slot_list(block_index, live_block_count, nrows_blk, shift, n_col)


    def exchange(block, begin):
        pairs = [(i * n_col + owner, (i + 1) * n_col + owner) for i in range(begin, n_dom - 1, 2)]
        return lax.ppermute(block, ("dom", "col"), pairs + [(b, a) for a, b in pairs])

    na = (nrows_blk * 13) // 32
    nb = nrows_blk - na
    *rows, panel, blocks = gather_rows(send_rows, tmat, stored_mass_blocks)
    even, odd = exchange(rows[0], 0), exchange(rows[1], 1)

    if n_col != 2 or n_dom < 16 or n_dom & (n_dom - 1):
        mass = mass_rows(lists, blocks, panel, odd, even, even, shift, 0, nrows_blk)
        total = lax.psum(contract(lax.psum(mass, "col"), tmat), "dom")
        return lax.dynamic_slice_in_dim(total, dom * share, share, 0)

    cut = nb * bsize
    early = cut - na * bsize
    ahead = lax.ppermute(tmat[:early], "col", [(0, 1)])

    own_a = own_products(lists, blocks, panel, shift, nb, na)
    sent = piece(lists, blocks, odd, even, own_a, tmat, shift, nb, na, early, n_col)
    sent, ahead = lax.optimization_barrier((sent, ahead))
    got = lax.ppermute(sent, "col", [(0, 1), (1, 0)])
    mass_b, own = panel_work(lists, blocks, panel, odd, even, sent, shift, nb)
    known, partner = partner_rows(mass_b, ahead, panel, na * bsize, n_col)

    def both(bit):
        return "dom", [(i, i ^ bit) for i in range(n_dom)]

    def panel_column(bit):
        return ("dom", "col"), [(i * n_col + owner, (i ^ bit) * n_col + owner) for i in range(n_dom)]

    parts, bit = [own.reshape(n_dom, share, width)], 1
    while bit < n_dom // 2:
        parts = step(panel_column, bit, 1, (parts, 0, width))
        if bit == 2:
            parts[1], known, partner = lax.optimization_barrier((parts[1], known, partner))
        bit *= 2
    got, parts[1] = lax.optimization_barrier((got, parts[1]))

    x = meet(got, partner, known, n_col)
    keep, got = step(both, bit, 1, *scatter(x.reshape(n_dom, share, width), both))
    own_keep, own_got = step(panel_column, bit, 1, (parts, 0, width))
    x = keep + got
    other = x + lax.ppermute(x, "col", [(1, 0)])
    return jnp.where(col == owner, own_keep + own_got, other).reshape(share, width)


def solution(mesh):
    return jax.shard_map(
        body,
        mesh=mesh,
        in_specs=(P("dom", "col"), P("dom", None, None), P("dom", None), P("dom"), P("dom", None)),
        out_specs=P("dom", "col"),
        check_vma=False,
    )
```

```python
import functools

import jax
import jax.numpy as jnp
from jax import lax
from jax.experimental import pallas as pl
from jax.experimental.pallas import tpu as pltpu
from jax.sharding import PartitionSpec as P

GROUP = 4
UNROLL = 8

ANYWHERE = pl.BlockSpec(memory_space=pl.ANY)
FAR = pl.BlockSpec(memory_space=pltpu.HBM)
NEAR = pl.BlockSpec(memory_space=pltpu.VMEM)
SCALAR = pl.BlockSpec(memory_space=pltpu.SMEM)


def contract(left, right):
    return lax.dot_general(
        left, right, (((0,), (0,)), ((), ())), preferred_element_type=jnp.float32
    )


def far(*arrays):
    return [pltpu.with_memory_space_constraint(a, pltpu.HBM) for a in arrays]


def room_for(*sizes):
    return pltpu.CompilerParams(vmem_limit_bytes=(6 << 20) + sum(sizes))


def nbytes(array):
    return array.size * array.dtype.itemsize


def near_nothing():
    return pl.CostEstimate(flops=1, bytes_accessed=1, transcendentals=0)


def columns_of(rows):
    count, width = rows.shape
    return jnp.concatenate([rows, jnp.zeros((8 - count, width), rows.dtype)], 0).T


def slot_kernel(nrows_blk, shift, n_col, live_count, index, first, owner_row, entries):
    slots = index.shape[1]
    nkeys = 2 * nrows_blk
    live = jnp.where(lax.axis_index("col") == n_col - 1, live_count[0], 0)

    def count_up(shape, axis):
        return lax.broadcasted_iota(jnp.int32, shape, axis)

    def keys_of(rows, cols):
        return rows + jnp.where(cols >= nrows_blk, nrows_blk, 0)

    def groups_of(hits, axis):
        return (jnp.sum(hits.astype(jnp.int32), axis, keepdims=True) + (GROUP - 1)) // GROUP

    across = index[...]
    down = columns_of(across)
    row_a, col_a = across[0:1], across[1:2]
    row_d, col_d = down[:, 0:1], down[:, 1:2]
    key_a, key_d = keys_of(row_a, col_a), keys_of(row_d, col_d)
    k_a, k_d = count_up((1, slots), 1), count_up((slots, 1), 0)
    alive_a, alive_d = k_a < live, k_d < live
    rank = jnp.sum(((key_a == key_d) & alive_a & (k_a < k_d)).astype(jnp.int32), 1, keepdims=True)
    groups_d = groups_of((key_a == count_up((nkeys, 1), 0)) & alive_a, 1)
    groups_a = groups_of((key_d == count_up((1, nkeys), 1)) & alive_d, 0)
    room = first.shape[1]
    first_a = jnp.sum(jnp.where(count_up((nkeys, room), 0) < count_up((nkeys, room), 1), groups_d, 0), 0, keepdims=True)
    first_d = jnp.sum(jnp.where(count_up((nkeys, nkeys), 1) < count_up((nkeys, nkeys), 0), groups_a, 0), 1, keepdims=True)
    first[...] = first_a
    started = (first_d <= count_up((nkeys, owner_row.shape[1]), 1)).astype(jnp.int32)
    key = jnp.sum(started, 0, keepdims=True) - 1
    owner_row[...] = jnp.where(key >= nrows_blk, key - nrows_blk, key)
    begin = jnp.sum(jnp.where(key_d == count_up((slots, room), 1), first_a, 0), 1, keepdims=True)
    place = begin * GROUP + rank
    value = ((k_d + 1) << shift) + col_d - jnp.where(col_d >= nrows_blk, nrows_blk, 0)
    hit = (place == count_up((slots, entries.shape[1]), 1)) & alive_d
    entries[...] = jnp.sum(jnp.where(hit, value, 0), 0, keepdims=True)


def slot_list(block_index, live_block_count, nrows_blk, shift, n_col):
    slots = block_index.shape[0]
    total = slots // GROUP + 2 * nrows_blk

    def lanes(n):
        return jax.ShapeDtypeStruct((1, -(-n // 128) * 128), jnp.int32)

    return pl.pallas_call(
        functools.partial(slot_kernel, nrows_blk, shift, n_col),
        out_shape=[lanes(2 * nrows_blk + 1), lanes(total), lanes(total * GROUP)],
        in_specs=[SCALAR, NEAR],
        out_specs=[NEAR] * 3,
        compiler_params=room_for(),
        cost_estimate=near_nothing(),
    )(live_block_count, block_index.T)


def products(lists, begin, end, row0, shift, block_of, source, acc, bsize):
    _, owner_row, entries = lists

    @pl.loop(0, (end - begin + UNROLL - 1) // UNROLL)
    def _(step):
        rows, prods = [], []
        for u in range(UNROLL):
            g = begin + step * UNROLL + u
            inside = g < end
            g = jnp.minimum(g, end - 1)
            rows.append(jnp.where(inside, owner_row[0, g] - row0, 0))
            left, right = [], []
            for j in range(GROUP):
                entry = jnp.where(inside, entries[0, g * GROUP + j], 0)
                block = block_of(g, j, entry)
                column = entry & ((1 << shift) - 1)
                left.append(jnp.where(entry > 0, block, jnp.zeros_like(block)))
                right.append(source[pl.ds(pl.multiple_of(column * bsize, bsize), bsize), :])
            prods.append(
                jnp.dot(jnp.concatenate(left, 1), jnp.concatenate(right, 0), preferred_element_type=jnp.float32)
            )
        for row, prod in zip(rows, prods):
            acc[pl.ds(pl.multiple_of(row * bsize, bsize), bsize), :] += prod


def stored(blocks, shift):
    return lambda g, j, entry: blocks[jnp.maximum((entry >> shift) - 1, 0)]


def shared_range(first, nrows_blk, row0, nrows):
    return first[0, nrows_blk + row0], first[0, nrows_blk + row0 + nrows]


def gather_kernel(send_rows, tmat, blocks, first_rows, second_rows, panel, near_blocks, picked, sem):
    count = picked.shape[0]
    depth = 2 * count
    steps = panel.shape[0] // depth
    copy_blocks = pltpu.make_async_copy(blocks, near_blocks, sem.at[steps])

    def part(step):
        chunk = pl.ds(pl.multiple_of(step * depth, depth), depth)
        return pltpu.make_async_copy(tmat.at[chunk], panel.at[chunk], sem.at[step])

    for step in range(steps):
        part(step).start()
    copy_blocks.start()
    picked[...] = jnp.zeros_like(picked)
    lists = columns_of(send_rows[...])
    wanted = jnp.concatenate([lists[:, 0:1], lists[:, 1:2]], 0)

    @pl.loop(0, steps)
    def _(step):
        part(step).wait()
        begin = pl.multiple_of(step * depth, depth)
        numbers = lax.broadcasted_iota(jnp.int32, (count, depth), 1) + begin
        picks = jnp.where(wanted == numbers, 1.0, 0.0).astype(panel.dtype)
        picked[...] += jnp.dot(picks, panel[pl.ds(begin, depth), :], preferred_element_type=jnp.float32)

    half = count // 2
    odd = lax.axis_index("dom") % 2
    first_rows[...] = picked[pl.ds(pl.multiple_of((1 - odd) * half, half), half), :].astype(first_rows.dtype)
    second_rows[...] = picked[pl.ds(pl.multiple_of(odd * half, half), half), :].astype(second_rows.dtype)
    copy_blocks.wait()


def gather_rows(send_rows, tmat, blocks):
    width, picked = tmat.shape[1], send_rows.size
    return pl.pallas_call(
        gather_kernel,
        out_shape=[jax.ShapeDtypeStruct((picked // 2, width), tmat.dtype)] * 2
        + [jax.ShapeDtypeStruct(a.shape, a.dtype) for a in (tmat, blocks)],
        in_specs=[NEAR] + [FAR] * 2,
        out_specs=[NEAR] * 4,
        scratch_shapes=[
            pltpu.VMEM((picked, width), jnp.float32),
            pltpu.SemaphoreType.DMA((tmat.shape[0] // (2 * picked) + 1,)),
        ],
        compiler_params=room_for(nbytes(tmat), nbytes(blocks), 6 * picked * width),
        cost_estimate=near_nothing(),
    )(send_rows, *far(tmat, blocks))


def own_kernel(row0, nrows, shift, bsize, first, owner_row, entries, blocks, panel, acc):
    acc[...] = jnp.zeros_like(acc)
    lists = (first, owner_row, entries)
    products(lists, first[0, row0], first[0, row0 + nrows], row0, shift, stored(blocks, shift), panel, acc, bsize)


def own_products(lists, blocks, panel, shift, row0, nrows):
    bsize, width = blocks.shape[1], panel.shape[1]
    return pl.pallas_call(
        functools.partial(own_kernel, row0, nrows, shift, bsize),
        out_shape=jax.ShapeDtypeStruct((nrows * bsize, width), jnp.float32),
        in_specs=[SCALAR] * 3 + [NEAR] * 2,
        out_specs=NEAR,
        compiler_params=room_for(4 * nrows * bsize * width),
        cost_estimate=near_nothing(),
    )(*lists, blocks, panel)


def place_halo(even, odd, halo):
    sides = even.shape[0]
    odd_partition = lax.axis_index("dom") % 2
    halo[pl.ds(pl.multiple_of((1 - odd_partition) * sides, sides), sides), :] = even[...]
    halo[pl.ds(pl.multiple_of(odd_partition * sides, sides), sides), :] = odd[...]


def pieces_kernel(nrows_blk, row0, nrows, shift, bsize, other0, n_col, first, owner_row, entries, blocks, odd, even, own, tmat, out, halo, acc, sem):
    panel_column = lax.axis_index("col") == n_col - 1

    @pl.when(panel_column)
    def _():
        acc[...] = own[...]
        place_halo(even, odd, halo)
        lists = (first, owner_row, entries)
        products(lists, *shared_range(first, nrows_blk, row0, nrows), row0, shift, stored(blocks, shift), halo, acc, bsize)
        out[...] = acc[...].astype(out.dtype)

    @pl.when(jnp.logical_not(panel_column))
    def _():
        copy = pltpu.make_async_copy(tmat.at[pl.ds(other0, out.shape[0])], out, sem)
        copy.start()
        copy.wait()


def piece(lists, blocks, odd, even, own, tmat, shift, row0, nrows, other0, n_col):
    bsize, width = blocks.shape[1], tmat.shape[1]
    size = nrows * bsize
    return pl.pallas_call(
        functools.partial(pieces_kernel, tmat.shape[0] // bsize, row0, nrows, shift, bsize, other0, n_col),
        out_shape=jax.ShapeDtypeStruct((size, width), tmat.dtype),
        in_specs=[SCALAR] * 3 + [NEAR] * 4 + [FAR],
        out_specs=NEAR,
        scratch_shapes=[
            pltpu.VMEM((2 * even.shape[0], width), tmat.dtype),
            pltpu.VMEM((size, width), jnp.float32),
            pltpu.SemaphoreType.DMA,
        ],
        compiler_params=room_for(2 * nbytes(even), 6 * size * width),
        cost_estimate=near_nothing(),
    )(*lists, blocks, odd, even, own, *far(tmat))


def mass_kernel(nrows_blk, row0, nrows, shift, bsize, first, owner_row, entries, blocks, panel, odd, even, after, out, halo, acc):
    lists = (first, owner_row, entries)
    acc[...] = jnp.zeros_like(acc)
    place_halo(even, odd, halo)
    block_of = stored(blocks, shift)
    products(lists, first[0, row0], first[0, row0 + nrows], row0, shift, block_of, panel, acc, bsize)
    products(lists, *shared_range(first, nrows_blk, row0, nrows), row0, shift, block_of, halo, acc, bsize)
    out[...] = acc[...].astype(out.dtype)


def add_contract(total, left, right, left0=0, right0=0, rows=None, steps=4):
    depth = (left.shape[0] if rows is None else rows) // steps

    @pl.loop(0, steps)
    def _(i):
        begin = pl.multiple_of(i * depth, depth)
        total[...] += contract(left[pl.ds(left0 + begin, depth), :], right[pl.ds(right0 + begin, depth), :])


def panel_kernel(nrows_blk, nrows, shift, bsize, first, owner_row, entries, blocks, panel, odd, even, sent, out, result, halo, acc, near_sent, sem):
    copy = pltpu.make_async_copy(sent, near_sent, sem)
    copy.start()
    mass_kernel(nrows_blk, 0, nrows, shift, bsize, first, owner_row, entries, blocks, panel, odd, even, None, out, halo, acc)
    result[...] = jnp.zeros_like(result)
    add_contract(result, out, panel)
    copy.wait()
    add_contract(result, near_sent, panel, right0=nrows * bsize)


def panel_work(lists, blocks, panel, odd, even, sent, shift, nrows):
    bsize, width = blocks.shape[1], panel.shape[1]
    return pl.pallas_call(
        functools.partial(panel_kernel, panel.shape[0] // bsize, nrows, shift, bsize),
        out_shape=[
            jax.ShapeDtypeStruct((nrows * bsize, width), panel.dtype),
            jax.ShapeDtypeStruct((width, width), jnp.float32),
        ],
        in_specs=[SCALAR] * 3 + [NEAR] * 4 + [ANYWHERE],
        out_specs=[NEAR] * 2,
        scratch_shapes=[
            pltpu.VMEM((2 * even.shape[0], width), panel.dtype),
            pltpu.VMEM((nrows * bsize, width), jnp.float32),
            pltpu.VMEM(sent.shape, sent.dtype),
            pltpu.SemaphoreType.DMA,
        ],
        compiler_params=room_for(4 * nbytes(even), 6 * nrows * bsize * width, 2 * nbytes(sent), 4 * width * width),
        cost_estimate=near_nothing(),
    )(*lists, blocks, panel, odd, even, sent)


def partner_kernel(n_col, mass, ahead, panel, known, partner):
    early, rows = ahead.shape[0], partner.shape[0]
    panel_column = lax.axis_index("col") == n_col - 1
    known[...] = jnp.zeros_like(known)

    @pl.when(panel_column)
    def _():
        add_contract(known, mass, ahead, rows=early)
        partner[...] = mass[pl.ds(early, rows), :]

    @pl.when(jnp.logical_not(panel_column))
    def _():
        partner[...] = panel[pl.ds(panel.shape[0] - rows, rows), :]


def partner_rows(mass, ahead, panel, rows, n_col):
    width = mass.shape[1]
    return pl.pallas_call(
        functools.partial(partner_kernel, n_col),
        out_shape=[jax.ShapeDtypeStruct((width, width), jnp.float32), jax.ShapeDtypeStruct((rows, width), mass.dtype)],
        in_specs=[NEAR] * 3,
        out_specs=[NEAR] * 2,
        compiler_params=room_for(2 * nbytes(ahead), 4 * width * width, 4 * rows * width),
        cost_estimate=near_nothing(),
    )(mass, ahead, panel)


def meet_kernel(n_col, got, partner, known, out):
    panel_column = lax.axis_index("col") == n_col - 1
    out[...] = known[...]

    @pl.when(panel_column)
    def _():
        add_contract(out, partner, got, steps=2)

    @pl.when(jnp.logical_not(panel_column))
    def _():
        add_contract(out, got, partner, steps=2)


def meet(got, partner, known, n_col):
    return pl.pallas_call(
        functools.partial(meet_kernel, n_col),
        out_shape=jax.ShapeDtypeStruct(known.shape, jnp.float32),
        in_specs=[NEAR] * 3,
        out_specs=NEAR,
        compiler_params=room_for(4 * nbytes(got), 2 * nbytes(known)),
        cost_estimate=near_nothing(),
    )(got, partner, known)


def mass_rows(lists, blocks, panel, odd, even, after, shift, row0, nrows):
    bsize, width = blocks.shape[1], panel.shape[1]
    return pl.pallas_call(
        functools.partial(mass_kernel, panel.shape[0] // bsize, row0, nrows, shift, bsize),
        out_shape=jax.ShapeDtypeStruct((nrows * bsize, width), panel.dtype),
        in_specs=[SCALAR] * 3 + [NEAR] * 5,
        out_specs=NEAR,
        scratch_shapes=[
            pltpu.VMEM((2 * even.shape[0], width), panel.dtype),
            pltpu.VMEM((nrows * bsize, width), jnp.float32),
        ],
        compiler_params=room_for(4 * nbytes(even), 6 * nrows * bsize * width, nbytes(after)),
        cost_estimate=near_nothing(),
    )(*lists, blocks, panel, odd, even, after)


def fold_kernel(bit, inner, counts, *refs):
    keep, send = refs[-2:]
    mine = (lax.axis_index("dom") // bit) % 2
    for t in range(keep.shape[0]):
        outer, rest = divmod(t, inner)
        for out, side in ((keep, mine), (send, 1 - mine)):
            place = (2 * outer + side) * inner + rest
            sources, col = refs[:-2], 0
            for count, begin, width in counts:
                cols = pl.ds(begin, width)
                total = sources[0][place, :, cols]
                for part in sources[1:count]:
                    total += part[place, :, cols]
                out[t, :, pl.ds(col, width)] = total
                sources, col = sources[count:], col + width


def fold(bit, inner, *columns):
    targets, rows, _ = columns[0][0][0].shape
    half = jax.ShapeDtypeStruct((targets // 2, rows, sum(width for _, _, width in columns)), jnp.float32)
    arrays = [a for some, _, _ in columns for a in some]
    return pl.pallas_call(
        functools.partial(fold_kernel, bit, inner, [(len(some), begin, width) for some, begin, width in columns]),
        out_shape=[half] * 2,
        in_specs=[NEAR] * len(arrays),
        out_specs=[NEAR] * 2,
        compiler_params=room_for(),
        cost_estimate=near_nothing(),
    )(*arrays)


def step(route, bit, inner, *columns):
    keep, send = fold(bit, inner, *columns)
    return [keep, lax.ppermute(send, *route(bit))]


def scatter(x, route):
    targets, rows, width = x.shape
    half = width // 2
    whole = step(route, 1, 1, ([x], 0, width))
    left, right = step(route, 2, 1, (whole, 0, half)), step(route, 4, 2, (whole, half, half))
    left, right = step(route, 4, 1, (left, 0, half)), step(route, 2, 1, (right, 0, half))
    bit, columns = 8, [(left, 0, half), (right, 0, half)]
    while bit < targets // 2:
        columns = [(step(route, bit, 1, *columns), 0, width)]
        bit *= 2
    return columns


def body(tmat, stored_mass_blocks, block_index, live_block_count, send_rows):
    n_col, n_dom = lax.axis_size("col"), lax.axis_size("dom")
    owner = n_col - 1
    col, dom = lax.axis_index("col"), lax.axis_index("dom")
    rows_dev, width = tmat.shape
    bsize = stored_mass_blocks.shape[1]
    nrows_blk = rows_dev // bsize
    share = width // n_dom
    shift = nrows_blk.bit_length()
    lists = slot_list(block_index, live_block_count, nrows_blk, shift, n_col)


    def exchange(block, begin):
        pairs = [(i * n_col + owner, (i + 1) * n_col + owner) for i in range(begin, n_dom - 1, 2)]
        return lax.ppermute(block, ("dom", "col"), pairs + [(b, a) for a, b in pairs])

    na = (nrows_blk * 13) // 32
    nb = nrows_blk - na
    *rows, panel, blocks = gather_rows(send_rows, tmat, stored_mass_blocks)
    even, odd = exchange(rows[0], 0), exchange(rows[1], 1)

    if n_col != 2 or n_dom < 16 or n_dom & (n_dom - 1):
        mass = mass_rows(lists, blocks, panel, odd, even, even, shift, 0, nrows_blk)
        total = lax.psum(contract(lax.psum(mass, "col"), tmat), "dom")
        return lax.dynamic_slice_in_dim(total, dom * share, share, 0)

    cut = nb * bsize
    early = cut - na * bsize
    ahead = lax.ppermute(tmat[:early], "col", [(0, 1)])

    own_a = own_products(lists, blocks, panel, shift, nb, na)
    sent = piece(lists, blocks, odd, even, own_a, tmat, shift, nb, na, early, n_col)
    sent, ahead = lax.optimization_barrier((sent, ahead))
    got = lax.ppermute(sent, "col", [(0, 1), (1, 0)])
    mass_b, own = panel_work(lists, blocks, panel, odd, even, sent, shift, nb)
    known, partner = partner_rows(mass_b, ahead, panel, na * bsize, n_col)

    def both(bit):
        return "dom", [(i, i ^ bit) for i in range(n_dom)]

    def panel_column(bit):
        return ("dom", "col"), [(i * n_col + owner, (i ^ bit) * n_col + owner) for i in range(n_dom)]

    parts, bit = [own.reshape(n_dom, share, width)], 1
    while bit < n_dom // 2:
        parts = step(panel_column, bit, 1, (parts, 0, width))
        if bit == 2:
            parts[1], known, partner = lax.optimization_barrier((parts[1], known, partner))
        bit *= 2
    got, parts[1] = lax.optimization_barrier((got, parts[1]))

    x = meet(got, partner, known, n_col)
    keep, got = step(both, bit, 1, *scatter(x.reshape(n_dom, share, width), both))
    own_keep, own_got = step(panel_column, bit, 1, (parts, 0, width))
    x = keep + got
    other = x + lax.ppermute(x, "col", [(1, 0)])
    return jnp.where(col == owner, own_keep + own_got, other).reshape(share, width)


def solution(mesh):
    return jax.shard_map(
        body,
        mesh=mesh,
        in_specs=(P("dom", "col"), P("dom", None, None), P("dom", None), P("dom"), P("dom", None)),
        out_specs=P("dom", "col"),
        check_vma=False,
    )
```

```python
import functools

import jax
import jax.numpy as jnp
from jax import lax
from jax.experimental import pallas as pl
from jax.experimental.pallas import tpu as pltpu
from jax.sharding import PartitionSpec as P

GROUP = 4
UNROLL = 8

ANYWHERE = pl.BlockSpec(memory_space=pl.ANY)
FAR = pl.BlockSpec(memory_space=pltpu.HBM)
NEAR = pl.BlockSpec(memory_space=pltpu.VMEM)
SCALAR = pl.BlockSpec(memory_space=pltpu.SMEM)


def contract(left, right):
    return lax.dot_general(
        left, right, (((0,), (0,)), ((), ())), preferred_element_type=jnp.float32
    )


def far(*arrays):
    return [pltpu.with_memory_space_constraint(a, pltpu.HBM) for a in arrays]


def room_for(*sizes):
    return pltpu.CompilerParams(vmem_limit_bytes=(6 << 20) + sum(sizes))


def nbytes(array):
    return array.size * array.dtype.itemsize


def near_nothing():
    return pl.CostEstimate(flops=1, bytes_accessed=1, transcendentals=0)


def columns_of(rows):
    count, width = rows.shape
    return jnp.concatenate([rows, jnp.zeros((8 - count, width), rows.dtype)], 0).T


def slot_kernel(nrows_blk, shift, n_col, live_count, index, first, owner_row, entries):
    slots = index.shape[1]
    nkeys = 2 * nrows_blk
    live = jnp.where(lax.axis_index("col") == n_col - 1, live_count[0], 0)

    def count_up(shape, axis):
        return lax.broadcasted_iota(jnp.int32, shape, axis)

    def keys_of(rows, cols):
        return rows + jnp.where(cols >= nrows_blk, nrows_blk, 0)

    def groups_of(hits, axis):
        return (jnp.sum(hits.astype(jnp.int32), axis, keepdims=True) + (GROUP - 1)) // GROUP

    across = index[...]
    down = columns_of(across)
    row_a, col_a = across[0:1], across[1:2]
    row_d, col_d = down[:, 0:1], down[:, 1:2]
    key_a, key_d = keys_of(row_a, col_a), keys_of(row_d, col_d)
    k_a, k_d = count_up((1, slots), 1), count_up((slots, 1), 0)
    alive_a, alive_d = k_a < live, k_d < live
    rank = jnp.sum(((key_a == key_d) & alive_a & (k_a < k_d)).astype(jnp.int32), 1, keepdims=True)
    groups_d = groups_of((key_a == count_up((nkeys, 1), 0)) & alive_a, 1)
    groups_a = groups_of((key_d == count_up((1, nkeys), 1)) & alive_d, 0)
    room = first.shape[1]
    first_a = jnp.sum(jnp.where(count_up((nkeys, room), 0) < count_up((nkeys, room), 1), groups_d, 0), 0, keepdims=True)
    first_d = jnp.sum(jnp.where(count_up((nkeys, nkeys), 1) < count_up((nkeys, nkeys), 0), groups_a, 0), 1, keepdims=True)
    first[...] = first_a
    started = (first_d <= count_up((nkeys, owner_row.shape[1]), 1)).astype(jnp.int32)
    key = jnp.sum(started, 0, keepdims=True) - 1
    owner_row[...] = jnp.where(key >= nrows_blk, key - nrows_blk, key)
    begin = jnp.sum(jnp.where(key_d == count_up((slots, room), 1), first_a, 0), 1, keepdims=True)
    place = begin * GROUP + rank
    value = ((k_d + 1) << shift) + col_d - jnp.where(col_d >= nrows_blk, nrows_blk, 0)
    hit = (place == count_up((slots, entries.shape[1]), 1)) & alive_d
    entries[...] = jnp.sum(jnp.where(hit, value, 0), 0, keepdims=True)


def slot_list(block_index, live_block_count, nrows_blk, shift, n_col):
    slots = block_index.shape[0]
    total = slots // GROUP + 2 * nrows_blk

    def lanes(n):
        return jax.ShapeDtypeStruct((1, -(-n // 128) * 128), jnp.int32)

    return pl.pallas_call(
        functools.partial(slot_kernel, nrows_blk, shift, n_col),
        out_shape=[lanes(2 * nrows_blk + 1), lanes(total), lanes(total * GROUP)],
        in_specs=[SCALAR, NEAR],
        out_specs=[NEAR] * 3,
        compiler_params=room_for(),
        cost_estimate=near_nothing(),
    )(live_block_count, block_index.T)


def products(lists, begin, end, row0, shift, block_of, source, acc, bsize):
    _, owner_row, entries = lists

    @pl.loop(0, (end - begin + UNROLL - 1) // UNROLL)
    def _(step):
        rows, prods = [], []
        for u in range(UNROLL):
            g = begin + step * UNROLL + u
            inside = g < end
            g = jnp.minimum(g, end - 1)
            rows.append(jnp.where(inside, owner_row[0, g] - row0, 0))
            left, right = [], []
            for j in range(GROUP):
                entry = jnp.where(inside, entries[0, g * GROUP + j], 0)
                block = block_of(g, j, entry)
                column = entry & ((1 << shift) - 1)
                left.append(jnp.where(entry > 0, block, jnp.zeros_like(block)))
                right.append(source[pl.ds(pl.multiple_of(column * bsize, bsize), bsize), :])
            prods.append(
                jnp.dot(jnp.concatenate(left, 1), jnp.concatenate(right, 0), preferred_element_type=jnp.float32)
            )
        for row, prod in zip(rows, prods):
            acc[pl.ds(pl.multiple_of(row * bsize, bsize), bsize), :] += prod


def stored(blocks, shift):
    return lambda g, j, entry: blocks[jnp.maximum((entry >> shift) - 1, 0)]


def shared_range(first, nrows_blk, row0, nrows):
    return first[0, nrows_blk + row0], first[0, nrows_blk + row0 + nrows]


def gather_kernel(send_rows, tmat, blocks, first_rows, second_rows, panel, near_blocks, picked, sem):
    count = picked.shape[0]
    depth = 2 * count
    steps = panel.shape[0] // depth
    copy_blocks = pltpu.make_async_copy(blocks, near_blocks, sem.at[steps])

    def part(step):
        chunk = pl.ds(pl.multiple_of(step * depth, depth), depth)
        return pltpu.make_async_copy(tmat.at[chunk], panel.at[chunk], sem.at[step])

    for step in range(steps):
        part(step).start()
    copy_blocks.start()
    picked[...] = jnp.zeros_like(picked)
    lists = columns_of(send_rows[...])
    wanted = jnp.concatenate([lists[:, 0:1], lists[:, 1:2]], 0)

    @pl.loop(0, steps)
    def _(step):
        part(step).wait()
        begin = pl.multiple_of(step * depth, depth)
        numbers = lax.broadcasted_iota(jnp.int32, (count, depth), 1) + begin
        picks = jnp.where(wanted == numbers, 1.0, 0.0).astype(panel.dtype)
        picked[...] += jnp.dot(picks, panel[pl.ds(begin, depth), :], preferred_element_type=jnp.float32)

    half = count // 2
    odd = lax.axis_index("dom") % 2
    first_rows[...] = picked[pl.ds(pl.multiple_of((1 - odd) * half, half), half), :].astype(first_rows.dtype)
    second_rows[...] = picked[pl.ds(pl.multiple_of(odd * half, half), half), :].astype(second_rows.dtype)
    copy_blocks.wait()


def gather_rows(send_rows, tmat, blocks):
    width, picked = tmat.shape[1], send_rows.size
    return pl.pallas_call(
        gather_kernel,
        out_shape=[jax.ShapeDtypeStruct((picked // 2, width), tmat.dtype)] * 2
        + [jax.ShapeDtypeStruct(a.shape, a.dtype) for a in (tmat, blocks)],
        in_specs=[NEAR] + [FAR] * 2,
        out_specs=[NEAR] * 4,
        scratch_shapes=[
            pltpu.VMEM((picked, width), jnp.float32),
            pltpu.SemaphoreType.DMA((tmat.shape[0] // (2 * picked) + 1,)),
        ],
        compiler_params=room_for(nbytes(tmat), nbytes(blocks), 6 * picked * width),
        cost_estimate=near_nothing(),
    )(send_rows, *far(tmat, blocks))


def own_kernel(row0, nrows, shift, bsize, first, owner_row, entries, blocks, panel, acc):
    acc[...] = jnp.zeros_like(acc)
    lists = (first, owner_row, entries)
    products(lists, first[0, row0], first[0, row0 + nrows], row0, shift, stored(blocks, shift), panel, acc, bsize)


def own_products(lists, blocks, panel, shift, row0, nrows):
    bsize, width = blocks.shape[1], panel.shape[1]
    return pl.pallas_call(
        functools.partial(own_kernel, row0, nrows, shift, bsize),
        out_shape=jax.ShapeDtypeStruct((nrows * bsize, width), jnp.float32),
        in_specs=[SCALAR] * 3 + [NEAR] * 2,
        out_specs=NEAR,
        compiler_params=room_for(4 * nrows * bsize * width),
        cost_estimate=near_nothing(),
    )(*lists, blocks, panel)


def place_halo(even, odd, halo):
    sides = even.shape[0]
    odd_partition = lax.axis_index("dom") % 2
    halo[pl.ds(pl.multiple_of((1 - odd_partition) * sides, sides), sides), :] = even[...]
    halo[pl.ds(pl.multiple_of(odd_partition * sides, sides), sides), :] = odd[...]


def pieces_kernel(nrows_blk, row0, nrows, shift, bsize, other0, n_col, first, owner_row, entries, blocks, odd, even, own, tmat, out, halo, acc, sem):
    panel_column = lax.axis_index("col") == n_col - 1

    @pl.when(panel_column)
    def _():
        acc[...] = own[...]
        place_halo(even, odd, halo)
        lists = (first, owner_row, entries)
        products(lists, *shared_range(first, nrows_blk, row0, nrows), row0, shift, stored(blocks, shift), halo, acc, bsize)
        out[...] = acc[...].astype(out.dtype)

    @pl.when(jnp.logical_not(panel_column))
    def _():
        copy = pltpu.make_async_copy(tmat.at[pl.ds(other0, out.shape[0])], out, sem)
        copy.start()
        copy.wait()


def piece(lists, blocks, odd, even, own, tmat, shift, row0, nrows, other0, n_col):
    bsize, width = blocks.shape[1], tmat.shape[1]
    size = nrows * bsize
    return pl.pallas_call(
        functools.partial(pieces_kernel, tmat.shape[0] // bsize, row0, nrows, shift, bsize, other0, n_col),
        out_shape=jax.ShapeDtypeStruct((size, width), tmat.dtype),
        in_specs=[SCALAR] * 3 + [NEAR] * 4 + [FAR],
        out_specs=NEAR,
        scratch_shapes=[
            pltpu.VMEM((2 * even.shape[0], width), tmat.dtype),
            pltpu.VMEM((size, width), jnp.float32),
            pltpu.SemaphoreType.DMA,
        ],
        compiler_params=room_for(2 * nbytes(even), 6 * size * width),
        cost_estimate=near_nothing(),
    )(*lists, blocks, odd, even, own, *far(tmat))


def mass_kernel(nrows_blk, row0, nrows, shift, bsize, first, owner_row, entries, blocks, panel, odd, even, after, out, halo, acc):
    lists = (first, owner_row, entries)
    acc[...] = jnp.zeros_like(acc)
    place_halo(even, odd, halo)
    block_of = stored(blocks, shift)
    products(lists, first[0, row0], first[0, row0 + nrows], row0, shift, block_of, panel, acc, bsize)
    products(lists, *shared_range(first, nrows_blk, row0, nrows), row0, shift, block_of, halo, acc, bsize)
    out[...] = acc[...].astype(out.dtype)


def add_contract(total, left, right, left0=0, right0=0, rows=None, steps=4):
    depth = (left.shape[0] if rows is None else rows) // steps

    @pl.loop(0, steps)
    def _(i):
        begin = pl.multiple_of(i * depth, depth)
        total[...] += contract(left[pl.ds(left0 + begin, depth), :], right[pl.ds(right0 + begin, depth), :])


def panel_kernel(nrows_blk, nrows, shift, bsize, first, owner_row, entries, blocks, panel, odd, even, sent, out, result, halo, acc, near_sent, sem):
    copy = pltpu.make_async_copy(sent, near_sent, sem)
    copy.start()
    mass_kernel(nrows_blk, 0, nrows, shift, bsize, first, owner_row, entries, blocks, panel, odd, even, None, out, halo, acc)
    result[...] = jnp.zeros_like(result)
    add_contract(result, out, panel)
    copy.wait()
    add_contract(result, near_sent, panel, right0=nrows * bsize)


def panel_work(lists, blocks, panel, odd, even, sent, shift, nrows):
    bsize, width = blocks.shape[1], panel.shape[1]
    return pl.pallas_call(
        functools.partial(panel_kernel, panel.shape[0] // bsize, nrows, shift, bsize),
        out_shape=[
            jax.ShapeDtypeStruct((nrows * bsize, width), panel.dtype),
            jax.ShapeDtypeStruct((width, width), jnp.float32),
        ],
        in_specs=[SCALAR] * 3 + [NEAR] * 4 + [ANYWHERE],
        out_specs=[NEAR] * 2,
        scratch_shapes=[
            pltpu.VMEM((2 * even.shape[0], width), panel.dtype),
            pltpu.VMEM((nrows * bsize, width), jnp.float32),
            pltpu.VMEM(sent.shape, sent.dtype),
            pltpu.SemaphoreType.DMA,
        ],
        compiler_params=room_for(4 * nbytes(even), 6 * nrows * bsize * width, 2 * nbytes(sent), 4 * width * width),
        cost_estimate=near_nothing(),
    )(*lists, blocks, panel, odd, even, sent)


def partner_kernel(n_col, mass, ahead, panel, known, partner):
    early, rows = ahead.shape[0], partner.shape[0]
    panel_column = lax.axis_index("col") == n_col - 1
    known[...] = jnp.zeros_like(known)

    @pl.when(panel_column)
    def _():
        add_contract(known, mass, ahead, rows=early)
        partner[...] = mass[pl.ds(early, rows), :]

    @pl.when(jnp.logical_not(panel_column))
    def _():
        partner[...] = panel[pl.ds(panel.shape[0] - rows, rows), :]


def partner_rows(mass, ahead, panel, rows, n_col):
    width = mass.shape[1]
    return pl.pallas_call(
        functools.partial(partner_kernel, n_col),
        out_shape=[jax.ShapeDtypeStruct((width, width), jnp.float32), jax.ShapeDtypeStruct((rows, width), mass.dtype)],
        in_specs=[NEAR] * 3,
        out_specs=[NEAR] * 2,
        compiler_params=room_for(2 * nbytes(ahead), 4 * width * width, 4 * rows * width),
        cost_estimate=near_nothing(),
    )(mass, ahead, panel)


def meet_kernel(n_col, got, partner, known, out):
    panel_column = lax.axis_index("col") == n_col - 1
    out[...] = known[...]

    @pl.when(panel_column)
    def _():
        add_contract(out, partner, got, steps=2)

    @pl.when(jnp.logical_not(panel_column))
    def _():
        add_contract(out, got, partner, steps=2)


def meet(got, partner, known, n_col):
    return pl.pallas_call(
        functools.partial(meet_kernel, n_col),
        out_shape=jax.ShapeDtypeStruct(known.shape, jnp.float32),
        in_specs=[NEAR] * 3,
        out_specs=NEAR,
        compiler_params=room_for(4 * nbytes(got), 2 * nbytes(known)),
        cost_estimate=near_nothing(),
    )(got, partner, known)


def mass_rows(lists, blocks, panel, odd, even, after, shift, row0, nrows):
    bsize, width = blocks.shape[1], panel.shape[1]
    return pl.pallas_call(
        functools.partial(mass_kernel, panel.shape[0] // bsize, row0, nrows, shift, bsize),
        out_shape=jax.ShapeDtypeStruct((nrows * bsize, width), panel.dtype),
        in_specs=[SCALAR] * 3 + [NEAR] * 5,
        out_specs=NEAR,
        scratch_shapes=[
            pltpu.VMEM((2 * even.shape[0], width), panel.dtype),
            pltpu.VMEM((nrows * bsize, width), jnp.float32),
        ],
        compiler_params=room_for(4 * nbytes(even), 6 * nrows * bsize * width, nbytes(after)),
        cost_estimate=near_nothing(),
    )(*lists, blocks, panel, odd, even, after)


def fold_kernel(bit, *refs):
    *parts, keep, send = refs
    mine = (lax.axis_index("dom") // bit) % 2
    for t in range(keep.shape[0]):
        for out, side in ((keep, mine), (send, 1 - mine)):
            total = parts[0][2 * t + side]
            for part in parts[1:]:
                total += part[2 * t + side].astype(jnp.float32)
            out[t] = total.astype(out.dtype)


def fold(bit, parts, kind):
    targets, rows, width = parts[0].shape
    shape = (targets // 2, rows, width)
    return pl.pallas_call(
        functools.partial(fold_kernel, bit),
        out_shape=[jax.ShapeDtypeStruct(shape, jnp.float32), jax.ShapeDtypeStruct(shape, kind)],
        in_specs=[NEAR] * len(parts),
        out_specs=[NEAR] * 2,
        compiler_params=room_for(),
        cost_estimate=near_nothing(),
    )(*parts)


def step(route, bit, parts, kind=jnp.float32):
    keep, send = fold(bit, parts, kind)
    return [keep, lax.ppermute(send, *route(bit))]


def body(tmat, stored_mass_blocks, block_index, live_block_count, send_rows):
    n_col, n_dom = lax.axis_size("col"), lax.axis_size("dom")
    owner = n_col - 1
    col, dom = lax.axis_index("col"), lax.axis_index("dom")
    rows_dev, width = tmat.shape
    bsize = stored_mass_blocks.shape[1]
    nrows_blk = rows_dev // bsize
    share = width // n_dom
    shift = nrows_blk.bit_length()
    lists = slot_list(block_index, live_block_count, nrows_blk, shift, n_col)


    def exchange(block, begin):
        pairs = [(i * n_col + owner, (i + 1) * n_col + owner) for i in range(begin, n_dom - 1, 2)]
        return lax.ppermute(block, ("dom", "col"), pairs + [(b, a) for a, b in pairs])

    na = (nrows_blk * 13) // 32
    nb = nrows_blk - na
    *rows, panel, blocks = gather_rows(send_rows, tmat, stored_mass_blocks)
    even, odd = exchange(rows[0], 0), exchange(rows[1], 1)

    if n_col != 2 or n_dom < 16 or n_dom & (n_dom - 1):
        mass = mass_rows(lists, blocks, panel, odd, even, even, shift, 0, nrows_blk)
        total = lax.psum(contract(lax.psum(mass, "col"), tmat), "dom")
        return lax.dynamic_slice_in_dim(total, dom * share, share, 0)

    cut = nb * bsize
    early = cut - na * bsize
    ahead = lax.ppermute(tmat[:early], "col", [(0, 1)])

    own_a = own_products(lists, blocks, panel, shift, nb, na)
    sent = piece(lists, blocks, odd, even, own_a, tmat, shift, nb, na, early, n_col)
    sent, ahead = lax.optimization_barrier((sent, ahead))
    got = lax.ppermute(sent, "col", [(0, 1), (1, 0)])
    mass_b, own = panel_work(lists, blocks, panel, odd, even, sent, shift, nb)
    known, partner = partner_rows(mass_b, ahead, panel, na * bsize, n_col)

    def both(bit):
        return "dom", [(i, i ^ bit) for i in range(n_dom)]

    def panel_column(bit):
        return ("dom", "col"), [(i * n_col + owner, (i ^ bit) * n_col + owner) for i in range(n_dom)]

    parts, bit = [own.reshape(n_dom, share, width)], 1
    while bit < n_dom // 2:
        parts = step(panel_column, bit, parts)
        if bit == 2:
            parts[1], known, partner = lax.optimization_barrier((parts[1], known, partner))
        bit *= 2
    got, parts[1] = lax.optimization_barrier((got, parts[1]))

    x = meet(got, partner, known, n_col)
    sums = [x.reshape(n_dom, share, width)]
    for b in range(bit.bit_length()):
        sums = step(both, 1 << b, sums, jnp.bfloat16 if b == 1 else jnp.float32)
    own_keep, own_got = step(panel_column, bit, parts)
    x = sums[0] + sums[1]
    other = x + lax.ppermute(x, "col", [(1, 0)])
    return jnp.where(col == owner, own_keep + own_got, other).reshape(share, width)


def solution(mesh):
    return jax.shard_map(
        body,
        mesh=mesh,
        in_specs=(P("dom", "col"), P("dom", None, None), P("dom", None), P("dom"), P("dom", None)),
        out_specs=P("dom", "col"),
        check_vma=False,
    )
```

```python
import functools

import jax
import jax.numpy as jnp
from jax import lax
from jax.experimental import pallas as pl
from jax.experimental.pallas import tpu as pltpu
from jax.sharding import PartitionSpec as P

GROUP = 4
UNROLL = 8

ANYWHERE = pl.BlockSpec(memory_space=pl.ANY)
FAR = pl.BlockSpec(memory_space=pltpu.HBM)
NEAR = pl.BlockSpec(memory_space=pltpu.VMEM)
SCALAR = pl.BlockSpec(memory_space=pltpu.SMEM)


def contract(left, right):
    return lax.dot_general(
        left, right, (((0,), (0,)), ((), ())), preferred_element_type=jnp.float32
    )


def far(*arrays):
    return [pltpu.with_memory_space_constraint(a, pltpu.HBM) for a in arrays]


def room_for(*sizes):
    return pltpu.CompilerParams(vmem_limit_bytes=(6 << 20) + sum(sizes))


def nbytes(array):
    return array.size * array.dtype.itemsize


def near_nothing():
    return pl.CostEstimate(flops=1, bytes_accessed=1, transcendentals=0)


def columns_of(rows):
    count, width = rows.shape
    return jnp.concatenate([rows, jnp.zeros((8 - count, width), rows.dtype)], 0).T


def slot_kernel(nrows_blk, shift, n_col, live_count, index, first, owner_row, entries):
    slots = index.shape[1]
    nkeys = 2 * nrows_blk
    live = jnp.where(lax.axis_index("col") == n_col - 1, live_count[0], 0)

    def count_up(shape, axis):
        return lax.broadcasted_iota(jnp.int32, shape, axis)

    def keys_of(rows, cols):
        return rows + jnp.where(cols >= nrows_blk, nrows_blk, 0)

    def groups_of(hits, axis):
        return (jnp.sum(hits.astype(jnp.int32), axis, keepdims=True) + (GROUP - 1)) // GROUP

    across = index[...]
    down = columns_of(across)
    row_a, col_a = across[0:1], across[1:2]
    row_d, col_d = down[:, 0:1], down[:, 1:2]
    key_a, key_d = keys_of(row_a, col_a), keys_of(row_d, col_d)
    k_a, k_d = count_up((1, slots), 1), count_up((slots, 1), 0)
    alive_a, alive_d = k_a < live, k_d < live
    rank = jnp.sum(((key_a == key_d) & alive_a & (k_a < k_d)).astype(jnp.int32), 1, keepdims=True)
    groups_d = groups_of((key_a == count_up((nkeys, 1), 0)) & alive_a, 1)
    groups_a = groups_of((key_d == count_up((1, nkeys), 1)) & alive_d, 0)
    room = first.shape[1]
    first_a = jnp.sum(jnp.where(count_up((nkeys, room), 0) < count_up((nkeys, room), 1), groups_d, 0), 0, keepdims=True)
    first_d = jnp.sum(jnp.where(count_up((nkeys, nkeys), 1) < count_up((nkeys, nkeys), 0), groups_a, 0), 1, keepdims=True)
    first[...] = first_a
    started = (first_d <= count_up((nkeys, owner_row.shape[1]), 1)).astype(jnp.int32)
    key = jnp.sum(started, 0, keepdims=True) - 1
    owner_row[...] = jnp.where(key >= nrows_blk, key - nrows_blk, key)
    begin = jnp.sum(jnp.where(key_d == count_up((slots, room), 1), first_a, 0), 1, keepdims=True)
    place = begin * GROUP + rank
    value = ((k_d + 1) << shift) + col_d - jnp.where(col_d >= nrows_blk, nrows_blk, 0)
    hit = (place == count_up((slots, entries.shape[1]), 1)) & alive_d
    entries[...] = jnp.sum(jnp.where(hit, value, 0), 0, keepdims=True)


def slot_list(block_index, live_block_count, nrows_blk, shift, n_col):
    slots = block_index.shape[0]
    total = slots // GROUP + 2 * nrows_blk

    def lanes(n):
        return jax.ShapeDtypeStruct((1, -(-n // 128) * 128), jnp.int32)

    return pl.pallas_call(
        functools.partial(slot_kernel, nrows_blk, shift, n_col),
        out_shape=[lanes(2 * nrows_blk + 1), lanes(total), lanes(total * GROUP)],
        in_specs=[SCALAR, NEAR],
        out_specs=[NEAR] * 3,
        compiler_params=room_for(),
        cost_estimate=near_nothing(),
    )(live_block_count, block_index.T)


def products(lists, begin, end, row0, shift, block_of, source, acc, bsize):
    _, owner_row, entries = lists

    @pl.loop(0, (end - begin + UNROLL - 1) // UNROLL)
    def _(step):
        rows, prods = [], []
        for u in range(UNROLL):
            g = begin + step * UNROLL + u
            inside = g < end
            g = jnp.minimum(g, end - 1)
            rows.append(jnp.where(inside, owner_row[0, g] - row0, 0))
            left, right = [], []
            for j in range(GROUP):
                entry = jnp.where(inside, entries[0, g * GROUP + j], 0)
                block = block_of(g, j, entry)
                column = entry & ((1 << shift) - 1)
                left.append(jnp.where(entry > 0, block, jnp.zeros_like(block)))
                right.append(source[pl.ds(pl.multiple_of(column * bsize, bsize), bsize), :])
            prods.append(
                jnp.dot(jnp.concatenate(left, 1), jnp.concatenate(right, 0), preferred_element_type=jnp.float32)
            )
        for row, prod in zip(rows, prods):
            acc[pl.ds(pl.multiple_of(row * bsize, bsize), bsize), :] += prod


def stored(blocks, shift):
    return lambda g, j, entry: blocks[jnp.maximum((entry >> shift) - 1, 0)]


def shared_range(first, nrows_blk, row0, nrows):
    return first[0, nrows_blk + row0], first[0, nrows_blk + row0 + nrows]


def gather_kernel(send_rows, tmat, blocks, first_rows, second_rows, panel, near_blocks, picked, sem):
    count = picked.shape[0]
    depth = 2 * count
    steps = panel.shape[0] // depth
    copy_blocks = pltpu.make_async_copy(blocks, near_blocks, sem.at[steps])

    def part(step):
        chunk = pl.ds(pl.multiple_of(step * depth, depth), depth)
        return pltpu.make_async_copy(tmat.at[chunk], panel.at[chunk], sem.at[step])

    for step in range(steps):
        part(step).start()
    copy_blocks.start()
    picked[...] = jnp.zeros_like(picked)
    lists = columns_of(send_rows[...])
    wanted = jnp.concatenate([lists[:, 0:1], lists[:, 1:2]], 0)

    @pl.loop(0, steps)
    def _(step):
        part(step).wait()
        begin = pl.multiple_of(step * depth, depth)
        numbers = lax.broadcasted_iota(jnp.int32, (count, depth), 1) + begin
        picks = jnp.where(wanted == numbers, 1.0, 0.0).astype(panel.dtype)
        picked[...] += jnp.dot(picks, panel[pl.ds(begin, depth), :], preferred_element_type=jnp.float32)

    half = count // 2
    odd = lax.axis_index("dom") % 2
    first_rows[...] = picked[pl.ds(pl.multiple_of((1 - odd) * half, half), half), :].astype(first_rows.dtype)
    second_rows[...] = picked[pl.ds(pl.multiple_of(odd * half, half), half), :].astype(second_rows.dtype)
    copy_blocks.wait()


def gather_rows(send_rows, tmat, blocks):
    width, picked = tmat.shape[1], send_rows.size
    return pl.pallas_call(
        gather_kernel,
        out_shape=[jax.ShapeDtypeStruct((picked // 2, width), tmat.dtype)] * 2
        + [jax.ShapeDtypeStruct(a.shape, a.dtype) for a in (tmat, blocks)],
        in_specs=[NEAR] + [FAR] * 2,
        out_specs=[NEAR] * 4,
        scratch_shapes=[
            pltpu.VMEM((picked, width), jnp.float32),
            pltpu.SemaphoreType.DMA((tmat.shape[0] // (2 * picked) + 1,)),
        ],
        compiler_params=room_for(nbytes(tmat), nbytes(blocks), 6 * picked * width),
        cost_estimate=near_nothing(),
    )(send_rows, *far(tmat, blocks))


def own_kernel(row0, nrows, shift, bsize, first, owner_row, entries, blocks, panel, acc):
    acc[...] = jnp.zeros_like(acc)
    lists = (first, owner_row, entries)
    products(lists, first[0, row0], first[0, row0 + nrows], row0, shift, stored(blocks, shift), panel, acc, bsize)


def own_products(lists, blocks, panel, shift, row0, nrows):
    bsize, width = blocks.shape[1], panel.shape[1]
    return pl.pallas_call(
        functools.partial(own_kernel, row0, nrows, shift, bsize),
        out_shape=jax.ShapeDtypeStruct((nrows * bsize, width), jnp.float32),
        in_specs=[SCALAR] * 3 + [NEAR] * 2,
        out_specs=NEAR,
        compiler_params=room_for(4 * nrows * bsize * width),
        cost_estimate=near_nothing(),
    )(*lists, blocks, panel)


def place_halo(even, odd, halo):
    sides = even.shape[0]
    odd_partition = lax.axis_index("dom") % 2
    halo[pl.ds(pl.multiple_of((1 - odd_partition) * sides, sides), sides), :] = even[...]
    halo[pl.ds(pl.multiple_of(odd_partition * sides, sides), sides), :] = odd[...]


def pieces_kernel(nrows_blk, row0, nrows, shift, bsize, other0, n_col, first, owner_row, entries, blocks, odd, even, own, tmat, out, halo, acc, sem):
    panel_column = lax.axis_index("col") == n_col - 1

    @pl.when(panel_column)
    def _():
        acc[...] = own[...]
        place_halo(even, odd, halo)
        lists = (first, owner_row, entries)
        products(lists, *shared_range(first, nrows_blk, row0, nrows), row0, shift, stored(blocks, shift), halo, acc, bsize)
        out[...] = acc[...].astype(out.dtype)

    @pl.when(jnp.logical_not(panel_column))
    def _():
        copy = pltpu.make_async_copy(tmat.at[pl.ds(other0, out.shape[0])], out, sem)
        copy.start()
        copy.wait()


def piece(lists, blocks, odd, even, own, tmat, shift, row0, nrows, other0, n_col):
    bsize, width = blocks.shape[1], tmat.shape[1]
    size = nrows * bsize
    return pl.pallas_call(
        functools.partial(pieces_kernel, tmat.shape[0] // bsize, row0, nrows, shift, bsize, other0, n_col),
        out_shape=jax.ShapeDtypeStruct((size, width), tmat.dtype),
        in_specs=[SCALAR] * 3 + [NEAR] * 4 + [FAR],
        out_specs=NEAR,
        scratch_shapes=[
            pltpu.VMEM((2 * even.shape[0], width), tmat.dtype),
            pltpu.VMEM((size, width), jnp.float32),
            pltpu.SemaphoreType.DMA,
        ],
        compiler_params=room_for(2 * nbytes(even), 6 * size * width),
        cost_estimate=near_nothing(),
    )(*lists, blocks, odd, even, own, *far(tmat))


def mass_kernel(nrows_blk, row0, nrows, shift, bsize, first, owner_row, entries, blocks, panel, odd, even, after, out, halo, acc):
    lists = (first, owner_row, entries)
    acc[...] = jnp.zeros_like(acc)
    place_halo(even, odd, halo)
    block_of = stored(blocks, shift)
    products(lists, first[0, row0], first[0, row0 + nrows], row0, shift, block_of, panel, acc, bsize)
    products(lists, *shared_range(first, nrows_blk, row0, nrows), row0, shift, block_of, halo, acc, bsize)
    out[...] = acc[...].astype(out.dtype)


def add_contract(total, left, right, left0=0, right0=0, rows=None, steps=4):
    depth = (left.shape[0] if rows is None else rows) // steps

    @pl.loop(0, steps)
    def _(i):
        begin = pl.multiple_of(i * depth, depth)
        total[...] += contract(left[pl.ds(left0 + begin, depth), :], right[pl.ds(right0 + begin, depth), :])


def panel_kernel(nrows_blk, nrows, shift, bsize, first, owner_row, entries, blocks, panel, odd, even, sent, out, result, halo, acc, near_sent, sem):
    copy = pltpu.make_async_copy(sent, near_sent, sem)
    copy.start()
    mass_kernel(nrows_blk, 0, nrows, shift, bsize, first, owner_row, entries, blocks, panel, odd, even, None, out, halo, acc)
    result[...] = jnp.zeros_like(result)
    add_contract(result, out, panel)
    copy.wait()
    add_contract(result, near_sent, panel, right0=nrows * bsize)


def panel_work(lists, blocks, panel, odd, even, sent, shift, nrows):
    bsize, width = blocks.shape[1], panel.shape[1]
    return pl.pallas_call(
        functools.partial(panel_kernel, panel.shape[0] // bsize, nrows, shift, bsize),
        out_shape=[
            jax.ShapeDtypeStruct((nrows * bsize, width), panel.dtype),
            jax.ShapeDtypeStruct((width, width), jnp.float32),
        ],
        in_specs=[SCALAR] * 3 + [NEAR] * 4 + [ANYWHERE],
        out_specs=[NEAR] * 2,
        scratch_shapes=[
            pltpu.VMEM((2 * even.shape[0], width), panel.dtype),
            pltpu.VMEM((nrows * bsize, width), jnp.float32),
            pltpu.VMEM(sent.shape, sent.dtype),
            pltpu.SemaphoreType.DMA,
        ],
        compiler_params=room_for(4 * nbytes(even), 6 * nrows * bsize * width, 2 * nbytes(sent), 4 * width * width),
        cost_estimate=near_nothing(),
    )(*lists, blocks, panel, odd, even, sent)


def partner_kernel(n_col, mass, ahead, panel, known, partner):
    early, rows = ahead.shape[0], partner.shape[0]
    panel_column = lax.axis_index("col") == n_col - 1
    known[...] = jnp.zeros_like(known)

    @pl.when(panel_column)
    def _():
        add_contract(known, mass, ahead, rows=early)
        partner[...] = mass[pl.ds(early, rows), :]

    @pl.when(jnp.logical_not(panel_column))
    def _():
        partner[...] = panel[pl.ds(panel.shape[0] - rows, rows), :]


def partner_rows(mass, ahead, panel, rows, n_col):
    width = mass.shape[1]
    return pl.pallas_call(
        functools.partial(partner_kernel, n_col),
        out_shape=[jax.ShapeDtypeStruct((width, width), jnp.float32), jax.ShapeDtypeStruct((rows, width), mass.dtype)],
        in_specs=[NEAR] * 3,
        out_specs=[NEAR] * 2,
        compiler_params=room_for(2 * nbytes(ahead), 4 * width * width, 4 * rows * width),
        cost_estimate=near_nothing(),
    )(mass, ahead, panel)


def meet_kernel(n_col, got, partner, known, out):
    panel_column = lax.axis_index("col") == n_col - 1
    out[...] = known[...]

    @pl.when(panel_column)
    def _():
        add_contract(out, partner, got, steps=2)

    @pl.when(jnp.logical_not(panel_column))
    def _():
        add_contract(out, got, partner, steps=2)


def meet(got, partner, known, n_col):
    return pl.pallas_call(
        functools.partial(meet_kernel, n_col),
        out_shape=jax.ShapeDtypeStruct(known.shape, jnp.float32),
        in_specs=[NEAR] * 3,
        out_specs=NEAR,
        compiler_params=room_for(4 * nbytes(got), 2 * nbytes(known)),
        cost_estimate=near_nothing(),
    )(got, partner, known)


def mass_rows(lists, blocks, panel, odd, even, after, shift, row0, nrows):
    bsize, width = blocks.shape[1], panel.shape[1]
    return pl.pallas_call(
        functools.partial(mass_kernel, panel.shape[0] // bsize, row0, nrows, shift, bsize),
        out_shape=jax.ShapeDtypeStruct((nrows * bsize, width), panel.dtype),
        in_specs=[SCALAR] * 3 + [NEAR] * 5,
        out_specs=NEAR,
        scratch_shapes=[
            pltpu.VMEM((2 * even.shape[0], width), panel.dtype),
            pltpu.VMEM((nrows * bsize, width), jnp.float32),
        ],
        compiler_params=room_for(4 * nbytes(even), 6 * nrows * bsize * width, nbytes(after)),
        cost_estimate=near_nothing(),
    )(*lists, blocks, panel, odd, even, after)


def fold_kernel(bit, *refs):
    *parts, keep, send = refs
    mine = (lax.axis_index("dom") // bit) % 2
    for t in range(keep.shape[0]):
        for out, side in ((keep, mine), (send, 1 - mine)):
            total = parts[0][2 * t + side]
            for part in parts[1:]:
                total += part[2 * t + side].astype(jnp.float32)
            out[t] = total.astype(out.dtype)


def fold(bit, parts, kind):
    targets, rows, width = parts[0].shape
    shape = (targets // 2, rows, width)
    return pl.pallas_call(
        functools.partial(fold_kernel, bit),
        out_shape=[jax.ShapeDtypeStruct(shape, jnp.float32), jax.ShapeDtypeStruct(shape, kind)],
        in_specs=[NEAR] * len(parts),
        out_specs=[NEAR] * 2,
        compiler_params=room_for(),
        cost_estimate=near_nothing(),
    )(*parts)


def step(route, bit, parts, kind=jnp.float32):
    keep, send = fold(bit, parts, kind)
    return [keep, lax.ppermute(send, *route(bit))]


def body(tmat, stored_mass_blocks, block_index, live_block_count, send_rows):
    n_col, n_dom = lax.axis_size("col"), lax.axis_size("dom")
    owner = n_col - 1
    col, dom = lax.axis_index("col"), lax.axis_index("dom")
    rows_dev, width = tmat.shape
    bsize = stored_mass_blocks.shape[1]
    nrows_blk = rows_dev // bsize
    share = width // n_dom
    shift = nrows_blk.bit_length()
    lists = slot_list(block_index, live_block_count, nrows_blk, shift, n_col)


    def exchange(block, begin):
        pairs = [(i * n_col + owner, (i + 1) * n_col + owner) for i in range(begin, n_dom - 1, 2)]
        return lax.ppermute(block, ("dom", "col"), pairs + [(b, a) for a, b in pairs])

    na = (nrows_blk * 13) // 32
    nb = nrows_blk - na
    *rows, panel, blocks = gather_rows(send_rows, tmat, stored_mass_blocks)
    even, odd = exchange(rows[0], 0), exchange(rows[1], 1)

    if n_col != 2 or n_dom < 16 or n_dom & (n_dom - 1):
        mass = mass_rows(lists, blocks, panel, odd, even, even, shift, 0, nrows_blk)
        total = lax.psum(contract(lax.psum(mass, "col"), tmat), "dom")
        return lax.dynamic_slice_in_dim(total, dom * share, share, 0)

    cut = nb * bsize
    early = cut - na * bsize
    ahead = lax.ppermute(tmat[:early], "col", [(0, 1), (1, 0)])

    own_a = own_products(lists, blocks, panel, shift, nb, na)
    sent = piece(lists, blocks, odd, even, own_a, tmat, shift, nb, na, early, n_col)
    sent, ahead = lax.optimization_barrier((sent, ahead))
    got = lax.ppermute(sent, "col", [(0, 1), (1, 0)])
    mass_b, own = panel_work(lists, blocks, panel, odd, even, sent, shift, nb)
    known, partner = partner_rows(mass_b, ahead, panel, na * bsize, n_col)

    def both(bit):
        return "dom", [(i, i ^ bit) for i in range(n_dom)]

    def panel_column(bit):
        return ("dom", "col"), [(i * n_col + owner, (i ^ bit) * n_col + owner) for i in range(n_dom)]

    parts, bit = [own.reshape(n_dom, share, width)], 1
    while bit < n_dom // 2:
        parts = step(panel_column, bit, parts)
        if bit == 2:
            parts[1], known, partner = lax.optimization_barrier((parts[1], known, partner))
        bit *= 2
    got, parts[1] = lax.optimization_barrier((got, parts[1]))

    x = meet(got, partner, known, n_col)
    sums = [x.reshape(n_dom, share, width)]
    for b in range(bit.bit_length()):
        sums = step(both, 1 << b, sums, jnp.bfloat16 if b == 1 else jnp.float32)
    own_keep, own_got = step(panel_column, bit, parts)
    x = sums[0] + sums[1]
    other = x + lax.ppermute(x, "col", [(0, 1), (1, 0)])
    return jnp.where(col == owner, own_keep + own_got, other).reshape(share, width)


def solution(mesh):
    return jax.shard_map(
        body,
        mesh=mesh,
        in_specs=(P("dom", "col"), P("dom", None, None), P("dom", None), P("dom"), P("dom", None)),
        out_specs=P("dom", "col"),
        check_vma=False,
    )
```

```python
import functools

import jax
import jax.numpy as jnp
from jax import lax
from jax.experimental import pallas as pl
from jax.experimental.pallas import tpu as pltpu
from jax.sharding import PartitionSpec as P

GROUP = 4
UNROLL = 8

ANYWHERE = pl.BlockSpec(memory_space=pl.ANY)
FAR = pl.BlockSpec(memory_space=pltpu.HBM)
NEAR = pl.BlockSpec(memory_space=pltpu.VMEM)
SCALAR = pl.BlockSpec(memory_space=pltpu.SMEM)


def contract(left, right):
    return lax.dot_general(
        left, right, (((0,), (0,)), ((), ())), preferred_element_type=jnp.float32
    )


def far(*arrays):
    return [pltpu.with_memory_space_constraint(a, pltpu.HBM) for a in arrays]


def room_for(*sizes):
    return pltpu.CompilerParams(vmem_limit_bytes=(6 << 20) + sum(sizes))


def nbytes(array):
    return array.size * array.dtype.itemsize


def near_nothing():
    return pl.CostEstimate(flops=1, bytes_accessed=1, transcendentals=0)


def columns_of(rows):
    count, width = rows.shape
    return jnp.concatenate([rows, jnp.zeros((8 - count, width), rows.dtype)], 0).T


def slot_kernel(nrows_blk, shift, n_col, live_count, index, first, owner_row, entries):
    slots = index.shape[1]
    nkeys = 2 * nrows_blk
    live = jnp.where(lax.axis_index("col") == n_col - 1, live_count[0], 0)

    def count_up(shape, axis):
        return lax.broadcasted_iota(jnp.int32, shape, axis)

    def keys_of(rows, cols):
        return rows + jnp.where(cols >= nrows_blk, nrows_blk, 0)

    def groups_of(hits, axis):
        return (jnp.sum(hits.astype(jnp.int32), axis, keepdims=True) + (GROUP - 1)) // GROUP

    across = index[...]
    down = columns_of(across)
    row_a, col_a = across[0:1], across[1:2]
    row_d, col_d = down[:, 0:1], down[:, 1:2]
    key_a, key_d = keys_of(row_a, col_a), keys_of(row_d, col_d)
    k_a, k_d = count_up((1, slots), 1), count_up((slots, 1), 0)
    alive_a, alive_d = k_a < live, k_d < live
    rank = jnp.sum(((key_a == key_d) & alive_a & (k_a < k_d)).astype(jnp.int32), 1, keepdims=True)
    groups_d = groups_of((key_a == count_up((nkeys, 1), 0)) & alive_a, 1)
    groups_a = groups_of((key_d == count_up((1, nkeys), 1)) & alive_d, 0)
    room = first.shape[1]
    first_a = jnp.sum(jnp.where(count_up((nkeys, room), 0) < count_up((nkeys, room), 1), groups_d, 0), 0, keepdims=True)
    first_d = jnp.sum(jnp.where(count_up((nkeys, nkeys), 1) < count_up((nkeys, nkeys), 0), groups_a, 0), 1, keepdims=True)
    first[...] = first_a
    started = (first_d <= count_up((nkeys, owner_row.shape[1]), 1)).astype(jnp.int32)
    key = jnp.sum(started, 0, keepdims=True) - 1
    owner_row[...] = jnp.where(key >= nrows_blk, key - nrows_blk, key)
    begin = jnp.sum(jnp.where(key_d == count_up((slots, room), 1), first_a, 0), 1, keepdims=True)
    place = begin * GROUP + rank
    value = ((k_d + 1) << shift) + col_d - jnp.where(col_d >= nrows_blk, nrows_blk, 0)
    hit = (place == count_up((slots, entries.shape[1]), 1)) & alive_d
    entries[...] = jnp.sum(jnp.where(hit, value, 0), 0, keepdims=True)


def slot_list(block_index, live_block_count, nrows_blk, shift, n_col):
    slots = block_index.shape[0]
    total = slots // GROUP + 2 * nrows_blk

    def lanes(n):
        return jax.ShapeDtypeStruct((1, -(-n // 128) * 128), jnp.int32)

    return pl.pallas_call(
        functools.partial(slot_kernel, nrows_blk, shift, n_col),
        out_shape=[lanes(2 * nrows_blk + 1), lanes(total), lanes(total * GROUP)],
        in_specs=[SCALAR, NEAR],
        out_specs=[NEAR] * 3,
        compiler_params=room_for(),
        cost_estimate=near_nothing(),
    )(live_block_count, block_index.T)


def products(lists, begin, end, row0, shift, block_of, source, acc, bsize):
    _, owner_row, entries = lists

    @pl.loop(0, (end - begin + UNROLL - 1) // UNROLL)
    def _(step):
        rows, prods = [], []
        for u in range(UNROLL):
            g = begin + step * UNROLL + u
            inside = g < end
            g = jnp.minimum(g, end - 1)
            rows.append(jnp.where(inside, owner_row[0, g] - row0, 0))
            left, right = [], []
            for j in range(GROUP):
                entry = jnp.where(inside, entries[0, g * GROUP + j], 0)
                block = block_of(g, j, entry)
                column = entry & ((1 << shift) - 1)
                left.append(jnp.where(entry > 0, block, jnp.zeros_like(block)))
                right.append(source[pl.ds(pl.multiple_of(column * bsize, bsize), bsize), :])
            prods.append(
                jnp.dot(jnp.concatenate(left, 1), jnp.concatenate(right, 0), preferred_element_type=jnp.float32)
            )
        for row, prod in zip(rows, prods):
            acc[pl.ds(pl.multiple_of(row * bsize, bsize), bsize), :] += prod


def stored(blocks, shift):
    return lambda g, j, entry: blocks[jnp.maximum((entry >> shift) - 1, 0)]


def shared_range(first, nrows_blk, row0, nrows):
    return first[0, nrows_blk + row0], first[0, nrows_blk + row0 + nrows]


def gather_kernel(send_rows, tmat, blocks, first_rows, second_rows, panel, near_blocks, picked, sem):
    count = picked.shape[0]
    depth = 2 * count
    steps = panel.shape[0] // depth
    copy_blocks = pltpu.make_async_copy(blocks, near_blocks, sem.at[steps])

    def part(step):
        chunk = pl.ds(pl.multiple_of(step * depth, depth), depth)
        return pltpu.make_async_copy(tmat.at[chunk], panel.at[chunk], sem.at[step])

    for step in range(steps):
        part(step).start()
    copy_blocks.start()
    picked[...] = jnp.zeros_like(picked)
    lists = columns_of(send_rows[...])
    wanted = jnp.concatenate([lists[:, 0:1], lists[:, 1:2]], 0)

    @pl.loop(0, steps)
    def _(step):
        part(step).wait()
        begin = pl.multiple_of(step * depth, depth)
        numbers = lax.broadcasted_iota(jnp.int32, (count, depth), 1) + begin
        picks = jnp.where(wanted == numbers, 1.0, 0.0).astype(panel.dtype)
        picked[...] += jnp.dot(picks, panel[pl.ds(begin, depth), :], preferred_element_type=jnp.float32)

    half = count // 2
    odd = lax.axis_index("dom") % 2
    first_rows[...] = picked[pl.ds(pl.multiple_of((1 - odd) * half, half), half), :].astype(first_rows.dtype)
    second_rows[...] = picked[pl.ds(pl.multiple_of(odd * half, half), half), :].astype(second_rows.dtype)
    copy_blocks.wait()


def gather_rows(send_rows, tmat, blocks):
    width, picked = tmat.shape[1], send_rows.size
    return pl.pallas_call(
        gather_kernel,
        out_shape=[jax.ShapeDtypeStruct((picked // 2, width), tmat.dtype)] * 2
        + [jax.ShapeDtypeStruct(a.shape, a.dtype) for a in (tmat, blocks)],
        in_specs=[NEAR] + [FAR] * 2,
        out_specs=[NEAR] * 4,
        scratch_shapes=[
            pltpu.VMEM((picked, width), jnp.float32),
            pltpu.SemaphoreType.DMA((tmat.shape[0] // (2 * picked) + 1,)),
        ],
        compiler_params=room_for(nbytes(tmat), nbytes(blocks), 6 * picked * width),
        cost_estimate=near_nothing(),
    )(send_rows, *far(tmat, blocks))


def own_kernel(row0, nrows, shift, bsize, first, owner_row, entries, blocks, panel, acc):
    acc[...] = jnp.zeros_like(acc)
    lists = (first, owner_row, entries)
    products(lists, first[0, row0], first[0, row0 + nrows], row0, shift, stored(blocks, shift), panel, acc, bsize)


def own_products(lists, blocks, panel, shift, row0, nrows):
    bsize, width = blocks.shape[1], panel.shape[1]
    return pl.pallas_call(
        functools.partial(own_kernel, row0, nrows, shift, bsize),
        out_shape=jax.ShapeDtypeStruct((nrows * bsize, width), jnp.float32),
        in_specs=[SCALAR] * 3 + [NEAR] * 2,
        out_specs=NEAR,
        compiler_params=room_for(4 * nrows * bsize * width),
        cost_estimate=near_nothing(),
    )(*lists, blocks, panel)


def place_halo(even, odd, halo):
    sides = even.shape[0]
    odd_partition = lax.axis_index("dom") % 2
    halo[pl.ds(pl.multiple_of((1 - odd_partition) * sides, sides), sides), :] = even[...]
    halo[pl.ds(pl.multiple_of(odd_partition * sides, sides), sides), :] = odd[...]


def pieces_kernel(nrows_blk, row0, nrows, shift, bsize, other0, n_col, first, owner_row, entries, blocks, odd, even, own, tmat, out, halo, acc, sem):
    panel_column = lax.axis_index("col") == n_col - 1

    @pl.when(panel_column)
    def _():
        acc[...] = own[...]
        place_halo(even, odd, halo)
        lists = (first, owner_row, entries)
        products(lists, *shared_range(first, nrows_blk, row0, nrows), row0, shift, stored(blocks, shift), halo, acc, bsize)
        out[...] = acc[...].astype(out.dtype)

    @pl.when(jnp.logical_not(panel_column))
    def _():
        copy = pltpu.make_async_copy(tmat.at[pl.ds(other0, out.shape[0])], out, sem)
        copy.start()
        copy.wait()


def piece(lists, blocks, odd, even, own, tmat, shift, row0, nrows, other0, n_col):
    bsize, width = blocks.shape[1], tmat.shape[1]
    size = nrows * bsize
    return pl.pallas_call(
        functools.partial(pieces_kernel, tmat.shape[0] // bsize, row0, nrows, shift, bsize, other0, n_col),
        out_shape=jax.ShapeDtypeStruct((size, width), tmat.dtype),
        in_specs=[SCALAR] * 3 + [NEAR] * 4 + [FAR],
        out_specs=NEAR,
        scratch_shapes=[
            pltpu.VMEM((2 * even.shape[0], width), tmat.dtype),
            pltpu.VMEM((size, width), jnp.float32),
            pltpu.SemaphoreType.DMA,
        ],
        compiler_params=room_for(2 * nbytes(even), 6 * size * width),
        cost_estimate=near_nothing(),
    )(*lists, blocks, odd, even, own, *far(tmat))


def mass_kernel(nrows_blk, row0, nrows, shift, bsize, first, owner_row, entries, blocks, panel, odd, even, after, out, halo, acc):
    lists = (first, owner_row, entries)
    acc[...] = jnp.zeros_like(acc)
    place_halo(even, odd, halo)
    block_of = stored(blocks, shift)
    products(lists, first[0, row0], first[0, row0 + nrows], row0, shift, block_of, panel, acc, bsize)
    products(lists, *shared_range(first, nrows_blk, row0, nrows), row0, shift, block_of, halo, acc, bsize)
    out[...] = acc[...].astype(out.dtype)


def add_contract(total, left, right, left0=0, right0=0, rows=None, steps=2):
    depth = (left.shape[0] if rows is None else rows) // steps

    @pl.loop(0, steps)
    def _(i):
        begin = pl.multiple_of(i * depth, depth)
        total[...] += contract(left[pl.ds(left0 + begin, depth), :], right[pl.ds(right0 + begin, depth), :])


def panel_kernel(nrows_blk, nrows, shift, bsize, first, owner_row, entries, blocks, panel, odd, even, sent, out, result, halo, acc, near_sent, sem):
    copy = pltpu.make_async_copy(sent, near_sent, sem)
    copy.start()
    mass_kernel(nrows_blk, 0, nrows, shift, bsize, first, owner_row, entries, blocks, panel, odd, even, None, out, halo, acc)
    result[...] = jnp.zeros_like(result)
    add_contract(result, out, panel)
    copy.wait()
    add_contract(result, near_sent, panel, right0=nrows * bsize)


def panel_work(lists, blocks, panel, odd, even, sent, shift, nrows):
    bsize, width = blocks.shape[1], panel.shape[1]
    return pl.pallas_call(
        functools.partial(panel_kernel, panel.shape[0] // bsize, nrows, shift, bsize),
        out_shape=[
            jax.ShapeDtypeStruct((nrows * bsize, width), panel.dtype),
            jax.ShapeDtypeStruct((width, width), jnp.float32),
        ],
        in_specs=[SCALAR] * 3 + [NEAR] * 4 + [ANYWHERE],
        out_specs=[NEAR] * 2,
        scratch_shapes=[
            pltpu.VMEM((2 * even.shape[0], width), panel.dtype),
            pltpu.VMEM((nrows * bsize, width), jnp.float32),
            pltpu.VMEM(sent.shape, sent.dtype),
            pltpu.SemaphoreType.DMA,
        ],
        compiler_params=room_for(4 * nbytes(even), 6 * nrows * bsize * width, 2 * nbytes(sent), 4 * width * width),
        cost_estimate=near_nothing(),
    )(*lists, blocks, panel, odd, even, sent)


def partner_kernel(n_col, mass, ahead, panel, known, partner):
    early, rows = ahead.shape[0], partner.shape[0]
    panel_column = lax.axis_index("col") == n_col - 1
    known[...] = jnp.zeros_like(known)

    @pl.when(panel_column)
    def _():
        add_contract(known, mass, ahead, rows=early)
        partner[...] = mass[pl.ds(early, rows), :]

    @pl.when(jnp.logical_not(panel_column))
    def _():
        partner[...] = panel[pl.ds(panel.shape[0] - rows, rows), :]


def partner_rows(mass, ahead, panel, rows, n_col):
    width = mass.shape[1]
    return pl.pallas_call(
        functools.partial(partner_kernel, n_col),
        out_shape=[jax.ShapeDtypeStruct((width, width), jnp.float32), jax.ShapeDtypeStruct((rows, width), mass.dtype)],
        in_specs=[NEAR] * 3,
        out_specs=[NEAR] * 2,
        compiler_params=room_for(2 * nbytes(ahead), 4 * width * width, 4 * rows * width),
        cost_estimate=near_nothing(),
    )(mass, ahead, panel)


def meet_kernel(n_col, got, partner, known, out):
    panel_column = lax.axis_index("col") == n_col - 1
    out[...] = known[...]

    @pl.when(panel_column)
    def _():
        add_contract(out, partner, got, steps=1)

    @pl.when(jnp.logical_not(panel_column))
    def _():
        add_contract(out, got, partner, steps=1)


def meet(got, partner, known, n_col):
    return pl.pallas_call(
        functools.partial(meet_kernel, n_col),
        out_shape=jax.ShapeDtypeStruct(known.shape, jnp.float32),
        in_specs=[NEAR] * 3,
        out_specs=NEAR,
        compiler_params=room_for(4 * nbytes(got), 2 * nbytes(known)),
        cost_estimate=near_nothing(),
    )(got, partner, known)


def mass_rows(lists, blocks, panel, odd, even, after, shift, row0, nrows):
    bsize, width = blocks.shape[1], panel.shape[1]
    return pl.pallas_call(
        functools.partial(mass_kernel, panel.shape[0] // bsize, row0, nrows, shift, bsize),
        out_shape=jax.ShapeDtypeStruct((nrows * bsize, width), panel.dtype),
        in_specs=[SCALAR] * 3 + [NEAR] * 5,
        out_specs=NEAR,
        scratch_shapes=[
            pltpu.VMEM((2 * even.shape[0], width), panel.dtype),
            pltpu.VMEM((nrows * bsize, width), jnp.float32),
        ],
        compiler_params=room_for(4 * nbytes(even), 6 * nrows * bsize * width, nbytes(after)),
        cost_estimate=near_nothing(),
    )(*lists, blocks, panel, odd, even, after)


def fold_kernel(bit, *refs):
    *parts, keep, send = refs
    mine = (lax.axis_index("dom") // bit) % 2
    for t in range(keep.shape[0]):
        for out, side in ((keep, mine), (send, 1 - mine)):
            total = parts[0][2 * t + side]
            for part in parts[1:]:
                total += part[2 * t + side].astype(jnp.float32)
            out[t] = total.astype(out.dtype)


def fold(bit, parts, kind):
    targets, rows, width = parts[0].shape
    shape = (targets // 2, rows, width)
    return pl.pallas_call(
        functools.partial(fold_kernel, bit),
        out_shape=[jax.ShapeDtypeStruct(shape, jnp.float32), jax.ShapeDtypeStruct(shape, kind)],
        in_specs=[NEAR] * len(parts),
        out_specs=[NEAR] * 2,
        compiler_params=room_for(),
        cost_estimate=near_nothing(),
    )(*parts)


def step(route, bit, parts, kind=jnp.float32):
    keep, send = fold(bit, parts, kind)
    return [keep, lax.ppermute(send, *route(bit))]


def body(tmat, stored_mass_blocks, block_index, live_block_count, send_rows):
    n_col, n_dom = lax.axis_size("col"), lax.axis_size("dom")
    owner = n_col - 1
    col, dom = lax.axis_index("col"), lax.axis_index("dom")
    rows_dev, width = tmat.shape
    bsize = stored_mass_blocks.shape[1]
    nrows_blk = rows_dev // bsize
    share = width // n_dom
    shift = nrows_blk.bit_length()
    lists = slot_list(block_index, live_block_count, nrows_blk, shift, n_col)


    def exchange(block, begin):
        pairs = [(i * n_col + owner, (i + 1) * n_col + owner) for i in range(begin, n_dom - 1, 2)]
        return lax.ppermute(block, ("dom", "col"), pairs + [(b, a) for a, b in pairs])

    na = (nrows_blk * 13) // 32
    nb = nrows_blk - na
    *rows, panel, blocks = gather_rows(send_rows, tmat, stored_mass_blocks)
    even, odd = exchange(rows[0], 0), exchange(rows[1], 1)

    if n_col != 2 or n_dom < 16 or n_dom & (n_dom - 1):
        mass = mass_rows(lists, blocks, panel, odd, even, even, shift, 0, nrows_blk)
        total = lax.psum(contract(lax.psum(mass, "col"), tmat), "dom")
        return lax.dynamic_slice_in_dim(total, dom * share, share, 0)

    cut = nb * bsize
    early = cut - na * bsize
    ahead = lax.ppermute(tmat[:early], "col", [(0, 1), (1, 0)])

    own_a = own_products(lists, blocks, panel, shift, nb, na)
    sent = piece(lists, blocks, odd, even, own_a, tmat, shift, nb, na, early, n_col)
    sent, ahead = lax.optimization_barrier((sent, ahead))
    got = lax.ppermute(sent, "col", [(0, 1), (1, 0)])
    mass_b, own = panel_work(lists, blocks, panel, odd, even, sent, shift, nb)
    known, partner = partner_rows(mass_b, ahead, panel, na * bsize, n_col)

    def both(bit):
        return "dom", [(i, i ^ bit) for i in range(n_dom)]

    def panel_column(bit):
        return ("dom", "col"), [(i * n_col + owner, (i ^ bit) * n_col + owner) for i in range(n_dom)]

    parts, bit = [own.reshape(n_dom, share, width)], 1
    while bit < n_dom // 2:
        parts = step(panel_column, bit, parts)
        if bit == 2:
            parts[1], known, partner = lax.optimization_barrier((parts[1], known, partner))
        bit *= 2
    got, parts[1] = lax.optimization_barrier((got, parts[1]))

    x = meet(got, partner, known, n_col)
    sums = [x.reshape(n_dom, share, width)]
    for b in range(bit.bit_length()):
        sums = step(both, 1 << b, sums, jnp.bfloat16 if b == 1 else jnp.float32)
    own_keep, own_got = step(panel_column, bit, parts)
    x = sums[0] + sums[1]
    other = x + lax.ppermute(x, "col", [(0, 1), (1, 0)])
    return jnp.where(col == owner, own_keep + own_got, other).reshape(share, width)


def solution(mesh):
    return jax.shard_map(
        body,
        mesh=mesh,
        in_specs=(P("dom", "col"), P("dom", None, None), P("dom", None), P("dom"), P("dom", None)),
        out_specs=P("dom", "col"),
        check_vma=False,
    )
```

```python
import functools

import jax
import jax.numpy as jnp
from jax import lax
from jax.experimental import pallas as pl
from jax.experimental.pallas import tpu as pltpu
from jax.sharding import PartitionSpec as P

GROUP = 4
UNROLL = 8

ANYWHERE = pl.BlockSpec(memory_space=pl.ANY)
FAR = pl.BlockSpec(memory_space=pltpu.HBM)
NEAR = pl.BlockSpec(memory_space=pltpu.VMEM)
SCALAR = pl.BlockSpec(memory_space=pltpu.SMEM)


def contract(left, right):
    return lax.dot_general(
        left, right, (((0,), (0,)), ((), ())), preferred_element_type=jnp.float32
    )


def far(*arrays):
    return [pltpu.with_memory_space_constraint(a, pltpu.HBM) for a in arrays]


def room_for(*sizes):
    return pltpu.CompilerParams(vmem_limit_bytes=(6 << 20) + sum(sizes))


def nbytes(array):
    return array.size * array.dtype.itemsize


def near_nothing():
    return pl.CostEstimate(flops=1, bytes_accessed=1, transcendentals=0)


def columns_of(rows):
    count, width = rows.shape
    return jnp.concatenate([rows, jnp.zeros((8 - count, width), rows.dtype)], 0).T


def slot_kernel(nrows_blk, shift, n_col, live_count, index, first, owner_row, entries):
    slots = index.shape[1]
    nkeys = 2 * nrows_blk
    live = jnp.where(lax.axis_index("col") == n_col - 1, live_count[0], 0)

    def count_up(shape, axis):
        return lax.broadcasted_iota(jnp.int32, shape, axis)

    def keys_of(rows, cols):
        return rows + jnp.where(cols >= nrows_blk, nrows_blk, 0)

    def groups_of(hits, axis):
        return (jnp.sum(hits.astype(jnp.int32), axis, keepdims=True) + (GROUP - 1)) // GROUP

    across = index[...]
    down = columns_of(across)
    row_a, col_a = across[0:1], across[1:2]
    row_d, col_d = down[:, 0:1], down[:, 1:2]
    key_a, key_d = keys_of(row_a, col_a), keys_of(row_d, col_d)
    k_a, k_d = count_up((1, slots), 1), count_up((slots, 1), 0)
    alive_a, alive_d = k_a < live, k_d < live
    rank = jnp.sum(((key_a == key_d) & alive_a & (k_a < k_d)).astype(jnp.int32), 1, keepdims=True)
    groups_d = groups_of((key_a == count_up((nkeys, 1), 0)) & alive_a, 1)
    groups_a = groups_of((key_d == count_up((1, nkeys), 1)) & alive_d, 0)
    room = first.shape[1]
    first_a = jnp.sum(jnp.where(count_up((nkeys, room), 0) < count_up((nkeys, room), 1), groups_d, 0), 0, keepdims=True)
    first_d = jnp.sum(jnp.where(count_up((nkeys, nkeys), 1) < count_up((nkeys, nkeys), 0), groups_a, 0), 1, keepdims=True)
    first[...] = first_a
    started = (first_d <= count_up((nkeys, owner_row.shape[1]), 1)).astype(jnp.int32)
    key = jnp.sum(started, 0, keepdims=True) - 1
    owner_row[...] = jnp.where(key >= nrows_blk, key - nrows_blk, key)
    begin = jnp.sum(jnp.where(key_d == count_up((slots, room), 1), first_a, 0), 1, keepdims=True)
    place = begin * GROUP + rank
    value = ((k_d + 1) << shift) + col_d - jnp.where(col_d >= nrows_blk, nrows_blk, 0)
    hit = (place == count_up((slots, entries.shape[1]), 1)) & alive_d
    entries[...] = jnp.sum(jnp.where(hit, value, 0), 0, keepdims=True)


def slot_list(block_index, live_block_count, nrows_blk, shift, n_col):
    slots = block_index.shape[0]
    total = slots // GROUP + 2 * nrows_blk

    def lanes(n):
        return jax.ShapeDtypeStruct((1, -(-n // 128) * 128), jnp.int32)

    return pl.pallas_call(
        functools.partial(slot_kernel, nrows_blk, shift, n_col),
        out_shape=[lanes(2 * nrows_blk + 1), lanes(total), lanes(total * GROUP)],
        in_specs=[SCALAR, NEAR],
        out_specs=[NEAR] * 3,
        compiler_params=room_for(),
        cost_estimate=near_nothing(),
    )(live_block_count, block_index.T)


def products(lists, begin, end, row0, shift, block_of, source, acc, bsize):
    _, owner_row, entries = lists

    @pl.loop(0, (end - begin + UNROLL - 1) // UNROLL)
    def _(step):
        rows, prods = [], []
        for u in range(UNROLL):
            g = begin + step * UNROLL + u
            inside = g < end
            g = jnp.minimum(g, end - 1)
            rows.append(jnp.where(inside, owner_row[0, g] - row0, 0))
            left, right = [], []
            for j in range(GROUP):
                entry = jnp.where(inside, entries[0, g * GROUP + j], 0)
                block = block_of(g, j, entry)
                column = entry & ((1 << shift) - 1)
                left.append(jnp.where(entry > 0, block, jnp.zeros_like(block)))
                right.append(source[pl.ds(pl.multiple_of(column * bsize, bsize), bsize), :])
            prods.append(
                jnp.dot(jnp.concatenate(left, 1), jnp.concatenate(right, 0), preferred_element_type=jnp.float32)
            )
        for row, prod in zip(rows, prods):
            acc[pl.ds(pl.multiple_of(row * bsize, bsize), bsize), :] += prod


def stored(blocks, shift):
    return lambda g, j, entry: blocks[jnp.maximum((entry >> shift) - 1, 0)]


def shared_range(first, nrows_blk, row0, nrows):
    return first[0, nrows_blk + row0], first[0, nrows_blk + row0 + nrows]


def gather_kernel(send_rows, tmat, blocks, first, owner_row, entries, first_rows, second_rows, panel, near_blocks, picked, sem):
    count = picked.shape[0]
    depth = 2 * count
    steps = panel.shape[0] // depth
    copy_blocks = pltpu.make_async_copy(blocks, near_blocks, sem.at[steps])

    def part(step):
        chunk = pl.ds(pl.multiple_of(step * depth, depth), depth)
        return pltpu.make_async_copy(tmat.at[chunk], panel.at[chunk], sem.at[step])

    for step in range(steps):
        part(step).start()
    copy_blocks.start()
    picked[...] = jnp.zeros_like(picked)
    lists = columns_of(send_rows[...])
    wanted = jnp.concatenate([lists[:, 0:1], lists[:, 1:2]], 0)

    @pl.loop(0, steps)
    def _(step):
        part(step).wait()
        begin = pl.multiple_of(step * depth, depth)
        numbers = lax.broadcasted_iota(jnp.int32, (count, depth), 1) + begin
        picks = jnp.where(wanted == numbers, 1.0, 0.0).astype(panel.dtype)
        picked[...] += jnp.dot(picks, panel[pl.ds(begin, depth), :], preferred_element_type=jnp.float32)

    half = count // 2
    odd = lax.axis_index("dom") % 2
    first_rows[...] = picked[pl.ds(pl.multiple_of((1 - odd) * half, half), half), :].astype(first_rows.dtype)
    second_rows[...] = picked[pl.ds(pl.multiple_of(odd * half, half), half), :].astype(second_rows.dtype)
    copy_blocks.wait()


def gather_rows(send_rows, tmat, blocks, after):
    width, picked = tmat.shape[1], send_rows.size
    return pl.pallas_call(
        gather_kernel,
        out_shape=[jax.ShapeDtypeStruct((picked // 2, width), tmat.dtype)] * 2
        + [jax.ShapeDtypeStruct(a.shape, a.dtype) for a in (tmat, blocks)],
        in_specs=[NEAR] + [FAR] * 2 + [NEAR] * 3,
        out_specs=[NEAR] * 4,
        scratch_shapes=[
            pltpu.VMEM((picked, width), jnp.float32),
            pltpu.SemaphoreType.DMA((tmat.shape[0] // (2 * picked) + 1,)),
        ],
        compiler_params=room_for(nbytes(tmat), nbytes(blocks), 6 * picked * width),
        cost_estimate=near_nothing(),
    )(send_rows, *far(tmat, blocks), *after)


def own_kernel(row0, nrows, shift, bsize, first, owner_row, entries, blocks, panel, acc):
    acc[...] = jnp.zeros_like(acc)
    lists = (first, owner_row, entries)
    products(lists, first[0, row0], first[0, row0 + nrows], row0, shift, stored(blocks, shift), panel, acc, bsize)


def own_products(lists, blocks, panel, shift, row0, nrows):
    bsize, width = blocks.shape[1], panel.shape[1]
    return pl.pallas_call(
        functools.partial(own_kernel, row0, nrows, shift, bsize),
        out_shape=jax.ShapeDtypeStruct((nrows * bsize, width), jnp.float32),
        in_specs=[SCALAR] * 3 + [NEAR] * 2,
        out_specs=NEAR,
        compiler_params=room_for(4 * nrows * bsize * width),
        cost_estimate=near_nothing(),
    )(*lists, blocks, panel)


def place_halo(even, odd, halo):
    sides = even.shape[0]
    odd_partition = lax.axis_index("dom") % 2
    halo[pl.ds(pl.multiple_of((1 - odd_partition) * sides, sides), sides), :] = even[...]
    halo[pl.ds(pl.multiple_of(odd_partition * sides, sides), sides), :] = odd[...]


def pieces_kernel(nrows_blk, row0, nrows, shift, bsize, other0, n_col, first, owner_row, entries, blocks, odd, even, own, tmat, out, halo, acc, sem):
    panel_column = lax.axis_index("col") == n_col - 1

    @pl.when(panel_column)
    def _():
        acc[...] = own[...]
        place_halo(even, odd, halo)
        lists = (first, owner_row, entries)
        products(lists, *shared_range(first, nrows_blk, row0, nrows), row0, shift, stored(blocks, shift), halo, acc, bsize)
        out[...] = acc[...].astype(out.dtype)

    @pl.when(jnp.logical_not(panel_column))
    def _():
        copy = pltpu.make_async_copy(tmat.at[pl.ds(other0, out.shape[0])], out, sem)
        copy.start()
        copy.wait()


def piece(lists, blocks, odd, even, own, tmat, shift, row0, nrows, other0, n_col):
    bsize, width = blocks.shape[1], tmat.shape[1]
    size = nrows * bsize
    return pl.pallas_call(
        functools.partial(pieces_kernel, tmat.shape[0] // bsize, row0, nrows, shift, bsize, other0, n_col),
        out_shape=jax.ShapeDtypeStruct((size, width), tmat.dtype),
        in_specs=[SCALAR] * 3 + [NEAR] * 4 + [FAR],
        out_specs=NEAR,
        scratch_shapes=[
            pltpu.VMEM((2 * even.shape[0], width), tmat.dtype),
            pltpu.VMEM((size, width), jnp.float32),
            pltpu.SemaphoreType.DMA,
        ],
        compiler_params=room_for(2 * nbytes(even), 6 * size * width),
        cost_estimate=near_nothing(),
    )(*lists, blocks, odd, even, own, *far(tmat))


def mass_kernel(nrows_blk, row0, nrows, shift, bsize, first, owner_row, entries, blocks, panel, odd, even, after, out, halo, acc):
    lists = (first, owner_row, entries)
    acc[...] = jnp.zeros_like(acc)
    place_halo(even, odd, halo)
    block_of = stored(blocks, shift)
    products(lists, first[0, row0], first[0, row0 + nrows], row0, shift, block_of, panel, acc, bsize)
    products(lists, *shared_range(first, nrows_blk, row0, nrows), row0, shift, block_of, halo, acc, bsize)
    out[...] = acc[...].astype(out.dtype)


def add_contract(total, left, right, left0=0, right0=0, rows=None, steps=2):
    depth = (left.shape[0] if rows is None else rows) // steps

    @pl.loop(0, steps)
    def _(i):
        begin = pl.multiple_of(i * depth, depth)
        total[...] += contract(left[pl.ds(left0 + begin, depth), :], right[pl.ds(right0 + begin, depth), :])


def panel_kernel(nrows_blk, nrows, shift, bsize, first, owner_row, entries, blocks, panel, odd, even, sent, out, result, halo, acc, near_sent, sem):
    copy = pltpu.make_async_copy(sent, near_sent, sem)
    copy.start()
    mass_kernel(nrows_blk, 0, nrows, shift, bsize, first, owner_row, entries, blocks, panel, odd, even, None, out, halo, acc)
    result[...] = jnp.zeros_like(result)
    add_contract(result, out, panel)
    copy.wait()
    add_contract(result, near_sent, panel, right0=nrows * bsize)


def panel_work(lists, blocks, panel, odd, even, sent, shift, nrows):
    bsize, width = blocks.shape[1], panel.shape[1]
    return pl.pallas_call(
        functools.partial(panel_kernel, panel.shape[0] // bsize, nrows, shift, bsize),
        out_shape=[
            jax.ShapeDtypeStruct((nrows * bsize, width), panel.dtype),
            jax.ShapeDtypeStruct((width, width), jnp.float32),
        ],
        in_specs=[SCALAR] * 3 + [NEAR] * 4 + [ANYWHERE],
        out_specs=[NEAR] * 2,
        scratch_shapes=[
            pltpu.VMEM((2 * even.shape[0], width), panel.dtype),
            pltpu.VMEM((nrows * bsize, width), jnp.float32),
            pltpu.VMEM(sent.shape, sent.dtype),
            pltpu.SemaphoreType.DMA,
        ],
        compiler_params=room_for(4 * nbytes(even), 6 * nrows * bsize * width, 2 * nbytes(sent), 4 * width * width),
        cost_estimate=near_nothing(),
    )(*lists, blocks, panel, odd, even, sent)


def partner_kernel(n_col, mass, ahead, panel, known, partner):
    early, rows = ahead.shape[0], partner.shape[0]
    panel_column = lax.axis_index("col") == n_col - 1
    known[...] = jnp.zeros_like(known)

    @pl.when(panel_column)
    def _():
        add_contract(known, mass, ahead, rows=early)
        partner[...] = mass[pl.ds(early, rows), :]

    @pl.when(jnp.logical_not(panel_column))
    def _():
        partner[...] = panel[pl.ds(panel.shape[0] - rows, rows), :]


def partner_rows(mass, ahead, panel, rows, n_col):
    width = mass.shape[1]
    return pl.pallas_call(
        functools.partial(partner_kernel, n_col),
        out_shape=[jax.ShapeDtypeStruct((width, width), jnp.float32), jax.ShapeDtypeStruct((rows, width), mass.dtype)],
        in_specs=[NEAR] * 3,
        out_specs=[NEAR] * 2,
        compiler_params=room_for(2 * nbytes(ahead), 4 * width * width, 4 * rows * width),
        cost_estimate=near_nothing(),
    )(mass, ahead, panel)


def meet_kernel(n_col, got, partner, known, out):
    panel_column = lax.axis_index("col") == n_col - 1
    out[...] = known[...]

    @pl.when(panel_column)
    def _():
        add_contract(out, partner, got, steps=1)

    @pl.when(jnp.logical_not(panel_column))
    def _():
        add_contract(out, got, partner, steps=1)


def meet(got, partner, known, n_col):
    return pl.pallas_call(
        functools.partial(meet_kernel, n_col),
        out_shape=jax.ShapeDtypeStruct(known.shape, jnp.float32),
        in_specs=[NEAR] * 3,
        out_specs=NEAR,
        compiler_params=room_for(4 * nbytes(got), 2 * nbytes(known)),
        cost_estimate=near_nothing(),
    )(got, partner, known)


def mass_rows(lists, blocks, panel, odd, even, after, shift, row0, nrows):
    bsize, width = blocks.shape[1], panel.shape[1]
    return pl.pallas_call(
        functools.partial(mass_kernel, panel.shape[0] // bsize, row0, nrows, shift, bsize),
        out_shape=jax.ShapeDtypeStruct((nrows * bsize, width), panel.dtype),
        in_specs=[SCALAR] * 3 + [NEAR] * 5,
        out_specs=NEAR,
        scratch_shapes=[
            pltpu.VMEM((2 * even.shape[0], width), panel.dtype),
            pltpu.VMEM((nrows * bsize, width), jnp.float32),
        ],
        compiler_params=room_for(4 * nbytes(even), 6 * nrows * bsize * width, nbytes(after)),
        cost_estimate=near_nothing(),
    )(*lists, blocks, panel, odd, even, after)


def fold_kernel(bit, *refs):
    *parts, keep, send = refs
    mine = (lax.axis_index("dom") // bit) % 2
    for t in range(keep.shape[0]):
        for out, side in ((keep, mine), (send, 1 - mine)):
            total = parts[0][2 * t + side]
            for part in parts[1:]:
                total += part[2 * t + side].astype(jnp.float32)
            out[t] = total.astype(out.dtype)


def fold(bit, parts, kind):
    targets, rows, width = parts[0].shape
    shape = (targets // 2, rows, width)
    return pl.pallas_call(
        functools.partial(fold_kernel, bit),
        out_shape=[jax.ShapeDtypeStruct(shape, jnp.float32), jax.ShapeDtypeStruct(shape, kind)],
        in_specs=[NEAR] * len(parts),
        out_specs=[NEAR] * 2,
        compiler_params=room_for(),
        cost_estimate=near_nothing(),
    )(*parts)


def step(route, bit, parts, kind=jnp.float32):
    keep, send = fold(bit, parts, kind)
    return [keep, lax.ppermute(send, *route(bit))]


def body(tmat, stored_mass_blocks, block_index, live_block_count, send_rows):
    n_col, n_dom = lax.axis_size("col"), lax.axis_size("dom")
    owner = n_col - 1
    col, dom = lax.axis_index("col"), lax.axis_index("dom")
    rows_dev, width = tmat.shape
    bsize = stored_mass_blocks.shape[1]
    nrows_blk = rows_dev // bsize
    share = width // n_dom
    shift = nrows_blk.bit_length()
    lists = slot_list(block_index, live_block_count, nrows_blk, shift, n_col)


    def exchange(block, begin):
        pairs = [(i * n_col + owner, (i + 1) * n_col + owner) for i in range(begin, n_dom - 1, 2)]
        return lax.ppermute(block, ("dom", "col"), pairs + [(b, a) for a, b in pairs])

    na = (nrows_blk * 13) // 32
    nb = nrows_blk - na
    *rows, panel, blocks = gather_rows(send_rows, tmat, stored_mass_blocks, lists)
    even, odd = exchange(rows[0], 0), exchange(rows[1], 1)

    if n_col != 2 or n_dom < 16 or n_dom & (n_dom - 1):
        mass = mass_rows(lists, blocks, panel, odd, even, even, shift, 0, nrows_blk)
        total = lax.psum(contract(lax.psum(mass, "col"), tmat), "dom")
        return lax.dynamic_slice_in_dim(total, dom * share, share, 0)

    cut = nb * bsize
    early = cut - na * bsize
    ahead = lax.ppermute(tmat[:early], "col", [(0, 1), (1, 0)])

    own_a = own_products(lists, blocks, panel, shift, nb, na)
    sent = piece(lists, blocks, odd, even, own_a, tmat, shift, nb, na, early, n_col)
    sent, ahead = lax.optimization_barrier((sent, ahead))
    got = lax.ppermute(sent, "col", [(0, 1), (1, 0)])
    mass_b, own = panel_work(lists, blocks, panel, odd, even, sent, shift, nb)
    known, partner = partner_rows(mass_b, ahead, panel, na * bsize, n_col)

    def both(bit):
        return "dom", [(i, i ^ bit) for i in range(n_dom)]

    def panel_column(bit):
        return ("dom", "col"), [(i * n_col + owner, (i ^ bit) * n_col + owner) for i in range(n_dom)]

    parts, bit = [own.reshape(n_dom, share, width)], 1
    while bit < n_dom // 2:
        parts = step(panel_column, bit, parts)
        if bit == 2:
            parts[1], known, partner = lax.optimization_barrier((parts[1], known, partner))
        bit *= 2
    got, parts[1] = lax.optimization_barrier((got, parts[1]))

    x = meet(got, partner, known, n_col)
    sums = [x.reshape(n_dom, share, width)]
    for b in range(bit.bit_length()):
        sums = step(both, 1 << b, sums, jnp.bfloat16 if b == 1 else jnp.float32)
    own_keep, own_got = step(panel_column, bit, parts)
    x = sums[0] + sums[1]
    other = x + lax.ppermute(x, "col", [(0, 1), (1, 0)])
    return jnp.where(col == owner, own_keep + own_got, other).reshape(share, width)


def solution(mesh):
    return jax.shard_map(
        body,
        mesh=mesh,
        in_specs=(P("dom", "col"), P("dom", None, None), P("dom", None), P("dom"), P("dom", None)),
        out_specs=P("dom", "col"),
        check_vma=False,
    )
```

```python
import functools

import jax
import jax.numpy as jnp
from jax import lax
from jax.experimental import pallas as pl
from jax.experimental.pallas import tpu as pltpu
from jax.sharding import PartitionSpec as P

GROUP = 4
UNROLL = 8

ANYWHERE = pl.BlockSpec(memory_space=pl.ANY)
FAR = pl.BlockSpec(memory_space=pltpu.HBM)
NEAR = pl.BlockSpec(memory_space=pltpu.VMEM)
SCALAR = pl.BlockSpec(memory_space=pltpu.SMEM)


def contract(left, right):
    return lax.dot_general(
        left, right, (((0,), (0,)), ((), ())), preferred_element_type=jnp.float32
    )


def far(*arrays):
    return [pltpu.with_memory_space_constraint(a, pltpu.HBM) for a in arrays]


def room_for(*sizes):
    return pltpu.CompilerParams(vmem_limit_bytes=(6 << 20) + sum(sizes))


def nbytes(array):
    return array.size * array.dtype.itemsize


def near_nothing():
    return pl.CostEstimate(flops=1, bytes_accessed=1, transcendentals=0)


def columns_of(rows):
    count, width = rows.shape
    return jnp.concatenate([rows, jnp.zeros((8 - count, width), rows.dtype)], 0).T


def slot_kernel(nrows_blk, shift, n_col, live_count, index, first, owner_row, entries):
    slots = index.shape[1]
    nkeys = 2 * nrows_blk
    live = jnp.where(lax.axis_index("col") == n_col - 1, live_count[0], 0)

    def count_up(shape, axis):
        return lax.broadcasted_iota(jnp.int32, shape, axis)

    def keys_of(rows, cols):
        return rows + jnp.where(cols >= nrows_blk, nrows_blk, 0)

    def groups_of(hits, axis):
        return (jnp.sum(hits.astype(jnp.int32), axis, keepdims=True) + (GROUP - 1)) // GROUP

    across = index[...]
    down = columns_of(across)
    row_a, col_a = across[0:1], across[1:2]
    row_d, col_d = down[:, 0:1], down[:, 1:2]
    key_a, key_d = keys_of(row_a, col_a), keys_of(row_d, col_d)
    k_a, k_d = count_up((1, slots), 1), count_up((slots, 1), 0)
    alive_a, alive_d = k_a < live, k_d < live
    rank = jnp.sum(((key_a == key_d) & alive_a & (k_a < k_d)).astype(jnp.int32), 1, keepdims=True)
    groups_d = groups_of((key_a == count_up((nkeys, 1), 0)) & alive_a, 1)
    groups_a = groups_of((key_d == count_up((1, nkeys), 1)) & alive_d, 0)
    room = first.shape[1]
    first_a = jnp.sum(jnp.where(count_up((nkeys, room), 0) < count_up((nkeys, room), 1), groups_d, 0), 0, keepdims=True)
    first_d = jnp.sum(jnp.where(count_up((nkeys, nkeys), 1) < count_up((nkeys, nkeys), 0), groups_a, 0), 1, keepdims=True)
    first[...] = first_a
    started = (first_d <= count_up((nkeys, owner_row.shape[1]), 1)).astype(jnp.int32)
    key = jnp.sum(started, 0, keepdims=True) - 1
    owner_row[...] = jnp.where(key >= nrows_blk, key - nrows_blk, key)
    begin = jnp.sum(jnp.where(key_d == count_up((slots, room), 1), first_a, 0), 1, keepdims=True)
    place = begin * GROUP + rank
    value = ((k_d + 1) << shift) + col_d - jnp.where(col_d >= nrows_blk, nrows_blk, 0)
    hit = (place == count_up((slots, entries.shape[1]), 1)) & alive_d
    entries[...] = jnp.sum(jnp.where(hit, value, 0), 0, keepdims=True)


def slot_list(block_index, live_block_count, nrows_blk, shift, n_col):
    slots = block_index.shape[0]
    total = slots // GROUP + 2 * nrows_blk

    def lanes(n):
        return jax.ShapeDtypeStruct((1, -(-n // 128) * 128), jnp.int32)

    return pl.pallas_call(
        functools.partial(slot_kernel, nrows_blk, shift, n_col),
        out_shape=[lanes(2 * nrows_blk + 1), lanes(total), lanes(total * GROUP)],
        in_specs=[SCALAR, NEAR],
        out_specs=[NEAR] * 3,
        compiler_params=room_for(),
        cost_estimate=near_nothing(),
    )(live_block_count, block_index.T)


def products(lists, begin, end, row0, shift, block_of, source, acc, bsize):
    _, owner_row, entries = lists

    @pl.loop(0, (end - begin + UNROLL - 1) // UNROLL)
    def _(step):
        rows, prods = [], []
        for u in range(UNROLL):
            g = begin + step * UNROLL + u
            inside = g < end
            g = jnp.minimum(g, end - 1)
            rows.append(jnp.where(inside, owner_row[0, g] - row0, 0))
            left, right = [], []
            for j in range(GROUP):
                entry = jnp.where(inside, entries[0, g * GROUP + j], 0)
                block = block_of(g, j, entry)
                column = entry & ((1 << shift) - 1)
                left.append(jnp.where(entry > 0, block, jnp.zeros_like(block)))
                right.append(source[pl.ds(pl.multiple_of(column * bsize, bsize), bsize), :])
            prods.append(
                jnp.dot(jnp.concatenate(left, 1), jnp.concatenate(right, 0), preferred_element_type=jnp.float32)
            )
        for row, prod in zip(rows, prods):
            acc[pl.ds(pl.multiple_of(row * bsize, bsize), bsize), :] += prod


def stored(blocks, shift):
    return lambda g, j, entry: blocks[jnp.maximum((entry >> shift) - 1, 0)]


def shared_range(first, nrows_blk, row0, nrows):
    return first[0, nrows_blk + row0], first[0, nrows_blk + row0 + nrows]


def gather_kernel(send_rows, tmat, blocks, first_rows, second_rows, panel, near_blocks, picked, sem):
    count = picked.shape[0]
    depth = 4 * count
    steps = panel.shape[0] // depth
    copy_blocks = pltpu.make_async_copy(blocks, near_blocks, sem.at[steps])

    def part(step):
        chunk = pl.ds(pl.multiple_of(step * depth, depth), depth)
        return pltpu.make_async_copy(tmat.at[chunk], panel.at[chunk], sem.at[step])

    for step in range(steps):
        part(step).start()
    copy_blocks.start()
    picked[...] = jnp.zeros_like(picked)
    lists = columns_of(send_rows[...])
    wanted = jnp.concatenate([lists[:, 0:1], lists[:, 1:2]], 0)

    @pl.loop(0, steps)
    def _(step):
        part(step).wait()
        begin = pl.multiple_of(step * depth, depth)
        numbers = lax.broadcasted_iota(jnp.int32, (count, depth), 1) + begin
        picks = jnp.where(wanted == numbers, 1.0, 0.0).astype(panel.dtype)
        picked[...] += jnp.dot(picks, panel[pl.ds(begin, depth), :], preferred_element_type=jnp.float32)

    half = count // 2
    odd = lax.axis_index("dom") % 2
    first_rows[...] = picked[pl.ds(pl.multiple_of((1 - odd) * half, half), half), :].astype(first_rows.dtype)
    second_rows[...] = picked[pl.ds(pl.multiple_of(odd * half, half), half), :].astype(second_rows.dtype)
    copy_blocks.wait()


def gather_rows(send_rows, tmat, blocks):
    width, picked = tmat.shape[1], send_rows.size
    return pl.pallas_call(
        gather_kernel,
        out_shape=[jax.ShapeDtypeStruct((picked // 2, width), tmat.dtype)] * 2
        + [jax.ShapeDtypeStruct(a.shape, a.dtype) for a in (tmat, blocks)],
        in_specs=[NEAR] + [FAR] * 2,
        out_specs=[NEAR] * 4,
        scratch_shapes=[
            pltpu.VMEM((picked, width), jnp.float32),
            pltpu.SemaphoreType.DMA((tmat.shape[0] // (4 * picked) + 1,)),
        ],
        compiler_params=room_for(nbytes(tmat), nbytes(blocks), 6 * picked * width),
        cost_estimate=near_nothing(),
    )(send_rows, *far(tmat, blocks))


def own_kernel(row0, nrows, shift, bsize, first, owner_row, entries, blocks, panel, acc):
    acc[...] = jnp.zeros_like(acc)
    lists = (first, owner_row, entries)
    products(lists, first[0, row0], first[0, row0 + nrows], row0, shift, stored(blocks, shift), panel, acc, bsize)


def own_products(lists, blocks, panel, shift, row0, nrows):
    bsize, width = blocks.shape[1], panel.shape[1]
    return pl.pallas_call(
        functools.partial(own_kernel, row0, nrows, shift, bsize),
        out_shape=jax.ShapeDtypeStruct((nrows * bsize, width), jnp.float32),
        in_specs=[SCALAR] * 3 + [NEAR] * 2,
        out_specs=NEAR,
        compiler_params=room_for(4 * nrows * bsize * width),
        cost_estimate=near_nothing(),
    )(*lists, blocks, panel)


def place_halo(even, odd, halo):
    sides = even.shape[0]
    odd_partition = lax.axis_index("dom") % 2
    halo[pl.ds(pl.multiple_of((1 - odd_partition) * sides, sides), sides), :] = even[...]
    halo[pl.ds(pl.multiple_of(odd_partition * sides, sides), sides), :] = odd[...]


def pieces_kernel(nrows_blk, row0, nrows, shift, bsize, other0, n_col, first, owner_row, entries, blocks, odd, even, own, tmat, out, halo, acc, sem):
    panel_column = lax.axis_index("col") == n_col - 1

    @pl.when(panel_column)
    def _():
        acc[...] = own[...]
        place_halo(even, odd, halo)
        lists = (first, owner_row, entries)
        products(lists, *shared_range(first, nrows_blk, row0, nrows), row0, shift, stored(blocks, shift), halo, acc, bsize)
        out[...] = acc[...].astype(out.dtype)

    @pl.when(jnp.logical_not(panel_column))
    def _():
        copy = pltpu.make_async_copy(tmat.at[pl.ds(other0, out.shape[0])], out, sem)
        copy.start()
        copy.wait()


def piece(lists, blocks, odd, even, own, tmat, shift, row0, nrows, other0, n_col):
    bsize, width = blocks.shape[1], tmat.shape[1]
    size = nrows * bsize
    return pl.pallas_call(
        functools.partial(pieces_kernel, tmat.shape[0] // bsize, row0, nrows, shift, bsize, other0, n_col),
        out_shape=jax.ShapeDtypeStruct((size, width), tmat.dtype),
        in_specs=[SCALAR] * 3 + [NEAR] * 4 + [FAR],
        out_specs=NEAR,
        scratch_shapes=[
            pltpu.VMEM((2 * even.shape[0], width), tmat.dtype),
            pltpu.VMEM((size, width), jnp.float32),
            pltpu.SemaphoreType.DMA,
        ],
        compiler_params=room_for(2 * nbytes(even), 6 * size * width),
        cost_estimate=near_nothing(),
    )(*lists, blocks, odd, even, own, *far(tmat))


def mass_kernel(nrows_blk, row0, nrows, shift, bsize, first, owner_row, entries, blocks, panel, odd, even, after, out, halo, acc):
    lists = (first, owner_row, entries)
    acc[...] = jnp.zeros_like(acc)
    place_halo(even, odd, halo)
    block_of = stored(blocks, shift)
    products(lists, first[0, row0], first[0, row0 + nrows], row0, shift, block_of, panel, acc, bsize)
    products(lists, *shared_range(first, nrows_blk, row0, nrows), row0, shift, block_of, halo, acc, bsize)
    out[...] = acc[...].astype(out.dtype)


def add_contract(total, left, right, left0=0, right0=0, rows=None, steps=2):
    depth = (left.shape[0] if rows is None else rows) // steps

    @pl.loop(0, steps)
    def _(i):
        begin = pl.multiple_of(i * depth, depth)
        total[...] += contract(left[pl.ds(left0 + begin, depth), :], right[pl.ds(right0 + begin, depth), :])


def panel_kernel(nrows_blk, nrows, shift, bsize, first, owner_row, entries, blocks, panel, odd, even, sent, out, result, halo, acc, near_sent, sem):
    copy = pltpu.make_async_copy(sent, near_sent, sem)
    copy.start()
    mass_kernel(nrows_blk, 0, nrows, shift, bsize, first, owner_row, entries, blocks, panel, odd, even, None, out, halo, acc)
    result[...] = jnp.zeros_like(result)
    add_contract(result, out, panel)
    copy.wait()
    add_contract(result, near_sent, panel, right0=nrows * bsize)


def panel_work(lists, blocks, panel, odd, even, sent, shift, nrows):
    bsize, width = blocks.shape[1], panel.shape[1]
    return pl.pallas_call(
        functools.partial(panel_kernel, panel.shape[0] // bsize, nrows, shift, bsize),
        out_shape=[
            jax.ShapeDtypeStruct((nrows * bsize, width), panel.dtype),
            jax.ShapeDtypeStruct((width, width), jnp.float32),
        ],
        in_specs=[SCALAR] * 3 + [NEAR] * 4 + [ANYWHERE],
        out_specs=[NEAR] * 2,
        scratch_shapes=[
            pltpu.VMEM((2 * even.shape[0], width), panel.dtype),
            pltpu.VMEM((nrows * bsize, width), jnp.float32),
            pltpu.VMEM(sent.shape, sent.dtype),
            pltpu.SemaphoreType.DMA,
        ],
        compiler_params=room_for(4 * nbytes(even), 6 * nrows * bsize * width, 2 * nbytes(sent), 4 * width * width),
        cost_estimate=near_nothing(),
    )(*lists, blocks, panel, odd, even, sent)


def partner_kernel(n_col, mass, ahead, panel, known, partner):
    early, rows = ahead.shape[0], partner.shape[0]
    panel_column = lax.axis_index("col") == n_col - 1
    known[...] = jnp.zeros_like(known)

    @pl.when(panel_column)
    def _():
        add_contract(known, mass, ahead, rows=early)
        partner[...] = mass[pl.ds(early, rows), :]

    @pl.when(jnp.logical_not(panel_column))
    def _():
        partner[...] = panel[pl.ds(panel.shape[0] - rows, rows), :]


def partner_rows(mass, ahead, panel, rows, n_col):
    width = mass.shape[1]
    return pl.pallas_call(
        functools.partial(partner_kernel, n_col),
        out_shape=[jax.ShapeDtypeStruct((width, width), jnp.float32), jax.ShapeDtypeStruct((rows, width), mass.dtype)],
        in_specs=[NEAR] * 3,
        out_specs=[NEAR] * 2,
        compiler_params=room_for(2 * nbytes(ahead), 4 * width * width, 4 * rows * width),
        cost_estimate=near_nothing(),
    )(mass, ahead, panel)


def meet_kernel(n_col, got, partner, known, out):
    panel_column = lax.axis_index("col") == n_col - 1
    out[...] = known[...]

    @pl.when(panel_column)
    def _():
        add_contract(out, partner, got, steps=1)

    @pl.when(jnp.logical_not(panel_column))
    def _():
        add_contract(out, got, partner, steps=1)


def meet(got, partner, known, n_col):
    return pl.pallas_call(
        functools.partial(meet_kernel, n_col),
        out_shape=jax.ShapeDtypeStruct(known.shape, jnp.float32),
        in_specs=[NEAR] * 3,
        out_specs=NEAR,
        compiler_params=room_for(4 * nbytes(got), 2 * nbytes(known)),
        cost_estimate=near_nothing(),
    )(got, partner, known)


def mass_rows(lists, blocks, panel, odd, even, after, shift, row0, nrows):
    bsize, width = blocks.shape[1], panel.shape[1]
    return pl.pallas_call(
        functools.partial(mass_kernel, panel.shape[0] // bsize, row0, nrows, shift, bsize),
        out_shape=jax.ShapeDtypeStruct((nrows * bsize, width), panel.dtype),
        in_specs=[SCALAR] * 3 + [NEAR] * 5,
        out_specs=NEAR,
        scratch_shapes=[
            pltpu.VMEM((2 * even.shape[0], width), panel.dtype),
            pltpu.VMEM((nrows * bsize, width), jnp.float32),
        ],
        compiler_params=room_for(4 * nbytes(even), 6 * nrows * bsize * width, nbytes(after)),
        cost_estimate=near_nothing(),
    )(*lists, blocks, panel, odd, even, after)


def fold_kernel(bit, *refs):
    *parts, keep, send = refs
    mine = (lax.axis_index("dom") // bit) % 2
    for t in range(keep.shape[0]):
        for out, side in ((keep, mine), (send, 1 - mine)):
            total = parts[0][2 * t + side]
            for part in parts[1:]:
                total += part[2 * t + side].astype(jnp.float32)
            out[t] = total.astype(out.dtype)


def fold(bit, parts, kind):
    targets, rows, width = parts[0].shape
    shape = (targets // 2, rows, width)
    return pl.pallas_call(
        functools.partial(fold_kernel, bit),
        out_shape=[jax.ShapeDtypeStruct(shape, jnp.float32), jax.ShapeDtypeStruct(shape, kind)],
        in_specs=[NEAR] * len(parts),
        out_specs=[NEAR] * 2,
        compiler_params=room_for(),
        cost_estimate=near_nothing(),
    )(*parts)


def step(route, bit, parts, kind=jnp.float32):
    keep, send = fold(bit, parts, kind)
    return [keep, lax.ppermute(send, *route(bit))]


def body(tmat, stored_mass_blocks, block_index, live_block_count, send_rows):
    n_col, n_dom = lax.axis_size("col"), lax.axis_size("dom")
    owner = n_col - 1
    col, dom = lax.axis_index("col"), lax.axis_index("dom")
    rows_dev, width = tmat.shape
    bsize = stored_mass_blocks.shape[1]
    nrows_blk = rows_dev // bsize
    share = width // n_dom
    shift = nrows_blk.bit_length()
    lists = slot_list(block_index, live_block_count, nrows_blk, shift, n_col)


    def exchange(block, begin):
        pairs = [(i * n_col + owner, (i + 1) * n_col + owner) for i in range(begin, n_dom - 1, 2)]
        return lax.ppermute(block, ("dom", "col"), pairs + [(b, a) for a, b in pairs])

    na = (nrows_blk * 13) // 32
    nb = nrows_blk - na
    *rows, panel, blocks = gather_rows(send_rows, tmat, stored_mass_blocks)
    even, odd = exchange(rows[0], 0), exchange(rows[1], 1)

    if n_col != 2 or n_dom < 16 or n_dom & (n_dom - 1):
        mass = mass_rows(lists, blocks, panel, odd, even, even, shift, 0, nrows_blk)
        total = lax.psum(contract(lax.psum(mass, "col"), tmat), "dom")
        return lax.dynamic_slice_in_dim(total, dom * share, share, 0)

    cut = nb * bsize
    early = cut - na * bsize
    ahead = lax.ppermute(tmat[:early], "col", [(0, 1), (1, 0)])

    own_a = own_products(lists, blocks, panel, shift, nb, na)
    sent = piece(lists, blocks, odd, even, own_a, tmat, shift, nb, na, early, n_col)
    sent, ahead = lax.optimization_barrier((sent, ahead))
    got = lax.ppermute(sent, "col", [(0, 1), (1, 0)])
    mass_b, own = panel_work(lists, blocks, panel, odd, even, sent, shift, nb)
    known, partner = partner_rows(mass_b, ahead, panel, na * bsize, n_col)

    def both(bit):
        return "dom", [(i, i ^ bit) for i in range(n_dom)]

    def panel_column(bit):
        return ("dom", "col"), [(i * n_col + owner, (i ^ bit) * n_col + owner) for i in range(n_dom)]

    parts, bit = [own.reshape(n_dom, share, width)], 1
    while bit < n_dom // 2:
        parts = step(panel_column, bit, parts)
        if bit == 2:
            parts[1], known, partner = lax.optimization_barrier((parts[1], known, partner))
        bit *= 2
    got, parts[1] = lax.optimization_barrier((got, parts[1]))

    x = meet(got, partner, known, n_col)
    sums = [x.reshape(n_dom, share, width)]
    for b in range(bit.bit_length()):
        sums = step(both, 1 << b, sums, jnp.bfloat16 if b == 1 else jnp.float32)
    own_keep, own_got = step(panel_column, bit, parts)
    x = sums[0] + sums[1]
    other = x + lax.ppermute(x, "col", [(0, 1), (1, 0)])
    return jnp.where(col == owner, own_keep + own_got, other).reshape(share, width)


def solution(mesh):
    return jax.shard_map(
        body,
        mesh=mesh,
        in_specs=(P("dom", "col"), P("dom", None, None), P("dom", None), P("dom"), P("dom", None)),
        out_specs=P("dom", "col"),
        check_vma=False,
    )
```
